32 devices in a mesh: row: 8 (over z, y), col: 4 (over x, core).
Axes of the slice: x: 2, y: 2, z: 4, core: 2. Of those that a mesh axis runs over, the one named last changes fastest.
Arguments:
- init_mean: float32 [256], replicated, may hold values from -6 to 6
- init_var: float32 [256], replicated, may hold values from 0.1 to 2
- decay: float32 [1024, 256], P(('row', 'col')), may hold values from 0 to 1
- coupling: bfloat16 [1024, 256, 256], P(('row', 'col')), may hold values from -0.0234375 to 0.0234375
- obs_map: bfloat16 [1024, 64, 256], P(('row', 'col')), may hold values from -0.375 to 0.375
- gain: bfloat16 [1024, 64, 256], P(('row', 'col')), may hold values from -0.0625 to 0.0625
- noise_factor: bfloat16 [256, 256], replicated, may hold values from -0.02734375 to 0.02734375
- obs_var: float32 [64], replicated, may hold values from 0.25 to 4
- observed: float32 [1024, 64], P(('row', 'col')), may hold values from -6 to 6
Outputs:
- means: float32 [1024, 256], P(('row', 'col'))
- variances: float32 [1024, 256], P(('row', 'col'))
The draws below stay inside these ranges and needn't reach their ends.
All inputs are finite; a program needn't handle non-finite values.
Results may differ from the reference program's by a relative error of at most 0.00037.
Values sent between devices are 32-bit elements; how exact they have to be, the bound alone decides.
No kernel may reach another device: no remote copies, remote signals or barrier semaphores. Data moves between devices by JAX's collectives and lax.ppermute only.
A program may use at most 128 MiB of HBM per device.

```python
import math
import jax
import jax.numpy as jnp
from jax import lax

S = 256
M = 64
STEPS_DEV = 32
T_STEPS = 1024


def draw_decay(key, part):
    subkeys = jax.random.split(jax.random.fold_in(key, 11), 7)
    slow_share = 0.5
    chooser = jax.random.uniform(subkeys[0], (S,), jnp.float32)
    slowly = chooser < slow_share
    slow_rate = jnp.exp(jax.random.uniform(subkeys[1], (S,), jnp.float32, math.log(0.05), math.log(1.0))) / T_STEPS
    fast_rate = 1.0 / jax.random.uniform(subkeys[2], (S,), jnp.float32, 30.0, 50.0)
    rates = jnp.where(slowly, slow_rate, fast_rate)
    factor = jnp.exp(jax.random.uniform(subkeys[3], (T_STEPS // STEPS_DEV, 1), jnp.float32, math.log(0.5), math.log(2.0)))
    factor = jnp.repeat(factor, STEPS_DEV, axis=0)
    jitter = jax.random.uniform(subkeys[4], (T_STEPS, S), jnp.float32, 0.5, 1.5)
    base = jnp.exp(-rates[None, :] * factor * jitter)
    spots = jax.random.randint(subkeys[5], (3,), 0, T_STEPS)
    struck = jnp.any(jnp.arange(T_STEPS)[:, None] == spots[None, :], axis=1)
    losses = jax.random.uniform(subkeys[6], (T_STEPS, S), jnp.float32, 0.6, 0.85)
    return jnp.where(struck[:, None] & slowly[None, :], base * losses, base)


def levels(own_key, dims, shards, low, high):
    level = 1.0
    for dim, parts in shards:
        draws = jax.random.uniform(jax.random.fold_in(jax.random.fold_in(own_key, 6), dim), (parts,), jnp.float32, low / len(shards), high / len(shards))
        level = level * jnp.repeat(jnp.exp(draws), dims[dim] // parts).reshape((-1,) + (1,) * (len(dims) - 1 - dim))
    return level


def centred(stream_key, dims, deviation, limit, cuts=(), held_as=jnp.bfloat16):
    entries = deviation * jax.random.normal(stream_key, dims, jnp.float32)
    if cuts:
        entries = entries * levels(stream_key, dims, cuts, -0.22, 0.18)
    return jnp.clip(entries, -limit, limit).astype(held_as)


def setup_inputs(seed: int = 0) -> dict:
    splits = jax.random.split(jax.random.key(seed), 10)
    init_mean = centred(splits[0], (S,), 1.0, 6.0, (), jnp.float32)
    init_var = jnp.clip(jnp.exp(jax.random.uniform(splits[1], (S,), jnp.float32, math.log(0.1), math.log(2.0))), 0.1, 2.0)
    decay = draw_decay(jax.random.fold_in(splits[9], 71), 0)
    coupling = centred(splits[3], (T_STEPS, S, S), (0.025 * S ** -0.5), 0.0234375, ((0, 32),))
    obs_map = centred(splits[4], (T_STEPS, M, S), S ** -0.5, 0.375, ((0, 32),))
    gain = centred(splits[5], (T_STEPS, M, S), (0.032 * M ** -0.5), 0.0625, ((0, 32),))
    noise_factor = centred(splits[6], (S, S), (0.03 * S ** -0.5), 0.02734375)
    obs_var = jnp.clip(jnp.exp(jax.random.uniform(splits[7], (M,), jnp.float32, math.log(0.25), math.log(4.0))), 0.25, 4.0)
    observed = centred(splits[8], (T_STEPS, M), 1.0, 6.0, ((0, 32),), jnp.float32)
    return {"init_mean": init_mean, "init_var": init_var, "decay": decay, "coupling": coupling, "obs_map": obs_map, "gain": gain, "noise_factor": noise_factor, "obs_var": obs_var, "observed": observed}


highest = lax.Precision.HIGHEST


def build(decay_t, coupling_t, obs_map_t, gain_t, noise_factor, obs_var, observed_t):
    trans = jnp.diag(decay_t) + coupling_t.astype(jnp.float32)
    obs_f = obs_map_t.astype(jnp.float32) * decay_t[None, :] + jnp.dot(obs_map_t, coupling_t, preferred_element_type=jnp.float32)
    obs_f = obs_f.astype(jnp.bfloat16)
    gain_trans = gain_t.T
    step_map = trans - jnp.dot(gain_trans, obs_f, preferred_element_type=jnp.float32)
    obs_g = jnp.dot(obs_map_t, noise_factor, preferred_element_type=jnp.float32).astype(jnp.bfloat16)
    shaped = noise_factor.astype(jnp.float32) - jnp.dot(gain_trans, obs_g, preferred_element_type=jnp.float32)
    shaped = shaped.astype(jnp.bfloat16)
    weighted = (gain_t.astype(jnp.float32) * obs_var[:, None]).astype(jnp.bfloat16)
    noise = jnp.dot(shaped, shaped.T, preferred_element_type=jnp.float32) + jnp.dot(gain_trans, weighted, preferred_element_type=jnp.float32)
    shift = jnp.dot(observed_t, gain_t.astype(jnp.float32), precision=highest)
    return step_map, shift, noise


def reference(init_mean, init_var, decay, coupling, obs_map, gain, noise_factor, obs_var, observed):
    def advance(carry, inputs):
        state_mean, state_cov = carry
        decay_t, coupling_t, obs_map_t, gain_t, observed_t = inputs
        step_map, shift, noise = build(decay_t, coupling_t, obs_map_t, gain_t, noise_factor, obs_var, observed_t)
        state_mean = jnp.dot(step_map, state_mean, precision=highest) + shift
        state_cov = jnp.dot(jnp.dot(step_map, state_cov, precision=highest), step_map.T, precision=highest) + noise
        return (state_mean, state_cov), (state_mean, jnp.diagonal(state_cov))

    start = (init_mean, jnp.diag(init_var))
    _, (means, variances) = lax.scan(advance, start, (decay, coupling, obs_map, gain, observed))
    return means, variances
```

```python
import functools
import jax
import jax.numpy as jnp
from jax import lax
from jax.experimental import pallas as pl
from jax.experimental.pallas import tpu as pltpu
from jax.sharding import PartitionSpec as P

f32, bf16 = jnp.float32, jnp.bfloat16
VMEM_LIMIT = 56 * 1024 * 1024


def nn(a, b):
    return jnp.dot(a, b, preferred_element_type=f32)


def nt(a, b):
    return lax.dot_general(a, b, (((1,), (1,)), ((), ())), preferred_element_type=f32)


def halves(x):
    high = x.astype(bf16)
    return high, (x - high.astype(f32)).astype(bf16)


def nn3(a, b):
    ah, al = halves(a)
    bh, bl = halves(b)
    return nn(ah, bh) + (nn(al, bh) + nn(ah, bl))


def nt3(a, b):
    ah, al = halves(a)
    bh, bl = halves(b)
    return nt(ah, bh) + (nt(al, bh) + nt(ah, bl))


def eye_mask(n):
    return lax.broadcasted_iota(jnp.int32, (n, n), 0) == lax.broadcasted_iota(jnp.int32, (n, n), 1)


def column(row):
    n = row.shape[1]
    out = []
    for k in range(0, n, 128):
        m = min(128, n - k)
        out.append(jnp.sum(jnp.where(eye_mask(m), row[:, k:k + m], 0.0), axis=1, keepdims=True))
    return out[0] if len(out) == 1 else jnp.concatenate(out, axis=0)


def diag_row(x):
    n = x.shape[1]
    out = []
    for k in range(0, n, 128):
        out.append(jnp.sum(jnp.where(eye_mask(128), x[k:k + 128, k:k + 128], 0.0), axis=0, keepdims=True))
    return jnp.concatenate(out, axis=1)


def joined(early, late):
    em, en, es = early
    lm, ln, ls = late
    n = em.shape[1]
    lh, ll = halves(lm)
    eh, el = halves(jnp.concatenate([em, en], axis=1))
    both = nn(lh, eh) + (nn(ll, eh) + nn(lh, el))
    xh, xl = halves(jnp.concatenate([both[:, n:], es], axis=0))
    out = nt(xh, lh) + (nt(xl, lh) + nt(xh, ll))
    return both[:, :n], out[:n] + ln, out[n:] + ls


def rank_of(axes):
    rank = 0
    for name, size in axes:
        rank = rank * size + lax.axis_index(name)
    return rank


def load(x):
    n = x.shape[1]
    return x[:n], x[n:2 * n], x[2 * n:]


def store(ref, at, element):
    n = ref.shape[-1]
    em, en, es = element
    ref[(*at, pl.ds(0, n), slice(None))] = em
    ref[(*at, pl.ds(n, n), slice(None))] = en
    ref[(*at, pl.ds(2 * n, es.shape[0]), slice(None))] = es


def choose(flag, a, b):
    return tuple(jnp.where(flag, x, y) for x, y in zip(a, b))


def identity(n):
    return jnp.where(eye_mask(n), 1.0, 0.0), jnp.zeros((n, n), f32), jnp.zeros((16, n), f32)


def local_kernel(subs, axes, mean_ref, init_ref, decay_ref, coup_ref, omap_ref, gain_ref, nf_ref, var_ref, seen_ref,
                 g_ref, delta_ref, shift_ref, diag_ref, sub_ref, total_ref, g_s, q_s, d_s, b_s):
    j = pl.program_id(0)
    steps = pl.num_programs(0)
    n = nf_ref.shape[0]
    m = omap_ref.shape[2]

    @pl.when(j == 0)
    def _():
        g_s[...] = jnp.zeros_like(g_s)
        q_s[...] = jnp.zeros_like(q_s)
        b_s[...] = jnp.zeros_like(b_s)
        d_s[...] = jnp.ones_like(d_s)

    @pl.when((j == 0) & (rank_of(axes) == 0))
    def _():
        q_s[0] = jnp.where(eye_mask(n), init_ref[...], 0.0)
        b_s[0] = jnp.broadcast_to(mean_ref[...], b_s.shape[1:])
        d_s[0] = jnp.zeros_like(d_s[0])

    nf = nf_ref[...]
    var_col = column(var_ref[...])
    obs_g = nn(omap_ref[...].reshape(subs * m, n), nf).astype(bf16)
    for s in range(subs):
        t = s * steps + j
        d_row = decay_ref[pl.ds(t, 1), :]
        d_col = column(d_row)
        coup = coup_ref[s, 0]
        gain = gain_ref[s, 0]
        omap = omap_ref[s, 0]
        gain32 = gain.astype(f32)
        obs_f = (omap.astype(f32) * d_row + nn(omap, coup)).astype(bf16)
        weighted = (gain32 * var_col).astype(bf16)
        gain_t = gain.T
        e = coup.astype(f32) - nn(gain_t, obs_f)
        shaped = (nf.astype(f32) - nn(gain_t, obs_g[s * m:(s + 1) * m])).astype(bf16)
        noise = nt(shaped, shaped) + nn(gain_t, weighted)
        shift = jnp.sum(gain32 * column(seen_ref[pl.ds(t, 1), :]), axis=0, keepdims=True)
        e_h, e_l = halves(e)
        g = g_s[s]
        q = q_s[s]
        delta = d_s[s, 0:1, :]
        b = b_s[s]
        g_new = d_col * g + e * delta + nn(e_h, g.astype(bf16))
        x = d_col * q + nn(e_h, q.astype(bf16))
        b_h, b_l = halves(b)
        y = nt(jnp.concatenate([x.astype(bf16), b_h, b_l], axis=0), e_h)
        q_new = x * d_row + y[:n] + noise
        b_new = d_row * b + (y[n:n + 16] + y[n + 16:] + nt(b_h, e_l)) + shift
        delta = delta * d_row
        g_s[s] = g_new
        q_s[s] = q_new
        b_s[s] = b_new
        d_s[s] = jnp.broadcast_to(delta, d_s.shape[1:])
        g_ref[s, 0] = g_new
        delta_ref[pl.ds(t, 1), :] = delta
        shift_ref[pl.ds(t, 1), :] = b_new[0:1, :]
        diag_ref[pl.ds(t, 1), :] = diag_row(q_new)

    @pl.when(j == steps - 1)
    def _():
        eye = eye_mask(n)
        for s in range(subs):
            sub_ref[s, 0:n, :] = g_s[s] + jnp.where(eye, d_s[s, 0:1, :], 0.0)
            sub_ref[s, n:2 * n, :] = q_s[s]
            sub_ref[s, 2 * n:, :] = b_s[s]
        pairs = [joined(load(sub_ref[s]), load(sub_ref[s + 1])) for s in (0, 2)]
        store(sub_ref, (subs,), pairs[0])
        store(total_ref, (), joined(*pairs))


def local_call(axes, init_mean, init_var, decay, coupling, obs_map, gain, noise_factor, obs_var, observed, subs=4):
    T, n = decay.shape
    m = obs_map.shape[1]
    steps = T // subs
    blk = lambda a, b: pl.BlockSpec((subs, 1, a, b), lambda j: (0, j, 0, 0))
    full = lambda *sh: pl.BlockSpec(sh, lambda j: (0,) * len(sh))
    return pl.pallas_call(
        functools.partial(local_kernel, subs, axes),
        grid=(steps,),
        in_specs=[full(1, n), full(1, n), full(T, n), blk(n, n), blk(m, n), blk(m, n), full(n, n), full(1, m), full(T, m)],
        out_specs=[blk(n, n), full(T, n), full(T, n), full(T, n),
                   full(subs + 1, 2 * n + 16, n), full(2 * n + 16, n)],
        out_shape=[
            jax.ShapeDtypeStruct((subs, steps, n, n), f32),
            jax.ShapeDtypeStruct((T, n), f32),
            jax.ShapeDtypeStruct((T, n), f32),
            jax.ShapeDtypeStruct((T, n), f32),
            jax.ShapeDtypeStruct((subs + 1, 2 * n + 16, n), f32),
            jax.ShapeDtypeStruct((2 * n + 16, n), f32),
        ],
        scratch_shapes=[
            pltpu.VMEM((subs, n, n), f32),
            pltpu.VMEM((subs, n, n), f32),
            pltpu.VMEM((subs, 8, n), f32),
            pltpu.VMEM((subs, 16, n), f32),
        ],
        compiler_params=pltpu.CompilerParams(vmem_limit_bytes=VMEM_LIMIT),
        name="local_steps",
    )(init_mean.reshape(1, n), init_var.reshape(1, n), decay, coupling.reshape(subs, steps, n, n), obs_map.reshape(subs, steps, m, n),
      gain.reshape(subs, steps, m, n), noise_factor, obs_var.reshape(1, m), observed)


def core_kernel(axes, own_ref, other_ref, total_ref, half_ref):
    upper = rank_of(axes) % 2 == 1
    own, other = load(own_ref[...]), load(other_ref[...])
    store(total_ref, (), joined(choose(upper, other, own), choose(upper, own, other)))
    put_half(half_ref, total_ref, upper)


def put_half(half_ref, total_ref, upper):
    rows = half_ref.shape[0]
    skip = total_ref.shape[0] - 2 * rows
    half_ref[...] = jnp.where(upper, total_ref[skip + rows:], total_ref[skip:skip + rows])


def whole(upper, mine_ref, others_ref):
    mine, others = mine_ref[...], others_ref[...]
    return jnp.concatenate([jnp.where(upper, others, mine), jnp.where(upper, mine, others)], axis=0)


def plane_kernel(axes, own_ref, r2, x2, r4, x4, r6, x6, token_ref, total_ref, half_ref, other_ref, first_ref):
    rank = rank_of(axes)
    upper, xbit, ybit = rank % 2 == 1, (rank // 2) % 2 == 1, (rank // 4) % 2 == 1
    own = load(own_ref[...])
    near = load(whole(upper, r2, x2))
    far = load(whole(upper, r4, x4))
    cross = load(whole(upper, r6, x6))
    first = choose(xbit, near, own)
    mine = joined(first, choose(xbit, own, near))
    other = joined(choose(xbit, cross, far), choose(xbit, far, cross))
    store(first_ref, (), first)
    store(other_ref, (), other)
    store(total_ref, (), joined(choose(ybit, other, mine), choose(ybit, mine, other)))
    put_half(half_ref, total_ref, upper)


def prefix_kernel(axes, first_ref, other_ref, core_ref, out_ref):
    rank = rank_of(axes)
    upper, xbit, ybit = rank % 2 == 1, (rank // 2) % 2 == 1, (rank // 4) % 2 == 1
    n = out_ref.shape[1]
    first = choose(xbit, load(first_ref[...]), identity(n))
    other = choose(ybit, load(other_ref[...]), identity(n))
    before = joined(other, first)
    store(out_ref, (), choose(upper, joined(before, load(core_ref[...])), before))


def level_kernel(axes, bit, own_ref, prefix_ref, r_ref, x_ref, total_ref, half_ref, out_ref):
    rank = rank_of(axes)
    upper, high = rank % 2 == 1, (rank // bit) % 2 == 1
    n = own_ref.shape[1]
    other = load(whole(upper, r_ref, x_ref))
    own = load(own_ref[...])
    store(total_ref, (), joined(choose(high, other, own), choose(high, own, other)))
    store(out_ref, (), choose(high, joined(other, load(prefix_ref[...])), load(prefix_ref[...])))
    put_half(half_ref, total_ref, upper)


def carry(element, noise, shift):
    em, en, es = element
    n = em.shape[1]
    lh, ll = halves(em)
    eh, el = halves(noise)
    x = nn(lh, eh) + (nn(ll, eh) + nn(lh, el))
    xh, xl = halves(jnp.concatenate([x, shift], axis=0))
    out = nt(xh, lh) + (nt(xl, lh) + nt(xh, ll))
    return out[:n] + en, out[n:] + es


def compose_kernel(per, g_ref, delta_ref, shift_ref, diag_ref, sub_ref, after_ref, out_ref, var_ref, mean_ref,
                   stack_s, col_s):
    s, i = pl.program_id(0), pl.program_id(1)
    n = g_ref.shape[-1]

    def use(element):
        stack_s[0:n, :] = element[0].T
        stack_s[n:2 * n, :] = element[1]
        col_s[...] = jnp.broadcast_to(column(element[2][0:1, :]), (n, 128))

    @pl.when((i == 0) & (s == 0))
    def _():
        use(identity(n))

    @pl.when((i == 0) & (s == 1))
    def _():
        use(load(sub_ref[0]))

    @pl.when((i == 0) & (s == 2))
    def _():
        use(load(sub_ref[4]))

    @pl.when((i == 0) & (s == 3))
    def _():
        use(joined(load(sub_ref[4]), load(sub_ref[2])))

    eye = eye_mask(n)
    lh, ll = halves(stack_s[...])
    col = jnp.concatenate([col_s[...], col_s[...]], axis=1)
    for k in range(per):
        t = (s * pl.num_programs(1) + i) * per + k
        phi = (g_ref[k] + jnp.where(eye, delta_ref[pl.ds(t, 1), :], 0.0)).T
        ph, plo = halves(phi)
        both = nn(lh, ph) + (nn(ll, ph) + nn(lh, plo))
        out_ref[k] = both[:n]
        var_ref[pl.ds(t, 1), :] = diag_ref[pl.ds(t, 1), :] + jnp.sum(phi * both[n:], axis=0, keepdims=True)
        mean_ref[pl.ds(t, 1), :] = shift_ref[pl.ds(t, 1), :] + jnp.sum(phi * col, axis=0, keepdims=True)


def finish_kernel(axes, bit, per, psi_ref, var_ref, mean_ref, place_ref, prefix_ref, r_ref, x_ref, means_ref, vars_ref,
                  p_s, col_s):
    i = pl.program_id(0)
    n = psi_ref.shape[-1]

    @pl.when(i == 0)
    def _():
        rank = rank_of(axes)
        upper, high = rank % 2 == 1, (rank // bit) % 2 == 1
        state = whole(upper, r_ref, x_ref)
        prefix = load(prefix_ref[...])
        noise, shift = carry(prefix, state[:n], state[n:])
        noise, shift = jnp.where(high, noise, prefix[1]), jnp.where(high, shift, prefix[2])
        noise, shift = carry(load(place_ref[...]), noise, shift)
        p_s[...] = noise
        col_s[...] = jnp.broadcast_to(column(shift[0:1, :]), (n, 128))

    eye = eye_mask(n)
    p = p_s[...]
    ph = p.astype(bf16)
    col = jnp.concatenate([col_s[...], col_s[...]], axis=1)
    for k in range(per):
        t = i * per + k
        psi = psi_ref[k]
        w = nn(ph, jnp.where(eye, 0.0, psi).astype(bf16)) + p * diag_row(psi)
        vars_ref[pl.ds(t, 1), :] = var_ref[pl.ds(t, 1), :] + jnp.sum(psi * w, axis=0, keepdims=True)
        means_ref[pl.ds(t, 1), :] = mean_ref[pl.ds(t, 1), :] + jnp.sum(psi * col, axis=0, keepdims=True)


PARAMS = pltpu.CompilerParams(vmem_limit_bytes=VMEM_LIMIT)


def call(kernel, name, shapes, *args):
    return pl.pallas_call(
        kernel,
        in_specs=[pl.BlockSpec(memory_space=pltpu.VMEM)] * len(args),
        out_specs=[pl.BlockSpec(memory_space=pltpu.VMEM)] * len(shapes),
        out_shape=[jax.ShapeDtypeStruct(s, f32) for s in shapes],
        compiler_params=PARAMS,
        name=name,
    )(*args)


def compose_call(g, delta, shift, diag, sub, after, per=4):
    subs, steps, n, _ = g.shape
    T = subs * steps
    full = lambda *sh: pl.BlockSpec(sh, lambda s, i: (0,) * len(sh))
    blk = pl.BlockSpec((per, n, n), lambda s, i: (s * (steps // per) + i, 0, 0))
    return pl.pallas_call(
        functools.partial(compose_kernel, per),
        grid=(subs, steps // per),
        in_specs=[blk, full(T, n), full(T, n), full(T, n), full(*sub.shape), pl.BlockSpec(memory_space=pl.ANY)],
        out_specs=[blk, full(T, n), full(T, n)],
        out_shape=[jax.ShapeDtypeStruct((T, n, n), f32), jax.ShapeDtypeStruct((T, n), f32),
                   jax.ShapeDtypeStruct((T, n), f32)],
        scratch_shapes=[pltpu.VMEM((2 * n, n), f32), pltpu.VMEM((n, 128), f32)],
        compiler_params=PARAMS,
        name="compose_steps",
    )(g.reshape(T, n, n), delta, shift, diag, sub, after)


def finish_call(axes, bit, psi, var, mean, place, prefix, r, x, per=4):
    T, n, _ = psi.shape
    full = lambda *sh: pl.BlockSpec(sh, lambda i: (0,) * len(sh))
    return pl.pallas_call(
        functools.partial(finish_kernel, axes, bit, per),
        grid=(T // per,),
        in_specs=[pl.BlockSpec((per, n, n), lambda i: (i, 0, 0)), full(T, n), full(T, n), full(*place.shape),
                  full(*prefix.shape), full(*r.shape), full(*x.shape)],
        out_specs=[full(T, n), full(T, n)],
        out_shape=[jax.ShapeDtypeStruct((T, n), f32)] * 2,
        scratch_shapes=[pltpu.VMEM((n, n), f32), pltpu.VMEM((n, 128), f32)],
        compiler_params=PARAMS,
        name="finish_steps",
    )(psi, var, mean, place, prefix, r, x)


def per_device(axes, init_mean, init_var, decay, coupling, obs_map, gain, noise_factor, obs_var, observed):
    n = decay.shape[1]
    count = 1
    for _, size in axes:
        count *= size
    names = tuple(name for name, _ in axes)

    def swap(x, bit):
        return lax.ppermute(x, names, [(k, k ^ bit) for k in range(count)])

    rows = 2 * n + 16
    part = rows // 2
    g, delta, shift, diag, sub, own = local_call(
        axes, init_mean, init_var, decay, coupling, obs_map, gain, noise_factor, obs_var, observed)
    other = swap(own, 1)
    chip, half = call(functools.partial(core_kernel, axes), "core_join", [(rows, n), (part, n)], own, other)
    got = [swap(half, bit) for bit in (2, 4, 6)]
    psi, var, mean = compose_call(g, delta, shift, diag, sub, chip)
    both = [x for r in got for x in (r, swap(r, 1))]
    bits = []
    bit = 8
    while bit < count:
        bits.append(bit)
        bit *= 2
    small = (n + 16) // 2
    total, half, second, first = call(
        functools.partial(plane_kernel, axes), "plane_join",
        [(rows, n), (part if len(bits) > 1 else small, n), (rows, n), (rows, n)], chip, *both, var)
    (place,) = call(functools.partial(prefix_kernel, axes), "place_join", [(rows, n)], first, second, other)
    prefix = jnp.concatenate([jnp.eye(n, dtype=f32), jnp.zeros((rows - n, n), f32)], axis=0)
    for k, bit in enumerate(bits[:-1]):
        r = swap(half, bit)
        total, half, prefix = call(
            functools.partial(level_kernel, axes, bit), "level_join",
            [(rows, n), (part if k < len(bits) - 2 else small, n), (rows, n)], total, prefix, r, swap(r, 1))
    r = swap(half, bits[-1])
    return tuple(finish_call(axes, bits[-1], psi, var, mean, place, prefix, r, swap(r, 1)))


def solution(mesh):
    axes = tuple((name, mesh.shape[name]) for name in mesh.axis_names)
    time = P(tuple(mesh.axis_names))
    return jax.shard_map(
        functools.partial(per_device, axes),
        mesh=mesh,
        in_specs=(P(), P(), time, time, time, time, P(), P(), time),
        out_specs=(time, time),
        check_vma=False,
    )
```

```python
import functools

import jax
import jax.numpy as jnp
from jax import lax
from jax.experimental import pallas as pl
from jax.experimental.pallas import tpu as pltpu
from jax.sharding import PartitionSpec as P

f32, bf16 = jnp.float32, jnp.bfloat16
PLANE = 8


def nn(a, b):
    return jnp.dot(a, b, preferred_element_type=f32)


def nt(a, b):
    return lax.dot_general(a, b, (((1,), (1,)), ((), ())), preferred_element_type=f32)


def halves(x):
    high = x.astype(bf16)
    return high, (x - high.astype(f32)).astype(bf16)


def times(late, early):
    (lh, ll), (eh, el) = late, early
    return nn(lh, eh) + (nn(ll, eh) + nn(lh, el))


def advance(late, noise, shift):
    n = noise.shape[1]
    lh, ll = late
    xh, xl = halves(jnp.concatenate([times(late, halves(noise)), shift], axis=0))
    out = nt(xh, lh) + (nt(xl, lh) + nt(xh, ll))
    return out[:n], out[n:]


def joined(early, late):
    parts = halves(late[0])
    noise, shift = advance(parts, early[1], early[2])
    return times(parts, halves(early[0])), noise + late[1], shift + late[2]


def eye_mask(n):
    return lax.broadcasted_iota(jnp.int32, (n, n), 0) == lax.broadcasted_iota(jnp.int32, (n, n), 1)


def column(row):
    n = row.shape[1]
    out = []
    for k in range(0, n, 128):
        m = min(128, n - k)
        out.append(jnp.sum(jnp.where(eye_mask(m), row[:, k:k + m], 0.0), axis=1, keepdims=True))
    return out[0] if len(out) == 1 else jnp.concatenate(out, axis=0)


def row_of(col):
    n = col.shape[0]
    out = [jnp.sum(jnp.where(eye_mask(128), col[k:k + 128], 0.0), axis=0, keepdims=True) for k in range(0, n, 128)]
    return jnp.concatenate(out, axis=1)


def diag_row(x):
    n = x.shape[1]
    out = [jnp.sum(jnp.where(eye_mask(128), x[k:k + 128, k:k + 128], 0.0), axis=0, keepdims=True)
           for k in range(0, n, 128)]
    return jnp.concatenate(out, axis=1)


def rows16(row):
    return jnp.broadcast_to(row, (16, row.shape[1]))


def pack(noise, shift):
    n = noise.shape[1]
    h = n // 2
    lower = lax.broadcasted_iota(jnp.int32, (h, h), 0) >= lax.broadcasted_iota(jnp.int32, (h, h), 1)
    a, b, c = noise[:h, :h], noise[:h, h:], noise[h:, h:]
    body = jnp.concatenate([jnp.where(lower, a, c), b], axis=1)
    extra = jnp.concatenate([jnp.zeros((1, h), f32), diag_row(noise)[:, h:]], axis=1)
    return jnp.concatenate([body, shift[0:1], extra, jnp.zeros((6, n), f32)], axis=0)


def unpack(x):
    n = x.shape[1]
    h = n // 2
    i = lax.broadcasted_iota(jnp.int32, (h, h), 0)
    j = lax.broadcasted_iota(jnp.int32, (h, h), 1)
    body, b = x[:h, :h], x[:h, h:]
    turned = body.T
    a = jnp.where(i >= j, body, turned)
    c = jnp.where(i == j, x[h + 1:h + 2, h:], jnp.where(i < j, body, turned))
    noise = jnp.concatenate([jnp.concatenate([a, b], axis=1), jnp.concatenate([b.T, c], axis=1)], axis=0)
    return noise, rows16(x[h:h + 1])


def rank_of(axes):
    rank = 0
    for name, size in axes:
        rank = rank * size + lax.axis_index(name)
    return rank


def bit_of(rank, bit):
    return (rank // bit) % 2


def whole(upper, mine_ref, others_ref):
    mine, others = mine_ref[...], others_ref[...]
    return jnp.concatenate([jnp.where(upper, others, mine), jnp.where(upper, mine, others)], axis=0)


def identity(n):
    return jnp.where(eye_mask(n), 1.0, 0.0), jnp.zeros((n, n), f32), jnp.zeros((16, n), f32)


def maps_kernel(subs, axes, mean_hbm, decay_hbm, coup_hbm, omap_hbm, gain_hbm, seen_hbm,
                g_ref, e_ref, dcol_ref, delta_ref, shift_ref, maps_ref, total_ref,
                mean_ref, decay_ref, coup_ref, omap_ref, gain_ref, seen_ref, small_sem, sem):
    n = decay_ref.shape[1]
    steps = coup_ref.shape[1]
    small = [pltpu.make_async_copy(x, y, small_sem.at[k]) for k, (x, y) in enumerate(
        [(mean_hbm, mean_ref), (decay_hbm, decay_ref), (seen_hbm, seen_ref)])]

    def chunk(j):
        return [pltpu.make_async_copy(x.at[:, j], y.at[:, j], sem.at[k, j]) for k, (x, y) in enumerate(
            [(coup_hbm, coup_ref), (omap_hbm, omap_ref), (gain_hbm, gain_ref)])]

    for c in small + chunk(0):
        c.start()
    for j in range(1, steps):
        for c in chunk(j):
            c.start()
    for c in small:
        c.wait()
    begins = rank_of(axes) == 0

    def step(j, first):
        for c in chunk(j):
            c.wait()
        for s in range(subs):
            t = s * steps + j
            d_row = decay_ref[pl.ds(t, 1), :]
            d_col = jnp.broadcast_to(column(d_row), (n, 128))
            dcol_ref[s, j] = d_col
            coup = coup_ref[s, j]
            gain = gain_ref[s, j]
            omap = omap_ref[s, j]
            obs_f = (omap.astype(f32) * d_row + nn(omap, coup)).astype(bf16)
            e = coup.astype(f32) - nn(gain.T, obs_f)
            e_h = e.astype(bf16)
            e_ref[s, j] = e_h
            shift = jnp.sum(gain.astype(f32) * column(seen_ref[pl.ds(t, 1), :]), axis=0, keepdims=True)
            if first and s > 0:
                g_ref[s, j] = e
                delta = d_row
                b_new = shift
            else:
                if first:
                    delta = jnp.where(begins, 0.0, jnp.ones((1, n), f32))
                    b = jnp.where(begins, mean_ref[...], 0.0)
                    g_ref[s, j] = e * delta
                else:
                    delta = delta_ref[pl.ds(t - 1, 1), :]
                    b = shift_ref[pl.ds(t - 1, 1), :]
                    g = g_ref[s, j - 1]
                    both = jnp.concatenate([d_col, d_col], axis=1)
                    g_ref[s, j] = both * g + e * delta + nn(e_h, g.astype(bf16))
                b_new = d_row * b + row_of(jnp.sum(e * b, axis=1, keepdims=True)) + shift
                delta = delta * d_row
            delta_ref[pl.ds(t, 1), :] = delta
            shift_ref[pl.ds(t, 1), :] = b_new

    step(0, True)
    lax.fori_loop(1, steps, lambda j, c: (step(j, False), c)[1], 0)

    eye = eye_mask(n)
    maps = [g_ref[s, steps - 1] + jnp.where(eye, delta_ref[(s + 1) * steps - 1:(s + 1) * steps, :], 0.0)
            for s in range(subs)]
    for s in range(subs):
        maps_ref[s] = maps[s]
    parts = [halves(m) for m in maps]
    low, high = times(parts[1], parts[0]), times(parts[3], parts[2])
    maps_ref[subs] = low
    maps_ref[subs + 1] = high
    total_ref[...] = times(halves(high), halves(low))


def noises_kernel(subs, axes, init_ref, decay_ref, e_ref, dcol_ref, omap_ref, gain_ref, nf_ref, var_ref, shift_ref,
                  maps_ref, diag_ref, noises_ref, total_ref, q_s):
    n = nf_ref.shape[0]
    m = omap_ref.shape[2]
    steps = e_ref.shape[1]
    nf = nf_ref[...]
    var_col = column(var_ref[...])

    def moved(s, j, q, noise):
        d_row = decay_ref[pl.ds(s * steps + j, 1), :]
        d_col = jnp.concatenate([dcol_ref[s, j], dcol_ref[s, j]], axis=1)
        x = d_col * q + nn(e_ref[s, j], q.astype(bf16))
        return x * d_row + nt(x.astype(bf16), e_ref[s, j]) + noise

    def step(j, first):
        obs_g = nn(jnp.concatenate([omap_ref[s, j] for s in range(subs)], axis=0), nf).astype(bf16)
        for s in range(subs):
            gain = gain_ref[s, j]
            weighted = (gain.astype(f32) * var_col).astype(bf16)
            gain_t = gain.T
            shaped = (nf.astype(f32) - nn(gain_t, obs_g[s * m:(s + 1) * m])).astype(bf16)
            q_new = nt(shaped, shaped) + nn(gain_t, weighted)
            if not first:
                q_new = moved(s, j, q_s[s], q_new)
            q_s[s] = q_new
            if first and s == 0:
                @pl.when(rank_of(axes) == 0)
                def _():
                    q_s[0] = moved(0, 0, jnp.where(eye_mask(n), init_ref[...], 0.0), q_s[0])
            diag_ref[pl.ds(s * steps + j, 1), :] = diag_row(q_s[s] if first else q_new)

    step(0, True)
    lax.fori_loop(1, steps, lambda j, c: (step(j, False), c)[1], 0)

    shift = [rows16(shift_ref[(s + 1) * steps - 1:(s + 1) * steps, :]) for s in range(subs)]
    pairs = []
    for s in (0, 2):
        noise, along = advance(halves(maps_ref[s + 1]), q_s[s], shift[s])
        pairs.append((noise + q_s[s + 1], along + shift[s + 1]))
    for s in range(subs):
        noises_ref[s, 0:n, :] = q_s[s]
        noises_ref[s, n:, :] = shift[s]
    noises_ref[subs, 0:n, :] = pairs[0][0]
    noises_ref[subs, n:, :] = pairs[0][1]
    noise, along = advance(halves(maps_ref[subs + 1]), *pairs[0])
    total_ref[...] = pack(noise + pairs[1][0], along + pairs[1][1])


def core_kernel(axes, own_map_ref, other_map_ref, own_ref, other_ref, out_ref):
    upper = rank_of(axes) % 2 == 1
    own, other = unpack(own_ref[...]), unpack(other_ref[...])
    late = halves(jnp.where(upper, own_map_ref[...], other_map_ref[...]))
    noise, shift = advance(late, *(jnp.where(upper, a, b) for a, b in zip(other, own)))
    out_ref[...] = pack(noise + jnp.where(upper, own[0], other[0]), shift + jnp.where(upper, own[1], other[1]))


def fetch(rank, refs, dst, sem):
    place = (rank % PLANE) // (PLANE // len(refs))
    copies = [pltpu.make_async_copy(r, dst.at[place ^ k], sem.at[k]) for k, r in enumerate(refs)]
    for c in copies:
        c.start()
    for c in copies:
        c.wait()


def plane_maps_kernel(axes, *refs):
    ins, (_, _, late_ref, total_ref, half_ref, picks_ref, map_s, chip_s, sem) = refs[:PLANE], refs[PLANE:]
    rank = rank_of(axes)
    fetch(rank, ins, map_s, sem)
    place = rank % PLANE
    y = bit_of(rank, 4)
    chips = []
    for k in range(4):
        late = halves(map_s[2 * k + 1])
        late_ref[k, 0], late_ref[k, 1] = late
        chips.append(times(late, halves(map_s[2 * k])))
        chip_s[k] = chips[k]
    pairs = []
    for k in range(2):
        late = halves(chips[2 * k + 1])
        late_ref[4 + k, 0], late_ref[4 + k, 1] = late
        pairs.append(times(late, halves(chips[2 * k])))
    late = halves(pairs[1])
    late_ref[6, 0], late_ref[6, 1] = late
    total_ref[...] = times(late, halves(pairs[0]))
    h = half_ref.shape[0]
    half_ref[...] = jnp.where(rank % 2 == 1, total_ref[h:], total_ref[:h])
    picks_ref[0] = pairs[0]
    picks_ref[1] = chip_s[2 * y]
    picks_ref[2] = map_s[place - place % 2]


def plane_noises_kernel(axes, *refs):
    ins, (late_ref, core_ref, total_ref, picks_ref, in_s, sem) = refs[:4], refs[4:]
    rank = rank_of(axes)
    fetch(rank, ins, in_s, sem)
    n = late_ref.shape[-1]

    def join(k, early, late):
        noise, shift = advance((late_ref[k, 0], late_ref[k, 1]), *early)
        return noise + late[0], shift + late[1]

    chips = [unpack(in_s[k]) for k in range(4)]
    pairs = [join(4 + k, chips[2 * k], chips[2 * k + 1]) for k in range(2)]
    total_ref[...] = pack(*join(6, pairs[0], pairs[1]))
    picks_ref[0, 0:n], picks_ref[0, n:] = pairs[0]
    picks_ref[1, 0:n], picks_ref[1, n:] = unpack(in_s[2 * bit_of(rank, 4)])
    picks_ref[2, 0:n], picks_ref[2, n:] = unpack(core_ref[...])


def level_kernel(axes, bit, own_map_ref, own_ref, r_ref, x_ref, other_ref, *outs):
    rank = rank_of(axes)
    upper, high = rank % 2 == 1, bit_of(rank, bit) == 1
    other_map, own_map = whole(upper, r_ref, x_ref), own_map_ref[...]
    other, own = unpack(other_ref[...]), unpack(own_ref[...])
    late = halves(jnp.where(high, own_map, other_map))
    noise, shift = advance(late, *(jnp.where(high, a, b) for a, b in zip(other, own)))
    outs[0][...] = pack(noise + jnp.where(high, own[0], other[0]), shift + jnp.where(high, own[1], other[1]))
    if len(outs) > 1:
        outs[1][...] = times(late, halves(jnp.where(high, other_map, own_map)))
        h = outs[2].shape[0]
        outs[2][...] = jnp.where(upper, outs[1][h:], outs[1][:h])


def place_kernel(axes, bits, maps_ref, noises_ref, *refs):
    out_ref = refs[-1]
    rank = rank_of(axes)
    upper = rank % 2 == 1
    n = out_ref.shape[1]
    before = identity(n)
    for k, bit in enumerate(bits):
        r_ref, x_ref, other_ref = refs[3 * k:3 * k + 3]
        other = (whole(upper, r_ref, x_ref), *unpack(other_ref[...]))
        new = other if k == 0 else joined(other, before)
        before = tuple(jnp.where(bit_of(rank, bit) == 1, a, b) for a, b in zip(new, before))
    one = identity(n)
    parts = []
    for k, bit in enumerate((4, 2, 1)):
        element = (maps_ref[k], noises_ref[k, 0:n], noises_ref[k, n:])
        parts.append(tuple(jnp.where(bit_of(rank, bit) == 1, a, b) for a, b in zip(element, one)))
    em, en, es = joined(joined(before, parts[0]), joined(parts[1], parts[2]))
    out_ref[0:n, :], out_ref[n:2 * n, :], out_ref[2 * n:, :] = em, en, es


def compose_kernel(sub, g_ref, delta_ref, shift_ref, diag_ref, maps_ref, noises_ref, token_ref,
                   out_ref, var_ref, mean_ref, stack_s, col_s):
    steps, n = out_ref.shape[:2]
    eye = eye_mask(n)

    def element(k):
        return maps_ref[k], noises_ref[k, 0:n, :], noises_ref[k, n:, :]

    if sub:
        em, en, es = element(0) if sub == 1 else element(4) if sub == 2 else joined(element(4), element(2))
        turned = em.T
        stack_s[0:n, :] = turned
        stack_s[n:2 * n, :] = en
        col_s[0] = jnp.broadcast_to(column(es[0:1, :]), (n, 128))
        col_s[1] = jnp.broadcast_to(column(diag_row(turned)), (n, 128))

    def step(j, carry):
        t = sub * steps + j
        turned = g_ref[sub, j].T
        delta = delta_ref[pl.ds(t, 1), :]
        phi = turned + jnp.where(eye, delta, 0.0)
        if sub:
            mask = jnp.concatenate([eye, jnp.zeros((n, n), jnp.bool_)], axis=0)
            stack = stack_s[...]
            both = stack * delta + nn(jnp.where(mask, 0.0, stack).astype(bf16), turned.astype(bf16))
            out_ref[j] = both[:n] + jnp.concatenate([col_s[1], col_s[1]], axis=1) * turned
            var_ref[pl.ds(j, 1), :] = diag_ref[pl.ds(t, 1), :] + jnp.sum(phi * both[n:], axis=0, keepdims=True)
            mean_ref[pl.ds(j, 1), :] = shift_ref[pl.ds(t, 1), :] + jnp.sum(
                phi * jnp.concatenate([col_s[0], col_s[0]], axis=1), axis=0, keepdims=True)
        else:
            out_ref[j] = phi
            var_ref[pl.ds(j, 1), :] = diag_ref[pl.ds(t, 1), :]
            mean_ref[pl.ds(j, 1), :] = shift_ref[pl.ds(t, 1), :]
        return carry

    lax.fori_loop(0, steps, step, 0, unroll=2)


def finish_kernel(axes, bit, parts, *refs):
    psi = refs[:parts]
    var = refs[parts:2 * parts]
    mean = refs[2 * parts:3 * parts]
    place_ref, r_ref, means_ref, vars_ref, p_s, col_s = refs[3 * parts:]
    n = p_s.shape[1]
    high = bit_of(rank_of(axes), bit) == 1
    noise, shift = advance(halves(place_ref[0:n, :]), *unpack(r_ref[...]))
    p_s[...] = jnp.where(high, noise, 0.0) + place_ref[n:2 * n, :]
    shift = jnp.where(high, shift, 0.0) + place_ref[2 * n:, :]
    col_s[...] = jnp.broadcast_to(column(shift[0:1, :]), (n, 128))
    eye = eye_mask(n)
    steps = psi[0].shape[0]

    def step(j, carry):
        p = p_s[...]
        ph = p.astype(bf16)
        col = jnp.concatenate([col_s[...], col_s[...]], axis=1)
        for a in range(parts):
            to = a * steps + j
            x = psi[a][j]
            w = nn(ph, jnp.where(eye, 0.0, x).astype(bf16)) + p * diag_row(x)
            vars_ref[pl.ds(to, 1), :] = var[a][pl.ds(j, 1), :] + jnp.sum(x * w, axis=0, keepdims=True)
            means_ref[pl.ds(to, 1), :] = mean[a][pl.ds(j, 1), :] + jnp.sum(x * col, axis=0, keepdims=True)
        return carry

    lax.fori_loop(0, steps, step, 0)


def vmem():
    return pl.BlockSpec(memory_space=pltpu.VMEM)


def anywhere():
    return pl.BlockSpec(memory_space=pl.ANY)


def shape(*dims, dtype=f32):
    return jax.ShapeDtypeStruct(dims, dtype)


def call(kernel, name, outs, args, specs=None, scratch=(), limit=16, flops=10 ** 9):
    return pl.pallas_call(
        kernel,
        in_specs=specs or [vmem()] * len(args),
        out_specs=[vmem()] * len(outs),
        out_shape=outs,
        scratch_shapes=scratch,
        compiler_params=pltpu.CompilerParams(vmem_limit_bytes=limit * 1024 * 1024),
        cost_estimate=pl.CostEstimate(flops=flops, bytes_accessed=0, transcendentals=0),
        name=name,
    )(*args)


def hbm():
    return pl.BlockSpec(memory_space=pltpu.HBM)


def step_maps(axes, subs, init_mean, decay, coupling, obs_map, gain, observed):
    T, n = decay.shape
    m = obs_map.shape[1]
    steps = T // subs
    outs = [shape(subs, steps, n, n), shape(subs, steps, n, n, dtype=bf16), shape(subs, steps, n, 128),
            shape(T, n), shape(T, n), shape(subs + 2, n, n), shape(n, n)]
    args = [init_mean.reshape(1, n), decay, coupling.reshape(subs, steps, n, n), obs_map.reshape(subs, steps, m, n),
            gain.reshape(subs, steps, m, n), observed]
    scratch = [pltpu.VMEM(x.shape, x.dtype) for x in args]
    args = [pltpu.with_memory_space_constraint(x, pltpu.HBM) for x in args]
    scratch += [pltpu.SemaphoreType.DMA((3,)), pltpu.SemaphoreType.DMA((3, steps))]
    return call(functools.partial(maps_kernel, subs, axes), "step_maps", outs, args, [hbm()] * len(args), scratch,
                limit=20, flops=10 ** 10)


def step_noises(axes, subs, init_var, decay, e, dcol, obs_map, gain, noise_factor, obs_var, shift, maps):
    T, n = decay.shape
    m = obs_map.shape[1]
    steps = T // subs
    args = [init_var.reshape(1, n), decay, e, dcol, obs_map.reshape(subs, steps, m, n),
            gain.reshape(subs, steps, m, n), noise_factor, obs_var.reshape(1, m), shift, maps]
    return call(functools.partial(noises_kernel, subs, axes), "step_noises",
                [shape(T, n), shape(subs + 1, n + 16, n), shape(n // 2 + 8, n)], args,
                scratch=[pltpu.VMEM((subs, n, n), f32)])


def compose(sub, g, delta, shift, diag, maps, noises, token):
    _, steps, n, _ = g.shape
    return call(functools.partial(compose_kernel, sub), "compose",
                [shape(steps, n, n), shape(steps, n), shape(steps, n)],
                [g, delta, shift, diag, maps, noises, token], [vmem()] * 6 + [anywhere()],
                [pltpu.VMEM((2 * n, n), f32), pltpu.VMEM((2, n, 128), f32)], flops=4 * 10 ** 9)


def finish(axes, bit, composed, place, r):
    parts = len(composed)
    T, n, _ = composed[0][0].shape
    psi, var, mean = zip(*composed)
    return call(functools.partial(finish_kernel, axes, bit, parts), "finish", [shape(parts * T, n)] * 2,
                [*psi, *var, *mean, place, r], scratch=[pltpu.VMEM((n, n), f32), pltpu.VMEM((n, 128), f32)])


def per_device(axes, init_mean, init_var, decay, coupling, obs_map, gain, noise_factor, obs_var, observed):
    n = decay.shape[1]
    h = n // 2
    subs = 4
    count = 1
    for _, size in axes:
        count *= size
    names = tuple(name for name, _ in axes)

    def swap(x, bit):
        return lax.ppermute(x, names, [(k, k ^ bit) for k in range(count)])

    bits = []
    bit = PLANE
    while bit < count:
        bits.append(bit)
        bit *= 2

    g, e, dcol, delta, shift, maps, own = step_maps(axes, subs, init_mean, decay, coupling, obs_map, gain, observed)
    far = [swap(own, bit) for bit in (2, 4, 6)]
    other = swap(own, 1)
    diag, noises, packed = step_noises(
        axes, subs, init_var, decay, e, dcol, obs_map, gain, noise_factor, obs_var, shift, maps)
    other_packed = swap(packed, 1)
    (chip,) = call(functools.partial(core_kernel, axes), "core_noises", [shape(h + 8, n)],
                   [own, other, packed, other_packed])
    chips = [chip] + [swap(chip, bit) for bit in (2, 4, 6)]
    *far, token = lax.optimization_barrier((*far, chip))
    all_maps = [own, other] + [v for r in far for v in (r, swap(r, 1))]
    composed = [compose(k, g, delta, shift, diag, maps, noises, token) for k in (0, 1)]
    late, total, half, map_picks = call(
        functools.partial(plane_maps_kernel, axes), "plane_maps",
        [shape(PLANE - 1, 2, n, n, dtype=bf16), shape(n, n), shape(h, n), shape(3, n, n)],
        [*all_maps, composed[0][1], composed[1][1]], [anywhere()] * (PLANE + 2),
        [pltpu.VMEM((PLANE, n, n), f32), pltpu.VMEM((4, n, n), f32), pltpu.SemaphoreType.DMA((PLANE,))])
    packed, noise_picks = call(
        functools.partial(plane_noises_kernel, axes), "plane_noises",
        [shape(h + 8, n), shape(3, n + 16, n)],
        [*chips, late, other_packed], [anywhere()] * 4 + [vmem()] * 2,
        [pltpu.VMEM((4, h + 8, n), f32), pltpu.SemaphoreType.DMA((4,))])
    received = []
    for k, bit in enumerate(bits[:-1]):
        r = swap(half, bit)
        got = (r, swap(r, 1), swap(packed, bit))
        received += got
        more = k < len(bits) - 2
        new = call(functools.partial(level_kernel, axes, bit), "level",
                   [shape(h + 8, n)] + ([shape(n, n), shape(h, n)] if more else []), [total, packed, *got])
        if k == 0:
            composed.append(compose(2, g, delta, shift, diag, maps, noises, packed))
        packed = new[0]
        if more:
            total, half = new[1:]
    (place,) = call(functools.partial(place_kernel, axes, bits[:-1]), "place", [shape(2 * n + 16, n)],
                    [map_picks, noise_picks, *received], flops=10 ** 6)
    r = swap(packed, bits[-1])
    composed.append(compose(3, g, delta, shift, diag, maps, noises, packed))
    return tuple(finish(axes, bits[-1], composed, place, r))


def solution(mesh):
    axes = tuple((name, mesh.shape[name]) for name in mesh.axis_names)
    time = P(tuple(mesh.axis_names))
    return jax.shard_map(
        functools.partial(per_device, axes),
        mesh=mesh,
        in_specs=(P(), P(), time, time, time, time, P(), P(), time),
        out_specs=(time, time),
        check_vma=False,
    )
```

```python
import functools

import jax
import jax.numpy as jnp
from jax import lax
from jax.experimental import pallas as pl
from jax.experimental.pallas import tpu as pltpu
from jax.sharding import PartitionSpec as P

f32, bf16 = jnp.float32, jnp.bfloat16
PLANE = 8


def nn(a, b):
    return jnp.dot(a, b, preferred_element_type=f32)


def nt(a, b):
    return lax.dot_general(a, b, (((1,), (1,)), ((), ())), preferred_element_type=f32)


def halves(x):
    high = x.astype(bf16)
    return high, (x - high.astype(f32)).astype(bf16)


def times(late, early):
    (lh, ll), (eh, el) = late, early
    return nn(lh, eh) + (nn(ll, eh) + nn(lh, el))


def advance(late, noise, shift):
    n = noise.shape[1]
    lh, ll = late
    xh, xl = halves(jnp.concatenate([times(late, halves(noise)), shift], axis=0))
    out = nt(xh, lh) + (nt(xl, lh) + nt(xh, ll))
    return out[:n], out[n:]


def wide(col):
    return jnp.concatenate([col, col], axis=1)


def apart(late):
    row = diag_row(late)
    return row, spread(row), jnp.where(eye_mask(late.shape[0]), 0.0, late).astype(bf16)


def conjugate(late, noise):
    row, col, rest = late
    x = wide(col) * noise + nn(rest, noise.astype(bf16))
    return x * row + nt(x.astype(bf16), rest)


def through(late, shift):
    return row_of(jnp.sum(late * shift, axis=1, keepdims=True))


def joined(early, late):
    parts = halves(late[0])
    noise, shift = advance(parts, early[1], early[2])
    return times(parts, halves(early[0])), noise + late[1], shift + late[2]


def eye_mask(n):
    return lax.broadcasted_iota(jnp.int32, (n, n), 0) == lax.broadcasted_iota(jnp.int32, (n, n), 1)


def column(row):
    n = row.shape[1]
    out = []
    for k in range(0, n, 128):
        m = min(128, n - k)
        out.append(jnp.sum(jnp.where(eye_mask(m), row[:, k:k + m], 0.0), axis=1, keepdims=True))
    return out[0] if len(out) == 1 else jnp.concatenate(out, axis=0)


def spread(row):
    n = row.shape[1]
    return jnp.concatenate([jnp.broadcast_to(row[:, k:k + 128], (128, 128)).T for k in range(0, n, 128)], axis=0)


def row_of(col):
    n = col.shape[0]
    out = [jnp.sum(jnp.where(eye_mask(128), col[k:k + 128], 0.0), axis=0, keepdims=True) for k in range(0, n, 128)]
    return jnp.concatenate(out, axis=1)


def diag_row(x):
    n = x.shape[1]
    out = [jnp.sum(jnp.where(eye_mask(128), x[k:k + 128, k:k + 128], 0.0), axis=0, keepdims=True)
           for k in range(0, n, 128)]
    return jnp.concatenate(out, axis=1)


def rows16(row):
    return jnp.broadcast_to(row, (16, row.shape[1]))


def pack(noise, shift):
    n = noise.shape[1]
    h = n // 2
    lower = lax.broadcasted_iota(jnp.int32, (h, h), 0) >= lax.broadcasted_iota(jnp.int32, (h, h), 1)
    a, b, c = noise[:h, :h], noise[:h, h:], noise[h:, h:]
    body = jnp.concatenate([jnp.where(lower, a, c), b], axis=1)
    extra = jnp.concatenate([jnp.zeros((1, h), f32), diag_row(noise)[:, h:]], axis=1)
    return jnp.concatenate([body, shift[0:1], extra, jnp.zeros((6, n), f32)], axis=0)


def unpack(x):
    n = x.shape[1]
    h = n // 2
    i = lax.broadcasted_iota(jnp.int32, (h, h), 0)
    j = lax.broadcasted_iota(jnp.int32, (h, h), 1)
    body, b = x[:h, :h], x[:h, h:]
    turned = body.T
    a = jnp.where(i >= j, body, turned)
    c = jnp.where(i == j, x[h + 1:h + 2, h:], jnp.where(i < j, body, turned))
    noise = jnp.concatenate([jnp.concatenate([a, b], axis=1), jnp.concatenate([b.T, c], axis=1)], axis=0)
    return noise, x[h:h + 1]


def rank_of(axes):
    rank = 0
    for name, size in axes:
        rank = rank * size + lax.axis_index(name)
    return rank


def bit_of(rank, bit):
    return (rank // bit) % 2


def whole(upper, mine_ref, others_ref):
    mine, others = mine_ref[...], others_ref[...]
    return jnp.concatenate([jnp.where(upper, others, mine), jnp.where(upper, mine, others)], axis=0)


def identity(n):
    return jnp.where(eye_mask(n), 1.0, 0.0), jnp.zeros((n, n), f32), jnp.zeros((16, n), f32)


def maps_kernel(subs, axes, mean_hbm, decay_hbm, coup_hbm, omap_hbm, gain_hbm, seen_hbm,
                g_ref, e_ref, dcol_ref, delta_ref, shift_ref, maps_ref, total_ref,
                mean_ref, decay_ref, coup_ref, omap_ref, gain_ref, seen_ref, small_sem, sem, g_s, part_s, eh_s, row_s):
    n = decay_ref.shape[1]
    steps = coup_ref.shape[1]
    small = [pltpu.make_async_copy(x, y, small_sem.at[k]) for k, (x, y) in enumerate(
        [(mean_hbm, mean_ref), (decay_hbm, decay_ref), (seen_hbm, seen_ref)])]

    def chunk(j):
        return [pltpu.make_async_copy(x.at[:, j], y.at[:, j], sem.at[k, j]) for k, (x, y) in enumerate(
            [(coup_hbm, coup_ref), (omap_hbm, omap_ref), (gain_hbm, gain_ref)])]

    for c in small + chunk(0):
        c.start()
    for j in range(1, steps):
        for c in chunk(j):
            c.start()
    for c in small:
        c.wait()
    begins = rank_of(axes) == 0

    def step(j, first):
        for c in chunk(j):
            c.wait()
        all_subs = range(subs)
        rows = [decay_ref[pl.ds(s * steps + j, 1), :] for s in all_subs]
        obs_f = [(omap_ref[s, j].astype(f32) * rows[s] + nn(omap_ref[s, j], coup_ref[s, j])).astype(bf16)
                 for s in all_subs]

        def build(s):
            t = s * steps + j
            gain = gain_ref[s, j]
            e = coup_ref[s, j].astype(f32) - nn(gain.T, obs_f[s])
            e_h = e.astype(bf16)
            e_ref[s, j] = e_h
            eh_s[s] = e_h
            col = spread(rows[s])
            dcol_ref[s, j] = col
            if first:
                start = (s == 0) & begins
                delta = jnp.where(start, 0.0, jnp.ones((1, n), f32))
                b = jnp.where(start, mean_ref[...], 0.0)
                g_new = e * delta
                g_s[s] = g_new
                g_ref[s, j] = g_new
            else:
                delta = row_s[s, 0:1, :]
                b = row_s[s, 1:2, :]
                part_s[s] = jnp.concatenate([col, col], axis=1) * g_s[s] + e * delta
            along = row_of(jnp.sum(e * b, axis=1, keepdims=True))
            shift = jnp.sum(gain.astype(f32) * column(seen_ref[pl.ds(t, 1), :]), axis=0, keepdims=True)
            b_new = rows[s] * b + along + shift
            shift_ref[pl.ds(t, 1), :] = b_new
            delta_ref[pl.ds(t, 1), :] = delta * rows[s]
            row_s[s, 0:1, :] = delta * rows[s]
            row_s[s, 1:2, :] = b_new

        def follow(s):
            if not first:
                g_new = part_s[s] + nn(eh_s[s], g_s[s].astype(bf16))
                g_s[s] = g_new
                g_ref[s, j] = g_new

        build(0)
        build(1)
        follow(0)
        build(2)
        follow(1)
        build(3)
        follow(2)
        follow(3)

    step(0, True)
    lax.fori_loop(1, steps, lambda j, c: (step(j, False), c)[1], 0)

    eye = eye_mask(n)
    maps = [g_ref[s, steps - 1] + jnp.where(eye, delta_ref[(s + 1) * steps - 1:(s + 1) * steps, :], 0.0)
            for s in range(subs)]
    for s in range(subs):
        maps_ref[s] = maps[s]
    parts = [halves(m) for m in maps]
    low, high = times(parts[1], parts[0]), times(parts[3], parts[2])
    maps_ref[subs] = low
    maps_ref[subs + 1] = high
    total_ref[...] = times(halves(high), halves(low))


def noises_kernel(subs, axes, init_ref, decay_ref, e_ref, dcol_ref, omap_ref, gain_ref, nf_ref, var_ref, shift_ref,
                  maps_ref, diag_ref, noises_ref, total_ref, q_s, shaped_s):
    n = nf_ref.shape[0]
    m = omap_ref.shape[2]
    steps = e_ref.shape[1]
    nf = nf_ref[...]
    var_col = column(var_ref[...])

    all_subs = range(subs)

    def shape_step(j, slot):
        obs_g = nn(jnp.concatenate([omap_ref[s, j] for s in all_subs], axis=0), nf).astype(bf16)
        for s in all_subs:
            shaped_s[slot, s] = (nf.astype(f32) - nn(gain_ref[s, j].T, obs_g[s * m:(s + 1) * m])).astype(bf16)

    def noise(s, j, slot):
        shaped, gain = shaped_s[slot, s], gain_ref[s, j]
        return nt(shaped, shaped) + nn(gain.T, (gain.astype(f32) * var_col).astype(bf16))

    def first_half(s, j, q):
        d_col = jnp.concatenate([dcol_ref[s, j], dcol_ref[s, j]], axis=1)
        return d_col * q + nn(e_ref[s, j], q.astype(bf16))

    def second_half(s, j, slot, x):
        return x * decay_ref[pl.ds(s * steps + j, 1), :] + (nt(x.astype(bf16), e_ref[s, j]) + noise(s, j, slot))

    def step(j, carry):
        slot = j % 2
        x = [first_half(s, j, q_s[s]) for s in all_subs]
        shape_step(jnp.minimum(j + 1, steps - 1), 1 - slot)
        for s in all_subs:
            q_new = second_half(s, j, slot, x[s])
            q_s[s] = q_new
            diag_ref[pl.ds(s * steps + j, 1), :] = diag_row(q_new)
        return carry

    shape_step(0, 0)
    shape_step(1, 1)
    for s in all_subs:
        q_s[s] = noise(s, 0, 0)

    @pl.when(rank_of(axes) == 0)
    def _():
        q_s[0] = second_half(0, 0, 0, first_half(0, 0, jnp.where(eye_mask(n), init_ref[...], 0.0)))

    for s in all_subs:
        diag_ref[pl.ds(s * steps, 1), :] = diag_row(q_s[s])
    lax.fori_loop(1, steps, step, 0)

    shift = [shift_ref[(s + 1) * steps - 1:(s + 1) * steps, :] for s in range(subs)]
    pairs = [(conjugate(apart(maps_ref[s + 1]), q_s[s]) + q_s[s + 1], through(maps_ref[s + 1], shift[s]) + shift[s + 1])
             for s in (0, 2)]
    last = maps_ref[subs + 1]
    total_ref[...] = pack(conjugate(apart(last), pairs[0][0]) + pairs[1][0], through(last, pairs[0][1]) + pairs[1][1])
    for s in range(subs):
        noises_ref[s, 0:n, :] = q_s[s]
        noises_ref[s, n:, :] = rows16(shift[s])


def core_kernel(axes, own_map_ref, other_map_ref, own_ref, other_ref, out_ref):
    upper = rank_of(axes) % 2 == 1
    own, other = unpack(own_ref[...]), unpack(other_ref[...])
    late = jnp.where(upper, own_map_ref[...], other_map_ref[...])
    early_noise, early_shift = (jnp.where(upper, a, b) for a, b in zip(other, own))
    late_noise, late_shift = (jnp.where(upper, a, b) for a, b in zip(own, other))
    out_ref[...] = pack(conjugate(apart(late), early_noise) + late_noise, through(late, early_shift) + late_shift)


def fetch(rank, refs, dst, sem):
    place = (rank % PLANE) // (PLANE // len(refs))
    copies = [pltpu.make_async_copy(r, dst.at[place ^ k], sem.at[k]) for k, r in enumerate(refs)]
    for c in copies:
        c.start()
    for c in copies:
        c.wait()


def plane_maps_kernel(axes, *refs):
    ins, refs = refs[:PLANE], refs[PLANE:]
    late_ref, rest_ref, col_ref, row_ref, total_ref, half_ref, picks_ref, map_s, chip_s, sem = refs
    rank = rank_of(axes)
    fetch(rank, ins, map_s, sem)
    place = rank % PLANE
    y = bit_of(rank, 4)

    def keep(k, late):
        late_ref[k] = late
        row_ref[k:k + 1, :], col_ref[k], rest_ref[k] = apart(late)

    chips = [times(halves(map_s[2 * k + 1]), halves(map_s[2 * k])) for k in range(4)]
    for k in range(4):
        chip_s[k] = chips[k]
    pairs = [times(halves(chips[2 * k + 1]), halves(chips[2 * k])) for k in range(2)]
    total_ref[...] = times(halves(pairs[1]), halves(pairs[0]))
    for k, late in enumerate((chips[1], chips[3], pairs[1])):
        keep(k, late)
    h = half_ref.shape[0]
    half_ref[...] = jnp.where(rank % 2 == 1, total_ref[h:], total_ref[:h])
    picks_ref[0] = pairs[0]
    picks_ref[1] = chip_s[2 * y]
    picks_ref[2] = map_s[place - place % 2]


def plane_noises_kernel(axes, *refs):
    ins, (late_ref, rest_ref, col_ref, row_ref, core_ref, _, _, total_ref, picks_ref, in_s, sem) = refs[:4], refs[4:]
    rank = rank_of(axes)
    fetch(rank, ins, in_s, sem)
    n = late_ref.shape[-1]

    def join(k, early, late):
        noise = conjugate((row_ref[k:k + 1, :], col_ref[k], rest_ref[k]), early[0])
        return noise + late[0], through(late_ref[k], early[1]) + late[1]

    def pick(k, element):
        picks_ref[k, 0:n], picks_ref[k, n:] = element[0], rows16(element[1])

    chips = [unpack(in_s[k]) for k in range(4)]
    pairs = [join(k, chips[2 * k], chips[2 * k + 1]) for k in range(2)]
    total_ref[...] = pack(*join(2, pairs[0], pairs[1]))
    pick(0, pairs[0])
    pick(1, unpack(in_s[2 * bit_of(rank, 4)]))
    pick(2, unpack(core_ref[...]))


def level_kernel(axes, bit, own_map_ref, own_ref, r_ref, x_ref, other_ref, inner_ref, token_ref, *outs):
    rank = rank_of(axes)
    upper, high = rank % 2 == 1, bit_of(rank, bit) == 1
    other_map, own_map = whole(upper, r_ref, x_ref), own_map_ref[...]
    other, own = unpack(other_ref[...]), unpack(own_ref[...])
    late = jnp.where(high, own_map, other_map)
    early_noise, early_shift = (jnp.where(high, a, b) for a, b in zip(other, own))
    late_noise, late_shift = (jnp.where(high, a, b) for a, b in zip(own, other))
    outs[0][...] = pack(conjugate(apart(late), early_noise) + late_noise, through(late, early_shift) + late_shift)
    if len(outs) > 1:
        outs[1][...] = times(halves(late), halves(jnp.where(high, other_map, own_map)))
        h = outs[2].shape[0]
        outs[2][...] = jnp.where(upper, outs[1][h:], outs[1][:h])


def inner_kernel(axes, maps_ref, noises_ref, out_ref):
    rank = rank_of(axes)
    n = out_ref.shape[1]
    one = identity(n)
    parts = []
    for k, bit in enumerate((4, 2, 1)):
        element = (maps_ref[k], noises_ref[k, 0:n, :], noises_ref[k, n:, :])
        parts.append(tuple(jnp.where(bit_of(rank, bit) == 1, a, b) for a, b in zip(element, one)))
    em, en, es = joined(parts[0], joined(parts[1], parts[2]))
    out_ref[0:n, :], out_ref[n:2 * n, :], out_ref[2 * n:, :] = em, en, es


def place_kernel(axes, bits, subs_ref, sub_noises_ref, inner_ref, *refs):
    out_ref, rest_ref, col_ref, row_ref = refs[-4:]
    rank = rank_of(axes)
    upper = rank % 2 == 1
    n = out_ref.shape[2]
    before = identity(n)
    for k, bit in enumerate(bits):
        r_ref, x_ref, other_ref = refs[3 * k:3 * k + 3]
        noise, shift = unpack(other_ref[...])
        other = whole(upper, r_ref, x_ref), noise, rows16(shift)
        new = other if k == 0 else joined(other, before)
        before = tuple(jnp.where(bit_of(rank, bit) == 1, a, b) for a, b in zip(new, before))
    inner = inner_ref[0:n, :], inner_ref[n:2 * n, :], inner_ref[2 * n:, :]

    def put(s, element):
        em, en, es = element
        out_ref[s, 0:n, :], out_ref[s, n:2 * n, :], out_ref[s, 2 * n:, :] = em, en, es

    def sub(s, carry):
        before = out_ref[s, 0:n, :], out_ref[s, n:2 * n, :], out_ref[s, 2 * n:, :]
        put(s + 1, joined(before, (subs_ref[s], sub_noises_ref[s, 0:n, :], sub_noises_ref[s, n:, :])))
        return carry

    put(0, joined(before, inner))
    lax.fori_loop(0, out_ref.shape[0] - 1, sub, 0)

    def split(s, carry):
        row_ref[s, 0:1, :], col_ref[s], rest_ref[s] = apart(out_ref[s, 0:n, :])
        return carry

    lax.fori_loop(0, out_ref.shape[0], split, 0)


def turn_kernel(sub, g_ref, delta_ref, token_ref, high_ref, low_ref, diag_ref):
    steps, n = high_ref.shape[:2]
    eye = eye_mask(n)

    def step(j, carry):
        turned = g_ref[sub, j].T
        diag_ref[pl.ds(j, 1), :] = delta_ref[pl.ds(sub * steps + j, 1), :] + diag_row(turned)
        high_ref[j], low_ref[j] = halves(jnp.where(eye, 0.0, turned))
        return carry

    lax.fori_loop(0, steps, step, 0, unroll=2)


def finish_kernel(axes, bit, parts, *refs):
    high, low, diag = refs[:parts], refs[parts:2 * parts], refs[2 * parts:3 * parts]
    var_ref, mean_ref, place_ref, rest_ref, col_ref, arow_ref, r_ref, means_ref, vars_ref, left_s, row_s = refs[3 * parts:]
    n = left_s.shape[-1]
    steps = high[0].shape[0]
    is_high = bit_of(rank_of(axes), bit) == 1
    received, moved = unpack(r_ref[...])
    for s in range(parts):
        noise = conjugate((arow_ref[s, 0:1, :], col_ref[s], rest_ref[s]), received)
        p = jnp.where(is_high, noise, 0.0) + place_ref[s, n:2 * n, :]
        mean = jnp.where(is_high, through(place_ref[s, 0:n, :], moved), 0.0) + place_ref[s, 2 * n:2 * n + 1, :]
        mh, ml = halves(mean)
        left_s[s, 0:n, :] = p.astype(bf16)
        left_s[s, n:, :] = jnp.concatenate([mh, ml, jnp.zeros((14, n), bf16)], axis=0)
        row_s[s, 0:1, :] = mean
        row_s[s, 1:2, :] = diag_row(p)

    def step(j, carry):
        both = [nn(left_s[s], high[s][j]) for s in range(parts)]
        rest = [nn(left_s[s, n:, :], low[s][j]) for s in range(parts)]
        for s in range(parts):
            t = s * steps + j
            d = diag[s][pl.ds(j, 1), :]
            vars_ref[pl.ds(t, 1), :] = (var_ref[pl.ds(t, 1), :] + d * (d * row_s[s, 1:2, :] + 2.0 * diag_row(both[s]))
                                        + jnp.sum(high[s][j].astype(f32) * both[s][:n], axis=0, keepdims=True))
            means_ref[pl.ds(t, 1), :] = (mean_ref[pl.ds(t, 1), :] + d * row_s[s, 0:1, :]
                                         + both[s][n:n + 1] + (both[s][n + 1:n + 2] + rest[s][0:1]))
        return carry

    lax.fori_loop(0, steps, step, 0)


def vmem():
    return pl.BlockSpec(memory_space=pltpu.VMEM)


def anywhere():
    return pl.BlockSpec(memory_space=pl.ANY)


def shape(*dims, dtype=f32):
    return jax.ShapeDtypeStruct(dims, dtype)


def call(kernel, name, outs, args, specs=None, scratch=(), limit=16, flops=10 ** 9):
    return pl.pallas_call(
        kernel,
        in_specs=specs or [vmem()] * len(args),
        out_specs=[vmem()] * len(outs),
        out_shape=outs,
        scratch_shapes=scratch,
        compiler_params=pltpu.CompilerParams(vmem_limit_bytes=limit * 1024 * 1024),
        cost_estimate=pl.CostEstimate(flops=flops, bytes_accessed=0, transcendentals=0),
        name=name,
    )(*args)


def hbm():
    return pl.BlockSpec(memory_space=pltpu.HBM)


def step_maps(axes, subs, init_mean, decay, coupling, obs_map, gain, observed):
    T, n = decay.shape
    m = obs_map.shape[1]
    steps = T // subs
    outs = [shape(subs, steps, n, n), shape(subs, steps, n, n, dtype=bf16), shape(subs, steps, n, 128),
            shape(T, n), shape(T, n), shape(subs + 2, n, n), shape(n, n)]
    args = [init_mean.reshape(1, n), decay, coupling.reshape(subs, steps, n, n), obs_map.reshape(subs, steps, m, n),
            gain.reshape(subs, steps, m, n), observed]
    scratch = [pltpu.VMEM(x.shape, x.dtype) for x in args]
    args = [pltpu.with_memory_space_constraint(x, pltpu.HBM) for x in args]
    scratch += [pltpu.SemaphoreType.DMA((3,)), pltpu.SemaphoreType.DMA((3, steps)), pltpu.VMEM((subs, n, n), f32),
                pltpu.VMEM((subs, n, n), f32), pltpu.VMEM((subs, n, n), bf16), pltpu.VMEM((subs, 8, n), f32)]
    return call(functools.partial(maps_kernel, subs, axes), "step_maps", outs, args, [hbm()] * len(args), scratch,
                limit=26, flops=10 ** 10)


def step_noises(axes, subs, init_var, decay, e, dcol, obs_map, gain, noise_factor, obs_var, shift, maps):
    T, n = decay.shape
    m = obs_map.shape[1]
    steps = T // subs
    args = [init_var.reshape(1, n), decay, e, dcol, obs_map.reshape(subs, steps, m, n),
            gain.reshape(subs, steps, m, n), noise_factor, obs_var.reshape(1, m), shift, maps]
    return call(functools.partial(noises_kernel, subs, axes), "step_noises",
                [shape(T, n), shape(subs, n + 16, n), shape(n // 2 + 8, n)], args,
                scratch=[pltpu.VMEM((subs, n, n), f32), pltpu.VMEM((2, subs, n, n), bf16)])


def turn(sub, g, delta, token):
    _, steps, n, _ = g.shape
    return call(functools.partial(turn_kernel, sub), "turn",
                [shape(steps, n, n, dtype=bf16), shape(steps, n, n, dtype=bf16), shape(steps, n)],
                [g, delta, token], [vmem()] * 2 + [anywhere()], flops=4 * 10 ** 9)


def finish(axes, bit, turned, var, mean, placed, r):
    parts = len(turned)
    T, n = var.shape
    high, low, diag = zip(*turned)
    return call(functools.partial(finish_kernel, axes, bit, parts), "finish", [shape(T, n)] * 2,
                [*high, *low, *diag, var, mean, *placed, r],
                scratch=[pltpu.VMEM((parts, n + 16, n), bf16), pltpu.VMEM((parts, 8, n), f32)])


def per_device(axes, init_mean, init_var, decay, coupling, obs_map, gain, noise_factor, obs_var, observed):
    n = decay.shape[1]
    h = n // 2
    subs = 4
    count = 1
    for _, size in axes:
        count *= size
    names = tuple(name for name, _ in axes)

    def swap(x, bit):
        return lax.ppermute(x, names, [(k, k ^ bit) for k in range(count)])

    bits = []
    bit = PLANE
    while bit < count:
        bits.append(bit)
        bit *= 2

    g, e, dcol, delta, shift, maps, own = step_maps(axes, subs, init_mean, decay, coupling, obs_map, gain, observed)
    far = [swap(own, bit) for bit in (2, 4, 6)]
    other = swap(own, 1)
    diag, noises, packed = step_noises(
        axes, subs, init_var, decay, e, dcol, obs_map, gain, noise_factor, obs_var, shift, maps)
    other_packed = swap(packed, 1)
    (chip,) = call(functools.partial(core_kernel, axes), "core_noises", [shape(h + 8, n)],
                   [own, other, packed, other_packed])
    chips = [chip] + [swap(chip, bit) for bit in (2, 4, 6)]
    *far, _ = lax.optimization_barrier((*far, chip))
    all_maps = [own, other] + [v for r in far for v in (r, swap(r, 1))]
    turned = [turn(0, g, delta, chip)]
    *late, total, half, map_picks = call(
        functools.partial(plane_maps_kernel, axes), "plane_maps",
        [shape(3, n, n), shape(3, n, n, dtype=bf16), shape(3, n, 128), shape(8, n), shape(n, n), shape(h, n), shape(3, n, n)],
        all_maps, [anywhere()] * PLANE,
        [pltpu.VMEM((PLANE, n, n), f32), pltpu.VMEM((4, n, n), f32), pltpu.SemaphoreType.DMA((PLANE,))])
    turned.append(turn(1, g, delta, total))
    packed, noise_picks = call(
        functools.partial(plane_noises_kernel, axes), "plane_noises",
        [shape(h + 8, n), shape(3, n + 16, n)],
        [*chips, *late, other_packed, turned[0][2], turned[1][2]],
        [anywhere()] * 4 + [vmem()] * 5 + [anywhere()] * 2,
        [pltpu.VMEM((4, h + 8, n), f32), pltpu.SemaphoreType.DMA((4,))])
    (inner,) = call(functools.partial(inner_kernel, axes), "inner", [shape(2 * n + 16, n)], [map_picks, noise_picks])
    received = []
    for k, bit in enumerate(bits[:-1]):
        moving = swap(packed, bit)
        r, packed = lax.optimization_barrier((swap(half, bit), packed))
        got = (r, swap(r, 1), moving)
        received += got
        more = k < len(bits) - 2
        if k == 0:
            turned.append(turn(2, g, delta, packed))
        args = [total, packed, *got, inner, turned[2][2]]
        new = call(functools.partial(level_kernel, axes, bit), "level",
                   [shape(h + 8, n)] + ([shape(n, n), shape(h, n)] if more else []), args,
                   [vmem()] * 5 + [anywhere()] * 2)
        if k == 0:
            turned.append(turn(3, g, delta, new[0]))
        packed = new[0]
        if more:
            total, half = new[1:]
    placed = call(functools.partial(place_kernel, axes, bits[:-1]), "place",
                  [shape(subs, 2 * n + 16, n), shape(subs, n, n, dtype=bf16), shape(subs, n, 128), shape(subs, 8, n)],
                    [maps, noises, inner, *received], flops=10 ** 5)
    r = swap(packed, bits[-1])
    return tuple(finish(axes, bits[-1], turned, diag, shift, placed, r))


def solution(mesh):
    axes = tuple((name, mesh.shape[name]) for name in mesh.axis_names)
    time = P(tuple(mesh.axis_names))
    return jax.shard_map(
        functools.partial(per_device, axes),
        mesh=mesh,
        in_specs=(P(), P(), time, time, time, time, P(), P(), time),
        out_specs=(time, time),
        check_vma=False,
    )
```

```python
import functools

import jax
import jax.numpy as jnp
from jax import lax
from jax.experimental import pallas as pl
from jax.experimental.pallas import tpu as pltpu
from jax.sharding import PartitionSpec as P

f32, bf16 = jnp.float32, jnp.bfloat16
PLANE = 8


def nn(a, b):
    return jnp.dot(a, b, preferred_element_type=f32)


def nt(a, b):
    return lax.dot_general(a, b, (((1,), (1,)), ((), ())), preferred_element_type=f32)


def halves(x):
    high = x.astype(bf16)
    return high, (x - high.astype(f32)).astype(bf16)


def times(late, early):
    (lh, ll), (eh, el) = late, early
    return nn(lh, eh) + (nn(ll, eh) + nn(lh, el))


def advance(late, noise, shift):
    n = noise.shape[1]
    lh, ll = late
    xh, xl = halves(jnp.concatenate([times(late, halves(noise)), shift], axis=0))
    out = nt(xh, lh) + (nt(xl, lh) + nt(xh, ll))
    return out[:n], out[n:]


def wide(col):
    return jnp.concatenate([col, col], axis=1)


def apart(late):
    row = diag_row(late)
    return row, spread(row), jnp.where(eye_mask(late.shape[0]), 0.0, late).astype(bf16)


def conjugate(late, noise):
    row, col, rest = late
    x = wide(col) * noise + nn(rest, noise.astype(bf16))
    return x * row + nt(x.astype(bf16), rest)


def through(late, shift):
    return row_of(jnp.sum(late * shift, axis=1, keepdims=True))


def joined(early, late):
    parts = halves(late[0])
    noise, shift = advance(parts, early[1], early[2])
    return times(parts, halves(early[0])), noise + late[1], shift + late[2]


def eye_mask(n):
    return lax.broadcasted_iota(jnp.int32, (n, n), 0) == lax.broadcasted_iota(jnp.int32, (n, n), 1)


def column(row):
    n = row.shape[1]
    out = []
    for k in range(0, n, 128):
        m = min(128, n - k)
        out.append(jnp.sum(jnp.where(eye_mask(m), row[:, k:k + m], 0.0), axis=1, keepdims=True))
    return out[0] if len(out) == 1 else jnp.concatenate(out, axis=0)


def spread(row):
    n = row.shape[1]
    return jnp.concatenate([jnp.broadcast_to(row[:, k:k + 128], (128, 128)).T for k in range(0, n, 128)], axis=0)


def row_of(col):
    n = col.shape[0]
    out = [jnp.sum(jnp.where(eye_mask(128), col[k:k + 128], 0.0), axis=0, keepdims=True) for k in range(0, n, 128)]
    return jnp.concatenate(out, axis=1)


def diag_row(x):
    n = x.shape[1]
    out = [jnp.sum(jnp.where(eye_mask(128), x[k:k + 128, k:k + 128], 0.0), axis=0, keepdims=True)
           for k in range(0, n, 128)]
    return jnp.concatenate(out, axis=1)


def rows16(row):
    return jnp.broadcast_to(row, (16, row.shape[1]))


def pack(noise, shift):
    n = noise.shape[1]
    h = n // 2
    lower = lax.broadcasted_iota(jnp.int32, (h, h), 0) >= lax.broadcasted_iota(jnp.int32, (h, h), 1)
    a, b, c = noise[:h, :h], noise[:h, h:], noise[h:, h:]
    body = jnp.concatenate([jnp.where(lower, a, c), b], axis=1)
    extra = jnp.concatenate([jnp.zeros((1, h), f32), diag_row(noise)[:, h:]], axis=1)
    return jnp.concatenate([body, shift[0:1], extra, jnp.zeros((14, n), f32)], axis=0)


def unpack(x):
    n = x.shape[1]
    h = n // 2
    i = lax.broadcasted_iota(jnp.int32, (h, h), 0)
    j = lax.broadcasted_iota(jnp.int32, (h, h), 1)
    body, b = x[:h, :h], x[:h, h:]
    turned = body.T
    a = jnp.where(i >= j, body, turned)
    c = jnp.where(i == j, x[h + 1:h + 2, h:], jnp.where(i < j, body, turned))
    noise = jnp.concatenate([jnp.concatenate([a, b], axis=1), jnp.concatenate([b.T, c], axis=1)], axis=0)
    return noise, x[h:h + 1]


def rank_of(axes):
    rank = 0
    for name, size in axes:
        rank = rank * size + lax.axis_index(name)
    return rank


def bit_of(rank, bit):
    return (rank // bit) % 2


def put_half(ref, total_ref, upper):
    rows = ref.shape[0]
    ref[...] = jnp.where(upper, total_ref[rows:], total_ref[:rows])


def put_out(ref, total_ref, upper):
    if ref.shape[0] == total_ref.shape[0]:
        ref[...] = total_ref[...]
    else:
        put_half(ref, total_ref, upper)


def whole(upper, mine_ref, others_ref):
    mine, others = mine_ref[...], others_ref[...]
    return jnp.concatenate([jnp.where(upper, others, mine), jnp.where(upper, mine, others)], axis=0)


def identity(n):
    return jnp.where(eye_mask(n), 1.0, 0.0), jnp.zeros((n, n), f32), jnp.zeros((16, n), f32)


def maps_kernel(subs, decay_hbm, coup_hbm, omap_hbm, gain_hbm, seen_hbm,
                g_ref, e_ref, dcol_ref, delta_ref, shift_ref, maps_ref, total_ref,
                decay_ref, coup_ref, omap_ref, gain_ref, seen_ref, small_sem, sem, g_s, part_s, eh_s, row_s):
    n = decay_ref.shape[1]
    steps = coup_ref.shape[1]
    small = [pltpu.make_async_copy(x, y, small_sem.at[k]) for k, (x, y) in enumerate(
        [(decay_hbm, decay_ref), (seen_hbm, seen_ref)])]

    def chunk(j):
        return [pltpu.make_async_copy(x.at[:, j], y.at[:, j], sem.at[k, j]) for k, (x, y) in enumerate(
            [(coup_hbm, coup_ref), (omap_hbm, omap_ref), (gain_hbm, gain_ref)])]

    for c in small + chunk(0):
        c.start()
    for j in range(1, steps):
        for c in chunk(j):
            c.start()
    for c in small:
        c.wait()

    def step(j, first):
        for c in chunk(j):
            c.wait()
        all_subs = range(subs)
        rows = [decay_ref[pl.ds(s * steps + j, 1), :] for s in all_subs]
        obs_f = [(omap_ref[s, j].astype(f32) * rows[s] + nn(omap_ref[s, j], coup_ref[s, j])).astype(bf16)
                 for s in all_subs]

        def build(s):
            t = s * steps + j
            gain = gain_ref[s, j]
            e = coup_ref[s, j].astype(f32) - nn(gain.T, obs_f[s])
            e_h = e.astype(bf16)
            e_ref[s, j] = e_h
            eh_s[s] = e_h
            col = spread(rows[s])
            dcol_ref[s, j] = col
            shift = jnp.sum(gain.astype(f32) * column(seen_ref[pl.ds(t, 1), :]), axis=0, keepdims=True)
            if first:
                g_s[s] = e
                g_ref[s, j] = e
                delta, b_new = rows[s], shift
            else:
                delta = row_s[s, 0:1, :]
                b = row_s[s, 1:2, :]
                part_s[s] = wide(col) * g_s[s] + e * delta
                delta = delta * rows[s]
                b_new = rows[s] * b + row_of(jnp.sum(e * b, axis=1, keepdims=True)) + shift
            shift_ref[pl.ds(t, 1), :] = b_new
            delta_ref[pl.ds(t, 1), :] = delta
            row_s[s, 0:1, :] = delta
            row_s[s, 1:2, :] = b_new

        def follow(s):
            if not first:
                g_new = part_s[s] + nn(eh_s[s], g_s[s].astype(bf16))
                g_s[s] = g_new
                g_ref[s, j] = g_new

        build(0)
        build(1)
        follow(0)
        build(2)
        follow(1)
        build(3)
        follow(2)
        follow(3)

    step(0, True)
    lax.fori_loop(1, steps, lambda j, c: (step(j, False), c)[1], 0)

    eye = eye_mask(n)
    maps = [g_ref[s, steps - 1] + jnp.where(eye, delta_ref[(s + 1) * steps - 1:(s + 1) * steps, :], 0.0)
            for s in range(subs)]
    for s in range(subs):
        maps_ref[s] = maps[s]
    parts = [halves(m) for m in maps]
    low, high = times(parts[1], parts[0]), times(parts[3], parts[2])
    maps_ref[subs] = low
    maps_ref[subs + 1] = high
    total_ref[...] = times(halves(high), halves(low))


def shapes_kernel(omap_ref, gain_ref, nf_ref, _, shaped_ref, seen_s):
    subs, steps, m = omap_ref.shape[:3]
    nf = nf_ref[...]

    def see(j, carry):
        seen_s[j] = nn(jnp.concatenate([omap_ref[s, j] for s in range(subs)], axis=0), nf).astype(bf16)
        return carry

    def shape_step(j, carry):
        shaped = [(nf.astype(f32) - nn(gain_ref[s, j].T, seen_s[j, s * m:(s + 1) * m])).astype(bf16) for s in range(subs)]
        for s in range(subs):
            shaped_ref[s, j] = shaped[s]
        return carry

    lax.fori_loop(0, steps, see, 0, unroll=4)
    lax.fori_loop(0, steps, shape_step, 0, unroll=4)


def noises_kernel(subs, decay_ref, e_ref, dcol_ref, shaped_ref, gain_ref, var_ref, shift_ref,
                  maps_ref, _, diag_ref, noises_ref, total_ref, q_s):
    n = e_ref.shape[-1]
    steps = e_ref.shape[1]
    var_col = column(var_ref[...])
    all_subs = range(subs)

    def noise(s, j):
        shaped, gain = shaped_ref[s, j], gain_ref[s, j]
        return nt(shaped, shaped) + nn(gain.T, (gain.astype(f32) * var_col).astype(bf16))

    def first_half(s, j, q):
        return wide(dcol_ref[s, j]) * q + nn(e_ref[s, j], q.astype(bf16))

    def second_half(s, j, x):
        return x * decay_ref[pl.ds(s * steps + j, 1), :] + (nt(x.astype(bf16), e_ref[s, j]) + noise(s, j))

    def step(j, carry):
        x = [first_half(s, j, q_s[s]) for s in all_subs]
        for s in all_subs:
            q_new = second_half(s, j, x[s])
            q_s[s] = q_new
            diag_ref[pl.ds(s * steps + j, 1), :] = diag_row(q_new)
        return carry

    for s in all_subs:
        q_s[s] = noise(s, 0)

    for s in all_subs:
        diag_ref[pl.ds(s * steps, 1), :] = diag_row(q_s[s])
    lax.fori_loop(1, steps, step, 0)

    shift = [shift_ref[(s + 1) * steps - 1:(s + 1) * steps, :] for s in range(subs)]
    pairs = [(conjugate(apart(maps_ref[s + 1]), q_s[s]) + q_s[s + 1], through(maps_ref[s + 1], shift[s]) + shift[s + 1])
             for s in (0, 2)]
    last = maps_ref[subs + 1]
    total_ref[...] = pack(conjugate(apart(last), pairs[0][0]) + pairs[1][0], through(last, pairs[0][1]) + pairs[1][1])
    for s in range(subs):
        noises_ref[s, 0:n, :] = q_s[s]
        noises_ref[s, n:, :] = rows16(shift[s])


def chip_kernel(axes, own_ref, other_ref, _, out_ref):
    upper = rank_of(axes) % 2 == 1
    own, other = own_ref[...], other_ref[...]
    out_ref[...] = times(halves(jnp.where(upper, own, other)), halves(jnp.where(upper, other, own)))


def core_kernel(axes, own_map_ref, other_map_ref, own_ref, other_ref, out_ref, half_ref):
    upper = rank_of(axes) % 2 == 1
    own, other = unpack(own_ref[...]), unpack(other_ref[...])
    late = jnp.where(upper, own_map_ref[...], other_map_ref[...])
    early_noise, early_shift = (jnp.where(upper, a, b) for a, b in zip(other, own))
    late_noise, late_shift = (jnp.where(upper, a, b) for a, b in zip(own, other))
    out_ref[...] = pack(conjugate(apart(late), early_noise) + late_noise, through(late, early_shift) + late_shift)
    put_half(half_ref, out_ref, upper)


def fetch(rank, refs, dst, sem):
    place = (rank % PLANE) // (PLANE // len(refs))
    copies = [pltpu.make_async_copy(r, dst.at[place ^ k], sem.at[k]) for k, r in enumerate(refs)]
    for c in copies:
        c.start()
    for c in copies:
        c.wait()


def plane_maps_kernel(axes, *refs):
    ins, refs = refs[:4], refs[4:]
    core_ref, var_ref, mean_ref, late_ref, rest_ref, col_ref, row_ref, start_ref, total_ref, half_ref, picks_ref, chip_s, sem = refs
    rank = rank_of(axes)
    fetch(rank, ins, chip_s, sem)

    def keep(k, late):
        late_ref[k] = late
        row_ref[k:k + 1, :], col_ref[k], rest_ref[k] = apart(late)

    chips = [chip_s[k] for k in range(4)]
    pairs = [times(halves(chips[2 * k + 1]), halves(chips[2 * k])) for k in range(2)]
    total = times(halves(pairs[1]), halves(pairs[0]))
    first = rank // PLANE == 0
    n = total.shape[0]
    noise = conjugate(apart(total), jnp.where(eye_mask(n), var_ref[...], 0.0))
    start_ref[0:n, :] = jnp.where(first, noise, 0.0)
    start_ref[n:, :] = rows16(jnp.where(first, through(total, mean_ref[...]), 0.0))
    total_ref[...] = jnp.where(first, 0.0, total)
    for k, late in enumerate((chips[1], chips[3], pairs[1])):
        keep(k, late)
    h = half_ref.shape[0]
    half_ref[...] = jnp.where(rank % 2 == 1, total_ref[h:], total_ref[:h])
    picks_ref[0] = pairs[0]
    picks_ref[1] = chip_s[2 * bit_of(rank, 4)]
    picks_ref[2] = core_ref[...]


def plane_noises_kernel(axes, *refs):
    ins, (late_ref, rest_ref, col_ref, row_ref, start_ref, core_ref, out_ref, picks_ref, in_s, total_s, sem) = refs[:7], refs[7:]
    rank = rank_of(axes)
    place = (rank % PLANE) // 2
    rows = total_s.shape[0] // 2
    copies = [pltpu.make_async_copy(ins[0], in_s.at[place], sem.at[0])]
    for k in range(1, 4):
        for other in range(2):
            part = (rank % 2) ^ other
            copies.append(pltpu.make_async_copy(
                ins[2 * k - 1 + other], in_s.at[place ^ k, pl.ds(pl.multiple_of(part * rows, 8), rows)],
                sem.at[2 * k - 1 + other]))
    for c in copies:
        c.start()
    for c in copies:
        c.wait()
    n = late_ref.shape[-1]

    def join(k, early, late):
        noise = conjugate((row_ref[k:k + 1, :], col_ref[k], rest_ref[k]), early[0])
        return noise + late[0], through(late_ref[k], early[1]) + late[1]

    def pick(k, element):
        picks_ref[k, 0:n], picks_ref[k, n:] = element[0], rows16(element[1])

    chips = [unpack(in_s[k]) for k in range(4)]
    pairs = [join(k, chips[2 * k], chips[2 * k + 1]) for k in range(2)]
    noise, shift = join(2, pairs[0], pairs[1])
    total_s[...] = pack(noise + start_ref[0:n, :], shift + start_ref[n:n + 1, :])
    put_out(out_ref, total_s, rank % 2 == 1)
    pick(0, pairs[0])
    pick(1, unpack(in_s[2 * bit_of(rank, 4)]))
    pick(2, unpack(core_ref[...]))


def level_kernel(axes, bit, own_map_ref, own_ref, r_ref, x_ref, other_ref, _, __, *outs):
    *outs, total_s = outs
    rank = rank_of(axes)
    upper, high = rank % 2 == 1, bit_of(rank, bit) == 1
    other_map, own_map = whole(upper, r_ref, x_ref), own_map_ref[...]
    other, own = unpack(other_ref[...]), unpack(own_ref[...])
    late = jnp.where(high, own_map, other_map)
    early_noise, early_shift = (jnp.where(high, a, b) for a, b in zip(other, own))
    late_noise, late_shift = (jnp.where(high, a, b) for a, b in zip(own, other))
    total_s[...] = pack(conjugate(apart(late), early_noise) + late_noise, through(late, early_shift) + late_shift)
    put_out(outs[0], total_s, upper)
    if len(outs) > 1:
        outs[1][...] = times(halves(late), halves(jnp.where(high, other_map, own_map)))
        put_half(outs[2], outs[1], upper)


def place_kernel(axes, subs_ref, sub_noises_ref, maps_ref, noises_ref, out_ref, rest_ref, col_ref, row_ref):
    rank = rank_of(axes)
    n = out_ref.shape[2]
    one = identity(n)
    parts = []
    for k, bit in enumerate((4, 2, 1)):
        element = (maps_ref[k], noises_ref[k, 0:n], noises_ref[k, n:])
        parts.append(tuple(jnp.where(bit_of(rank, bit) == 1, a, b) for a, b in zip(element, one)))

    def put(s, element):
        em, en, es = element
        out_ref[s, 0:n, :], out_ref[s, n:2 * n, :], out_ref[s, 2 * n:, :] = em, en, es

    def sub(s, carry):
        before = out_ref[s, 0:n, :], out_ref[s, n:2 * n, :], out_ref[s, 2 * n:, :]
        put(s + 1, joined(before, (subs_ref[s], sub_noises_ref[s, 0:n, :], sub_noises_ref[s, n:, :])))
        return carry

    def split(s, carry):
        row_ref[s, 0:1, :], col_ref[s], rest_ref[s] = apart(out_ref[s, 0:n, :])
        return carry

    put(0, joined(parts[0], joined(parts[1], parts[2])))
    lax.fori_loop(0, out_ref.shape[0] - 1, sub, 0)
    lax.fori_loop(0, out_ref.shape[0], split, 0)


def before_kernel(axes, bits, var_ref, mean_ref, *refs):
    map_ref, noise_ref, shift_ref, rest_ref, col_ref, row_ref = refs[-6:]
    rank = rank_of(axes)
    before = identity(map_ref.shape[0])
    for k, bit in enumerate(bits):
        r_ref, x_ref, other_ref = refs[3 * k:3 * k + 3]
        noise, shift = unpack(other_ref[...])
        other = whole(rank % 2 == 1, r_ref, x_ref), noise, rows16(shift)
        new = other if k == 0 else joined(other, before)
        before = tuple(jnp.where(bit_of(rank, bit) == 1, a, b) for a, b in zip(new, before))
    n = map_ref.shape[0]
    start = jnp.zeros((n, n), f32), jnp.where(eye_mask(n), var_ref[...], 0.0), rows16(mean_ref[...])
    before = tuple(jnp.where(rank // PLANE == 0, a, b) for a, b in zip(start, before))
    map_ref[...], noise_ref[...], shift_ref[...] = before
    row_ref[0:1, :], col_ref[...], rest_ref[...] = apart(before[0])


def turn_kernel(sub, g_ref, delta_ref, token_ref, high_ref, low_ref, diag_ref):
    steps, n = high_ref.shape[:2]
    eye = eye_mask(n)

    def step(j, carry):
        turned = g_ref[sub, j].T
        diag_ref[pl.ds(j, 1), :] = delta_ref[pl.ds(sub * steps + j, 1), :] + diag_row(turned)
        high_ref[j], low_ref[j] = halves(jnp.where(eye, 0.0, turned))
        return carry

    lax.fori_loop(0, steps, step, 0, unroll=2)


def finish_kernel(axes, bit, parts, *refs):
    high, low, diag = refs[:parts], refs[parts:2 * parts], refs[2 * parts:3 * parts]
    var_ref, mean_ref, place_ref, rest_ref, col_ref, arow_ref, bmap_ref, bnoise_ref, bshift_ref, brest_ref, bcol_ref, brow_ref, r_ref, x_ref, means_ref, vars_ref, left_s, row_s = refs[3 * parts:]
    n = left_s.shape[-1]
    steps = high[0].shape[0]
    rank = rank_of(axes)
    is_high = bit_of(rank, bit) == 1
    received, moved = unpack(whole(rank % 2 == 1, r_ref, x_ref))
    noise = conjugate((brow_ref[0:1, :], bcol_ref[...], brest_ref[...]), received)
    state = jnp.where(is_high, noise, 0.0) + bnoise_ref[...]
    moved = jnp.where(is_high, through(bmap_ref[...], moved), 0.0) + bshift_ref[0:1, :]
    for s in range(parts):
        p = conjugate((arow_ref[s, 0:1, :], col_ref[s], rest_ref[s]), state) + place_ref[s, n:2 * n, :]
        mean = through(place_ref[s, 0:n, :], moved) + place_ref[s, 2 * n:2 * n + 1, :]
        mh, ml = halves(mean)
        left_s[s, 0:n, :] = p.astype(bf16)
        left_s[s, n:, :] = jnp.concatenate([mh, ml, jnp.zeros((14, n), bf16)], axis=0)
        row_s[s, 0:1, :] = mean
        row_s[s, 1:2, :] = diag_row(p)

    def step(j, carry):
        both = [nn(left_s[s], high[s][j]) for s in range(parts)]
        rest = [nn(left_s[s, n:, :], low[s][j]) for s in range(parts)]
        for s in range(parts):
            t = s * steps + j
            d = diag[s][pl.ds(j, 1), :]
            vars_ref[pl.ds(t, 1), :] = (var_ref[pl.ds(t, 1), :] + d * (d * row_s[s, 1:2, :] + 2.0 * diag_row(both[s]))
                                        + jnp.sum(high[s][j].astype(f32) * both[s][:n], axis=0, keepdims=True))
            means_ref[pl.ds(t, 1), :] = (mean_ref[pl.ds(t, 1), :] + d * row_s[s, 0:1, :]
                                         + both[s][n:n + 1] + (both[s][n + 1:n + 2] + rest[s][0:1]))
        return carry

    lax.fori_loop(0, steps, step, 0)


def vmem():
    return pl.BlockSpec(memory_space=pltpu.VMEM)


def anywhere():
    return pl.BlockSpec(memory_space=pl.ANY)


def shape(*dims, dtype=f32):
    return jax.ShapeDtypeStruct(dims, dtype)


def call(kernel, name, outs, args, specs=None, scratch=(), limit=16, flops=10 ** 5):
    return pl.pallas_call(
        kernel,
        in_specs=specs or [vmem()] * len(args),
        out_specs=[vmem()] * len(outs),
        out_shape=outs,
        scratch_shapes=scratch,
        compiler_params=pltpu.CompilerParams(vmem_limit_bytes=limit * 1024 * 1024),
        cost_estimate=pl.CostEstimate(flops=flops, bytes_accessed=0, transcendentals=0),
        name=name,
    )(*args)


def hbm():
    return pl.BlockSpec(memory_space=pltpu.HBM)


def step_maps(subs, decay, coupling, obs_map, gain, observed):
    T, n = decay.shape
    m = obs_map.shape[1]
    steps = T // subs
    outs = [shape(subs, steps, n, n), shape(subs, steps, n, n, dtype=bf16), shape(subs, steps, n, 128),
            shape(T, n), shape(T, n), shape(subs + 2, n, n), shape(n, n)]
    args = [decay, coupling.reshape(subs, steps, n, n), obs_map.reshape(subs, steps, m, n),
            gain.reshape(subs, steps, m, n), observed]
    scratch = [pltpu.VMEM(x.shape, x.dtype) for x in args]
    args = [pltpu.with_memory_space_constraint(x, pltpu.HBM) for x in args]
    scratch += [pltpu.SemaphoreType.DMA((2,)), pltpu.SemaphoreType.DMA((3, steps)), pltpu.VMEM((subs, n, n), f32),
                pltpu.VMEM((subs, n, n), f32), pltpu.VMEM((subs, n, n), bf16), pltpu.VMEM((subs, 8, n), f32)]
    return call(functools.partial(maps_kernel, subs), "step_maps", outs, args, [hbm()] * len(args), scratch,
                limit=26, flops=10 ** 10)


def step_shapes(subs, obs_map, gain, noise_factor, token):
    T, m, n = obs_map.shape
    steps = T // subs
    return call(shapes_kernel, "step_shapes", [shape(subs, steps, n, n, dtype=bf16)],
                [obs_map.reshape(subs, steps, m, n), gain.reshape(subs, steps, m, n), noise_factor, token],
                [vmem()] * 3 + [anywhere()], [pltpu.VMEM((steps, subs * m, n), bf16)])[0]


def step_noises(subs, decay, e, dcol, shaped, gain, obs_var, shift, maps, token):
    T, n = decay.shape
    m = gain.shape[1]
    args = [decay, e, dcol, shaped, gain.reshape(subs, T // subs, m, n), obs_var.reshape(1, m),
            shift, maps, token]
    return call(functools.partial(noises_kernel, subs), "step_noises",
                [shape(T, n), shape(subs, n + 16, n), shape(n // 2 + 16, n)], args, [vmem()] * 8 + [anywhere()],
                [pltpu.VMEM((subs, n, n), f32)])


def turn(sub, g, delta, token):
    _, steps, n, _ = g.shape
    return call(functools.partial(turn_kernel, sub), "turn",
                [shape(steps, n, n, dtype=bf16), shape(steps, n, n, dtype=bf16), shape(steps, n)],
                [g, delta, token], [vmem()] * 2 + [anywhere()], flops=10 ** 5)


def finish(axes, bit, turned, var, mean, placed, before, r, x):
    parts = len(turned)
    T, n = var.shape
    high, low, diag = zip(*turned)
    return call(functools.partial(finish_kernel, axes, bit, parts), "finish", [shape(T, n)] * 2,
                [*high, *low, *diag, var, mean, *placed, *before, r, x],
                scratch=[pltpu.VMEM((parts, n + 16, n), bf16), pltpu.VMEM((parts, 8, n), f32)])


def per_device(axes, init_mean, init_var, decay, coupling, obs_map, gain, noise_factor, obs_var, observed):
    n = decay.shape[1]
    h = n // 2
    subs = 4
    count = 1
    for _, size in axes:
        count *= size
    names = tuple(name for name, _ in axes)

    def swap(x, bit):
        return lax.ppermute(x, names, [(k, k ^ bit) for k in range(count)])

    bits = []
    bit = PLANE
    while bit < count:
        bits.append(bit)
        bit *= 2

    g, e, dcol, delta, shift, maps, own = step_maps(subs, decay, coupling, obs_map, gain, observed)
    other = swap(own, 1)
    shaped = step_shapes(subs, obs_map, gain, noise_factor, delta)
    (chip_map,) = call(functools.partial(chip_kernel, axes), "chip_maps", [shape(n, n)], [own, other, shaped],
                       [vmem()] * 2 + [anywhere()])
    far = [swap(chip_map, bit) for bit in (2, 4, 6)]
    diag, noises, packed = step_noises(subs, decay, e, dcol, shaped, gain, obs_var, shift, maps, chip_map)
    other_packed = swap(packed, 1)
    chip, chip_half = call(functools.partial(core_kernel, axes), "core_noises", [shape(h + 16, n), shape(h // 2 + 8, n)],
                   [own, other, packed, other_packed])
    chips = [chip] + [v for r in [swap(chip_half, bit) for bit in (2, 4, 6)] for v in (r, swap(r, 1))]
    *far, _ = lax.optimization_barrier((*far, chip))
    *late, total, half, map_picks = call(
        functools.partial(plane_maps_kernel, axes), "plane_maps",
        [shape(3, n, n), shape(3, n, n, dtype=bf16), shape(3, n, 128), shape(8, n), shape(n + 16, n), shape(n, n), shape(h, n), shape(3, n, n)],
        [chip_map, *far, other, init_var.reshape(1, n), init_mean.reshape(1, n)], [anywhere()] * 4 + [vmem()] * 3,
        [pltpu.VMEM((4, n, n), f32), pltpu.SemaphoreType.DMA((4,))])
    size = h + 16 if len(bits) > 1 else h // 2 + 8
    packed, noise_picks = call(
        functools.partial(plane_noises_kernel, axes), "plane_noises",
        [shape(size, n), shape(3, n + 16, n)],
        [*chips, *late, other_packed], [anywhere()] * 7 + [vmem()] * 6,
        [pltpu.VMEM((4, h + 16, n), f32), pltpu.VMEM((h + 16, n), f32), pltpu.SemaphoreType.DMA((7,))])
    placed = call(functools.partial(place_kernel, axes), "place",
                  [shape(subs, 2 * n + 16, n), shape(subs, n, n, dtype=bf16), shape(subs, n, 128), shape(subs, 8, n)],
                  [maps, noises, map_picks, noise_picks])
    turned = [turn(0, g, delta, packed)]
    received = []
    for k, bit in enumerate(bits[:-1]):
        moving = swap(packed, bit)
        r, packed = lax.optimization_barrier((swap(half, bit), packed))
        got = (r, swap(r, 1), moving)
        received += got
        more = k < len(bits) - 2
        size = h + 16 if more else h // 2 + 8
        new = call(functools.partial(level_kernel, axes, bit), "level",
                   [shape(size, n)] + ([shape(n, n), shape(h, n)] if more else []), [total, packed, *got, placed[3], turned[0][2]],
                   [vmem()] * 5 + [anywhere()] * 2, [pltpu.VMEM((h + 16, n), f32)])
        packed = new[0]
        if more:
            total, half = new[1:]
    before = call(functools.partial(before_kernel, axes, bits[:-1]), "before",
                  [shape(n, n), shape(n, n), shape(16, n), shape(n, n, dtype=bf16), shape(n, 128), shape(8, n)],
                  [init_var.reshape(1, n), init_mean.reshape(1, n), *received])
    turned += [turn(k, g, delta, packed) for k in range(1, subs)]
    r, *_ = lax.optimization_barrier((swap(packed, bits[-1]), *before, turned[1][2], turned[2][2]))
    return tuple(finish(axes, bits[-1], turned, diag, shift, placed, before, r, swap(r, 1)))


def solution(mesh):
    axes = tuple((name, mesh.shape[name]) for name in mesh.axis_names)
    time = P(tuple(mesh.axis_names))
    return jax.shard_map(
        functools.partial(per_device, axes),
        mesh=mesh,
        in_specs=(P(), P(), time, time, time, time, P(), P(), time),
        out_specs=(time, time),
        check_vma=False,
    )
```

```python
import functools

import jax
import jax.numpy as jnp
from jax import lax
from jax.experimental import pallas as pl
from jax.experimental.pallas import tpu as pltpu
from jax.sharding import PartitionSpec as P

f32, bf16 = jnp.float32, jnp.bfloat16
PLANE = 8


def nn(a, b):
    return jnp.dot(a, b, preferred_element_type=f32)


def nt(a, b):
    return lax.dot_general(a, b, (((1,), (1,)), ((), ())), preferred_element_type=f32)


def halves(x):
    high = x.astype(bf16)
    return high, (x - high.astype(f32)).astype(bf16)


def times(late, early):
    (lh, ll), (eh, el) = late, early
    return nn(lh, eh) + (nn(ll, eh) + nn(lh, el))


def advance(late, noise, shift):
    n = noise.shape[1]
    lh, ll = late
    xh, xl = halves(jnp.concatenate([times(late, halves(noise)), shift], axis=0))
    out = nt(xh, lh) + (nt(xl, lh) + nt(xh, ll))
    return out[:n], out[n:]


def wide(col):
    return jnp.concatenate([col, col], axis=1)


def apart(late):
    row = diag_row(late)
    return row, spread(row), jnp.where(eye_mask(late.shape[0]), 0.0, late).astype(bf16)


def conjugate(late, noise):
    row, col, rest = late
    x = wide(col) * noise + nn(rest, noise.astype(bf16))
    return x * row + nt(x.astype(bf16), rest)


def through(late, shift):
    return row_of(jnp.sum(late * shift, axis=1, keepdims=True))


def joined(early, late):
    parts = halves(late[0])
    noise, shift = advance(parts, early[1], early[2])
    return times(parts, halves(early[0])), noise + late[1], shift + late[2]


def eye_mask(n):
    return lax.broadcasted_iota(jnp.int32, (n, n), 0) == lax.broadcasted_iota(jnp.int32, (n, n), 1)


def column(row):
    n = row.shape[1]
    out = []
    for k in range(0, n, 128):
        m = min(128, n - k)
        out.append(jnp.sum(jnp.where(eye_mask(m), row[:, k:k + m], 0.0), axis=1, keepdims=True))
    return out[0] if len(out) == 1 else jnp.concatenate(out, axis=0)


def spread(row):
    n = row.shape[1]
    return jnp.concatenate([jnp.broadcast_to(row[:, k:k + 128], (128, 128)).T for k in range(0, n, 128)], axis=0)


def row_of(col):
    n = col.shape[0]
    out = [jnp.sum(jnp.where(eye_mask(128), col[k:k + 128], 0.0), axis=0, keepdims=True) for k in range(0, n, 128)]
    return jnp.concatenate(out, axis=1)


def diag_row(x):
    n = x.shape[1]
    out = [jnp.sum(jnp.where(eye_mask(128), x[k:k + 128, k:k + 128], 0.0), axis=0, keepdims=True)
           for k in range(0, n, 128)]
    return jnp.concatenate(out, axis=1)


def rows16(row):
    return jnp.broadcast_to(row, (16, row.shape[1]))


def pack(noise, shift):
    n = noise.shape[1]
    h = n // 2
    lower = lax.broadcasted_iota(jnp.int32, (h, h), 0) >= lax.broadcasted_iota(jnp.int32, (h, h), 1)
    a, b, c = noise[:h, :h], noise[:h, h:], noise[h:, h:]
    body = jnp.concatenate([jnp.where(lower, a, c), b], axis=1)
    extra = jnp.concatenate([jnp.zeros((1, h), f32), diag_row(noise)[:, h:]], axis=1)
    return jnp.concatenate([body, shift[0:1], extra, jnp.zeros((14, n), f32)], axis=0)


def unpack(x):
    n = x.shape[1]
    h = n // 2
    i = lax.broadcasted_iota(jnp.int32, (h, h), 0)
    j = lax.broadcasted_iota(jnp.int32, (h, h), 1)
    body, b = x[:h, :h], x[:h, h:]
    turned = body.T
    a = jnp.where(i >= j, body, turned)
    c = jnp.where(i == j, x[h + 1:h + 2, h:], jnp.where(i < j, body, turned))
    noise = jnp.concatenate([jnp.concatenate([a, b], axis=1), jnp.concatenate([b.T, c], axis=1)], axis=0)
    return noise, x[h:h + 1]


def rank_of(axes):
    rank = 0
    for name, size in axes:
        rank = rank * size + lax.axis_index(name)
    return rank


def bit_of(rank, bit):
    return (rank // bit) % 2


def put_half(ref, total_ref, upper):
    rows = ref.shape[0]
    ref[...] = jnp.where(upper, total_ref[rows:], total_ref[:rows])


def put_out(ref, total_ref, upper):
    if ref.shape[0] == total_ref.shape[0]:
        ref[...] = total_ref[...]
    else:
        put_half(ref, total_ref, upper)


def whole(upper, mine_ref, others_ref):
    mine, others = mine_ref[...], others_ref[...]
    return jnp.concatenate([jnp.where(upper, others, mine), jnp.where(upper, mine, others)], axis=0)


def identity(n):
    return jnp.where(eye_mask(n), 1.0, 0.0), jnp.zeros((n, n), f32), jnp.zeros((16, n), f32)


def maps_kernel(subs, decay_hbm, coup_hbm, omap_hbm, gain_hbm, seen_hbm,
                g_ref, e_ref, dcol_ref, delta_ref, shift_ref, maps_ref, total_ref,
                decay_ref, coup_ref, omap_ref, gain_ref, seen_ref, small_sem, sem, g_s, part_s, eh_s, row_s):
    n = decay_ref.shape[1]
    steps = coup_ref.shape[1]
    small = [pltpu.make_async_copy(x, y, small_sem.at[k]) for k, (x, y) in enumerate(
        [(decay_hbm, decay_ref), (seen_hbm, seen_ref)])]

    def chunk(j):
        return [pltpu.make_async_copy(x.at[:, j], y.at[:, j], sem.at[k, j]) for k, (x, y) in enumerate(
            [(coup_hbm, coup_ref), (omap_hbm, omap_ref), (gain_hbm, gain_ref)])]

    for c in small + chunk(0):
        c.start()
    for j in range(1, steps):
        for c in chunk(j):
            c.start()
    for c in small:
        c.wait()

    def step(j, first):
        for c in chunk(j):
            c.wait()
        all_subs = range(subs)
        rows = [decay_ref[pl.ds(s * steps + j, 1), :] for s in all_subs]
        obs_f = [(omap_ref[s, j].astype(f32) * rows[s] + nn(omap_ref[s, j], coup_ref[s, j])).astype(bf16)
                 for s in all_subs]

        def build(s):
            t = s * steps + j
            gain = gain_ref[s, j]
            e = coup_ref[s, j].astype(f32) - nn(gain.T, obs_f[s])
            e_h = e.astype(bf16)
            e_ref[s, j] = e_h
            eh_s[s] = e_h
            col = spread(rows[s])
            dcol_ref[s, j] = col
            shift = jnp.sum(gain.astype(f32) * column(seen_ref[pl.ds(t, 1), :]), axis=0, keepdims=True)
            if first:
                g_s[s] = e
                g_ref[s, j] = e
                delta, b_new = rows[s], shift
            else:
                delta = row_s[s, 0:1, :]
                b = row_s[s, 1:2, :]
                part_s[s] = wide(col) * g_s[s] + e * delta
                delta = delta * rows[s]
                b_new = rows[s] * b + row_of(jnp.sum(e * b, axis=1, keepdims=True)) + shift
            shift_ref[pl.ds(t, 1), :] = b_new
            delta_ref[pl.ds(t, 1), :] = delta
            row_s[s, 0:1, :] = delta
            row_s[s, 1:2, :] = b_new

        def follow(s):
            if not first:
                g_new = part_s[s] + nn(eh_s[s], g_s[s].astype(bf16))
                g_s[s] = g_new
                g_ref[s, j] = g_new

        build(0)
        build(1)
        follow(0)
        build(2)
        follow(1)
        build(3)
        follow(2)
        follow(3)

    step(0, True)
    lax.fori_loop(1, steps, lambda j, c: (step(j, False), c)[1], 0)

    eye = eye_mask(n)
    maps = [g_ref[s, steps - 1] + jnp.where(eye, delta_ref[(s + 1) * steps - 1:(s + 1) * steps, :], 0.0)
            for s in range(subs)]
    for s in range(subs):
        maps_ref[s] = maps[s]
    parts = [halves(m) for m in maps]
    low, high = times(parts[1], parts[0]), times(parts[3], parts[2])
    maps_ref[subs] = low
    maps_ref[subs + 1] = high
    total_ref[...] = times(halves(high), halves(low))


def shapes_kernel(omap_ref, gain_ref, nf_ref, _, shaped_ref, seen_s):
    subs, steps, m = omap_ref.shape[:3]
    nf = nf_ref[...]

    def see(j, carry):
        seen_s[j] = nn(jnp.concatenate([omap_ref[s, j] for s in range(subs)], axis=0), nf).astype(bf16)
        return carry

    def shape_step(j, carry):
        shaped = [(nf.astype(f32) - nn(gain_ref[s, j].T, seen_s[j, s * m:(s + 1) * m])).astype(bf16) for s in range(subs)]
        for s in range(subs):
            shaped_ref[s, j] = shaped[s]
        return carry

    lax.fori_loop(0, steps, see, 0, unroll=4)
    lax.fori_loop(0, steps, shape_step, 0, unroll=4)


def noises_kernel(subs, decay_ref, e_ref, dcol_ref, shaped_ref, gain_ref, var_ref, shift_ref,
                  maps_ref, _, diag_ref, noises_ref, total_ref, q_s):
    n = e_ref.shape[-1]
    steps = e_ref.shape[1]
    var_col = column(var_ref[...])
    all_subs = range(subs)

    def noise(s, j):
        shaped, gain = shaped_ref[s, j], gain_ref[s, j]
        return nt(shaped, shaped) + nn(gain.T, (gain.astype(f32) * var_col).astype(bf16))

    def first_half(s, j, q):
        return wide(dcol_ref[s, j]) * q + nn(e_ref[s, j], q.astype(bf16))

    def second_half(s, j, x):
        return x * decay_ref[pl.ds(s * steps + j, 1), :] + (nt(x.astype(bf16), e_ref[s, j]) + noise(s, j))

    def step(j, carry):
        x = [first_half(s, j, q_s[s]) for s in all_subs]
        for s in all_subs:
            q_new = second_half(s, j, x[s])
            q_s[s] = q_new
            diag_ref[pl.ds(s * steps + j, 1), :] = diag_row(q_new)
        return carry

    for s in all_subs:
        q_s[s] = noise(s, 0)

    for s in all_subs:
        diag_ref[pl.ds(s * steps, 1), :] = diag_row(q_s[s])
    lax.fori_loop(1, steps, step, 0)

    shift = [shift_ref[(s + 1) * steps - 1:(s + 1) * steps, :] for s in range(subs)]
    pairs = [(conjugate(apart(maps_ref[s + 1]), q_s[s]) + q_s[s + 1], through(maps_ref[s + 1], shift[s]) + shift[s + 1])
             for s in (0, 2)]
    last = maps_ref[subs + 1]
    total_ref[...] = pack(conjugate(apart(last), pairs[0][0]) + pairs[1][0], through(last, pairs[0][1]) + pairs[1][1])
    for s in range(subs):
        noises_ref[s, 0:n, :] = q_s[s]
        noises_ref[s, n:, :] = rows16(shift[s])


def chip_kernel(axes, own_ref, other_ref, _, out_ref):
    upper = rank_of(axes) % 2 == 1
    own, other = own_ref[...], other_ref[...]
    out_ref[...] = times(halves(jnp.where(upper, own, other)), halves(jnp.where(upper, other, own)))


def core_kernel(axes, own_map_ref, other_map_ref, own_ref, other_ref, out_ref, half_ref):
    upper = rank_of(axes) % 2 == 1
    own, other = unpack(own_ref[...]), unpack(other_ref[...])
    late = jnp.where(upper, own_map_ref[...], other_map_ref[...])
    early_noise, early_shift = (jnp.where(upper, a, b) for a, b in zip(other, own))
    late_noise, late_shift = (jnp.where(upper, a, b) for a, b in zip(own, other))
    out_ref[...] = pack(conjugate(apart(late), early_noise) + late_noise, through(late, early_shift) + late_shift)
    put_half(half_ref, out_ref, upper)


def fetch(rank, refs, dst, sem):
    place = (rank % PLANE) // (PLANE // len(refs))
    copies = [pltpu.make_async_copy(r, dst.at[place ^ k], sem.at[k]) for k, r in enumerate(refs)]
    for c in copies:
        c.start()
    for c in copies:
        c.wait()


def plane_maps_kernel(axes, *refs):
    ins, refs = refs[:4], refs[4:]
    core_ref, var_ref, mean_ref, late_ref, rest_ref, col_ref, row_ref, start_ref, total_ref, half_ref, picks_ref, chip_s, sem = refs
    rank = rank_of(axes)
    fetch(rank, ins, chip_s, sem)

    def keep(k, late):
        late_ref[k] = late
        row_ref[k:k + 1, :], col_ref[k], rest_ref[k] = apart(late)

    chips = [chip_s[k] for k in range(4)]
    pairs = [times(halves(chips[2 * k + 1]), halves(chips[2 * k])) for k in range(2)]
    total = times(halves(pairs[1]), halves(pairs[0]))
    first = rank // PLANE == 0
    n = total.shape[0]
    noise = conjugate(apart(total), jnp.where(eye_mask(n), var_ref[...], 0.0))
    start_ref[0:n, :] = jnp.where(first, noise, 0.0)
    start_ref[n:, :] = rows16(jnp.where(first, through(total, mean_ref[...]), 0.0))
    total_ref[...] = jnp.where(first, 0.0, total)
    for k, late in enumerate((chips[1], chips[3], pairs[1])):
        keep(k, late)
    h = half_ref.shape[0]
    half_ref[...] = jnp.where(rank % 2 == 1, total_ref[h:], total_ref[:h])
    picks_ref[0] = pairs[0]
    picks_ref[1] = chip_s[2 * bit_of(rank, 4)]
    picks_ref[2] = core_ref[...]


def plane_noises_kernel(axes, *refs):
    ins, (late_ref, rest_ref, col_ref, row_ref, start_ref, core_ref, out_ref, picks_ref, in_s, total_s, sem) = refs[:7], refs[7:]
    rank = rank_of(axes)
    place = (rank % PLANE) // 2
    rows = total_s.shape[0] // 2
    copies = [pltpu.make_async_copy(ins[0], in_s.at[place], sem.at[0])]
    for k in range(1, 4):
        for other in range(2):
            part = (rank % 2) ^ other
            copies.append(pltpu.make_async_copy(
                ins[2 * k - 1 + other], in_s.at[place ^ k, pl.ds(pl.multiple_of(part * rows, 8), rows)],
                sem.at[2 * k - 1 + other]))
    for c in copies:
        c.start()
    for c in copies:
        c.wait()
    n = late_ref.shape[-1]

    def join(k, early, late):
        noise = conjugate((row_ref[k:k + 1, :], col_ref[k], rest_ref[k]), early[0])
        return noise + late[0], through(late_ref[k], early[1]) + late[1]

    def pick(k, element):
        picks_ref[k, 0:n], picks_ref[k, n:] = element[0], rows16(element[1])

    chips = [unpack(in_s[k]) for k in range(4)]
    pairs = [join(k, chips[2 * k], chips[2 * k + 1]) for k in range(2)]
    noise, shift = join(2, pairs[0], pairs[1])
    total_s[...] = pack(noise + start_ref[0:n, :], shift + start_ref[n:n + 1, :])
    put_out(out_ref, total_s, rank % 2 == 1)
    pick(0, pairs[0])
    pick(1, unpack(in_s[2 * bit_of(rank, 4)]))
    pick(2, unpack(core_ref[...]))


def level_kernel(axes, bit, own_map_ref, own_ref, r_ref, x_ref, other_ref, _, *outs):
    *outs, total_s = outs
    rank = rank_of(axes)
    upper, high = rank % 2 == 1, bit_of(rank, bit) == 1
    other_map, own_map = whole(upper, r_ref, x_ref), own_map_ref[...]
    other, own = unpack(other_ref[...]), unpack(own_ref[...])
    late = jnp.where(high, own_map, other_map)
    early_noise, early_shift = (jnp.where(high, a, b) for a, b in zip(other, own))
    late_noise, late_shift = (jnp.where(high, a, b) for a, b in zip(own, other))
    total_s[...] = pack(conjugate(apart(late), early_noise) + late_noise, through(late, early_shift) + late_shift)
    put_out(outs[0], total_s, upper)
    if len(outs) > 1:
        outs[1][...] = times(halves(late), halves(jnp.where(high, other_map, own_map)))
        put_half(outs[2], outs[1], upper)


def place_kernel(axes, subs_ref, sub_noises_ref, maps_ref, noises_ref, out_ref, rest_ref, col_ref, row_ref):
    rank = rank_of(axes)
    n = out_ref.shape[2]
    one = identity(n)
    parts = []
    for k, bit in enumerate((4, 2, 1)):
        element = (maps_ref[k], noises_ref[k, 0:n], noises_ref[k, n:])
        parts.append(tuple(jnp.where(bit_of(rank, bit) == 1, a, b) for a, b in zip(element, one)))

    def put(s, element):
        em, en, es = element
        out_ref[s, 0:n, :], out_ref[s, n:2 * n, :], out_ref[s, 2 * n:, :] = em, en, es

    def sub(s, carry):
        before = out_ref[s, 0:n, :], out_ref[s, n:2 * n, :], out_ref[s, 2 * n:, :]
        put(s + 1, joined(before, (subs_ref[s], sub_noises_ref[s, 0:n, :], sub_noises_ref[s, n:, :])))
        return carry

    def split(s, carry):
        row_ref[s, 0:1, :], col_ref[s], rest_ref[s] = apart(out_ref[s, 0:n, :])
        return carry

    put(0, joined(parts[0], joined(parts[1], parts[2])))
    lax.fori_loop(0, out_ref.shape[0] - 1, sub, 0)
    lax.fori_loop(0, out_ref.shape[0], split, 0)


def before_kernel(axes, bits, var_ref, mean_ref, *refs):
    map_ref, noise_ref, shift_ref, rest_ref, col_ref, row_ref = refs[-6:]
    rank = rank_of(axes)
    before = identity(map_ref.shape[0])
    for k, bit in enumerate(bits):
        r_ref, x_ref, other_ref = refs[3 * k:3 * k + 3]
        noise, shift = unpack(other_ref[...])
        other = whole(rank % 2 == 1, r_ref, x_ref), noise, rows16(shift)
        new = other if k == 0 else joined(other, before)
        before = tuple(jnp.where(bit_of(rank, bit) == 1, a, b) for a, b in zip(new, before))
    n = map_ref.shape[0]
    start = jnp.zeros((n, n), f32), jnp.where(eye_mask(n), var_ref[...], 0.0), rows16(mean_ref[...])
    before = tuple(jnp.where(rank // PLANE == 0, a, b) for a, b in zip(start, before))
    map_ref[...], noise_ref[...], shift_ref[...] = before
    row_ref[0:1, :], col_ref[...], rest_ref[...] = apart(before[0])


def turn_kernel(sub, g_ref, delta_ref, token_ref, high_ref, low_ref, diag_ref):
    steps, n = high_ref.shape[:2]
    eye = eye_mask(n)

    def step(j, carry):
        turned = g_ref[sub, j].T
        diag_ref[pl.ds(j, 1), :] = delta_ref[pl.ds(sub * steps + j, 1), :] + diag_row(turned)
        high_ref[j], low_ref[j] = halves(jnp.where(eye, 0.0, turned))
        return carry

    lax.fori_loop(0, steps, step, 0, unroll=2)


def finish_kernel(axes, bit, parts, *refs):
    high, low, diag = refs[:parts], refs[parts:2 * parts], refs[2 * parts:3 * parts]
    var_ref, mean_ref, place_ref, rest_ref, col_ref, arow_ref, bmap_ref, bnoise_ref, bshift_ref, brest_ref, bcol_ref, brow_ref, r_ref, x_ref, means_ref, vars_ref, left_s, row_s = refs[3 * parts:]
    n = left_s.shape[-1]
    steps = high[0].shape[0]
    rank = rank_of(axes)
    is_high = bit_of(rank, bit) == 1
    received, moved = unpack(whole(rank % 2 == 1, r_ref, x_ref))
    noise = conjugate((brow_ref[0:1, :], bcol_ref[...], brest_ref[...]), received)
    state = jnp.where(is_high, noise, 0.0) + bnoise_ref[...]
    moved = jnp.where(is_high, through(bmap_ref[...], moved), 0.0) + bshift_ref[0:1, :]
    for s in range(parts):
        p = conjugate((arow_ref[s, 0:1, :], col_ref[s], rest_ref[s]), state) + place_ref[s, n:2 * n, :]
        mean = through(place_ref[s, 0:n, :], moved) + place_ref[s, 2 * n:2 * n + 1, :]
        mh, ml = halves(mean)
        left_s[s, 0:n, :] = p.astype(bf16)
        left_s[s, n:, :] = jnp.concatenate([mh, ml, jnp.zeros((14, n), bf16)], axis=0)
        row_s[s, 0:1, :] = mean
        row_s[s, 1:2, :] = diag_row(p)

    def step(j, carry):
        both = [nn(left_s[s], high[s][j]) for s in range(parts)]
        rest = [nn(left_s[s, n:, :], low[s][j]) for s in range(parts)]
        for s in range(parts):
            t = s * steps + j
            d = diag[s][pl.ds(j, 1), :]
            vars_ref[pl.ds(t, 1), :] = (var_ref[pl.ds(t, 1), :] + d * (d * row_s[s, 1:2, :] + 2.0 * diag_row(both[s]))
                                        + jnp.sum(high[s][j].astype(f32) * both[s][:n], axis=0, keepdims=True))
            means_ref[pl.ds(t, 1), :] = (mean_ref[pl.ds(t, 1), :] + d * row_s[s, 0:1, :]
                                         + both[s][n:n + 1] + (both[s][n + 1:n + 2] + rest[s][0:1]))
        return carry

    lax.fori_loop(0, steps, step, 0, unroll=4)


def vmem():
    return pl.BlockSpec(memory_space=pltpu.VMEM)


def anywhere():
    return pl.BlockSpec(memory_space=pl.ANY)


def shape(*dims, dtype=f32):
    return jax.ShapeDtypeStruct(dims, dtype)


def call(kernel, name, outs, args, specs=None, scratch=(), limit=16, flops=10 ** 5):
    return pl.pallas_call(
        kernel,
        in_specs=specs or [vmem()] * len(args),
        out_specs=[vmem()] * len(outs),
        out_shape=outs,
        scratch_shapes=scratch,
        compiler_params=pltpu.CompilerParams(vmem_limit_bytes=limit * 1024 * 1024),
        cost_estimate=pl.CostEstimate(flops=flops, bytes_accessed=0, transcendentals=0),
        name=name,
    )(*args)


def hbm():
    return pl.BlockSpec(memory_space=pltpu.HBM)


def step_maps(subs, decay, coupling, obs_map, gain, observed):
    T, n = decay.shape
    m = obs_map.shape[1]
    steps = T // subs
    outs = [shape(subs, steps, n, n), shape(subs, steps, n, n, dtype=bf16), shape(subs, steps, n, 128),
            shape(T, n), shape(T, n), shape(subs + 2, n, n), shape(n, n)]
    args = [decay, coupling.reshape(subs, steps, n, n), obs_map.reshape(subs, steps, m, n),
            gain.reshape(subs, steps, m, n), observed]
    scratch = [pltpu.VMEM(x.shape, x.dtype) for x in args]
    args = [pltpu.with_memory_space_constraint(x, pltpu.HBM) for x in args]
    scratch += [pltpu.SemaphoreType.DMA((2,)), pltpu.SemaphoreType.DMA((3, steps)), pltpu.VMEM((subs, n, n), f32),
                pltpu.VMEM((subs, n, n), f32), pltpu.VMEM((subs, n, n), bf16), pltpu.VMEM((subs, 8, n), f32)]
    return call(functools.partial(maps_kernel, subs), "step_maps", outs, args, [hbm()] * len(args), scratch,
                limit=26, flops=10 ** 10)


def step_shapes(subs, obs_map, gain, noise_factor, token):
    T, m, n = obs_map.shape
    steps = T // subs
    return call(shapes_kernel, "step_shapes", [shape(subs, steps, n, n, dtype=bf16)],
                [obs_map.reshape(subs, steps, m, n), gain.reshape(subs, steps, m, n), noise_factor, token],
                [vmem()] * 3 + [anywhere()], [pltpu.VMEM((steps, subs * m, n), bf16)])[0]


def step_noises(subs, decay, e, dcol, shaped, gain, obs_var, shift, maps, token):
    T, n = decay.shape
    m = gain.shape[1]
    args = [decay, e, dcol, shaped, gain.reshape(subs, T // subs, m, n), obs_var.reshape(1, m),
            shift, maps, token]
    return call(functools.partial(noises_kernel, subs), "step_noises",
                [shape(T, n), shape(subs, n + 16, n), shape(n // 2 + 16, n)], args, [vmem()] * 8 + [anywhere()],
                [pltpu.VMEM((subs, n, n), f32)])


def turn(sub, g, delta, token):
    _, steps, n, _ = g.shape
    return call(functools.partial(turn_kernel, sub), "turn",
                [shape(steps, n, n, dtype=bf16), shape(steps, n, n, dtype=bf16), shape(steps, n)],
                [g, delta, token], [vmem()] * 2 + [anywhere()], flops=10 ** 5)


def finish(axes, bit, turned, var, mean, placed, before, r, x):
    parts = len(turned)
    T, n = var.shape
    high, low, diag = zip(*turned)
    return call(functools.partial(finish_kernel, axes, bit, parts), "finish", [shape(T, n)] * 2,
                [*high, *low, *diag, var, mean, *placed, *before, r, x],
                scratch=[pltpu.VMEM((parts, n + 16, n), bf16), pltpu.VMEM((parts, 8, n), f32)])


def per_device(axes, init_mean, init_var, decay, coupling, obs_map, gain, noise_factor, obs_var, observed):
    n = decay.shape[1]
    h = n // 2
    subs = 4
    count = 1
    for _, size in axes:
        count *= size
    names = tuple(name for name, _ in axes)

    def swap(x, bit):
        return lax.ppermute(x, names, [(k, k ^ bit) for k in range(count)])

    bits = []
    bit = PLANE
    while bit < count:
        bits.append(bit)
        bit *= 2

    g, e, dcol, delta, shift, maps, own = step_maps(subs, decay, coupling, obs_map, gain, observed)
    other = swap(own, 1)
    shaped = step_shapes(subs, obs_map, gain, noise_factor, delta)
    (chip_map,) = call(functools.partial(chip_kernel, axes), "chip_maps", [shape(n, n)], [own, other, shaped],
                       [vmem()] * 2 + [anywhere()])
    far = [swap(chip_map, bit) for bit in (2, 4, 6)]
    diag, noises, packed = step_noises(subs, decay, e, dcol, shaped, gain, obs_var, shift, maps, chip_map)
    other_packed = swap(packed, 1)
    chip, chip_half = call(functools.partial(core_kernel, axes), "core_noises", [shape(h + 16, n), shape(h // 2 + 8, n)],
                   [own, other, packed, other_packed])
    chips = [chip] + [v for r in [swap(chip_half, bit) for bit in (2, 4, 6)] for v in (r, swap(r, 1))]
    *far, _ = lax.optimization_barrier((*far, chip))
    *late, total, half, map_picks = call(
        functools.partial(plane_maps_kernel, axes), "plane_maps",
        [shape(3, n, n), shape(3, n, n, dtype=bf16), shape(3, n, 128), shape(8, n), shape(n + 16, n), shape(n, n), shape(h, n), shape(3, n, n)],
        [chip_map, *far, other, init_var.reshape(1, n), init_mean.reshape(1, n)], [anywhere()] * 4 + [vmem()] * 3,
        [pltpu.VMEM((4, n, n), f32), pltpu.SemaphoreType.DMA((4,))])
    size = h + 16 if len(bits) > 1 else h // 2 + 8
    packed, noise_picks = call(
        functools.partial(plane_noises_kernel, axes), "plane_noises",
        [shape(size, n), shape(3, n + 16, n)],
        [*chips, *late, other_packed], [anywhere()] * 7 + [vmem()] * 6,
        [pltpu.VMEM((4, h + 16, n), f32), pltpu.VMEM((h + 16, n), f32), pltpu.SemaphoreType.DMA((7,))])
    placed = call(functools.partial(place_kernel, axes), "place",
                  [shape(subs, 2 * n + 16, n), shape(subs, n, n, dtype=bf16), shape(subs, n, 128), shape(subs, 8, n)],
                  [maps, noises, map_picks, noise_picks])
    received = []
    for k, bit in enumerate(bits[:-1]):
        moving = swap(packed, bit)
        r, packed = lax.optimization_barrier((swap(half, bit), packed))
        got = (r, swap(r, 1), moving)
        received += got
        more = k < len(bits) - 2
        size = h + 16 if more else h // 2 + 8
        new = call(functools.partial(level_kernel, axes, bit), "level",
                   [shape(size, n)] + ([shape(n, n), shape(h, n)] if more else []), [total, packed, *got, placed[3]],
                   [vmem()] * 5 + [anywhere()], [pltpu.VMEM((h + 16, n), f32)])
        packed = new[0]
        if more:
            total, half = new[1:]
    before = call(functools.partial(before_kernel, axes, bits[:-1]), "before",
                  [shape(n, n), shape(n, n), shape(16, n), shape(n, n, dtype=bf16), shape(n, 128), shape(8, n)],
                  [init_var.reshape(1, n), init_mean.reshape(1, n), *received])
    turned = [turn(k, g, delta, packed) for k in range(subs)]
    r, *_ = lax.optimization_barrier((swap(packed, bits[-1]), *before, *(x[2] for x in turned[:3])))
    return tuple(finish(axes, bits[-1], turned, diag, shift, placed, before, r, swap(r, 1)))


def solution(mesh):
    axes = tuple((name, mesh.shape[name]) for name in mesh.axis_names)
    time = P(tuple(mesh.axis_names))
    return jax.shard_map(
        functools.partial(per_device, axes),
        mesh=mesh,
        in_specs=(P(), P(), time, time, time, time, P(), P(), time),
        out_specs=(time, time),
        check_vma=False,
    )
```

```python
import functools

import jax
import jax.numpy as jnp
from jax import lax
from jax.experimental import pallas as pl
from jax.experimental.pallas import tpu as pltpu
from jax.sharding import PartitionSpec as P

f32, bf16 = jnp.float32, jnp.bfloat16
PLANE = 8


def nn(a, b):
    return jnp.dot(a, b, preferred_element_type=f32)


def nt(a, b):
    return lax.dot_general(a, b, (((1,), (1,)), ((), ())), preferred_element_type=f32)


def halves(x):
    high = x.astype(bf16)
    return high, (x - high.astype(f32)).astype(bf16)


def times(late, early):
    (lh, ll), (eh, el) = late, early
    return nn(lh, eh) + (nn(ll, eh) + nn(lh, el))


def advance(late, noise, shift):
    n = noise.shape[1]
    lh, ll = late
    xh, xl = halves(jnp.concatenate([times(late, halves(noise)), shift], axis=0))
    out = nt(xh, lh) + (nt(xl, lh) + nt(xh, ll))
    return out[:n], out[n:]


def wide(col):
    return jnp.concatenate([col, col], axis=1)


def apart(late):
    row = diag_row(late)
    return row, spread(row), jnp.where(eye_mask(late.shape[0]), 0.0, late).astype(bf16)


def conjugate(late, noise):
    row, col, rest = late
    x = wide(col) * noise + nn(rest, noise.astype(bf16))
    return x * row + nt(x.astype(bf16), rest)


def through(late, shift):
    return row_of(jnp.sum(late * shift, axis=1, keepdims=True))


def joined(early, late):
    parts = halves(late[0])
    noise, shift = advance(parts, early[1], early[2])
    return times(parts, halves(early[0])), noise + late[1], shift + late[2]


def eye_mask(n):
    return lax.broadcasted_iota(jnp.int32, (n, n), 0) == lax.broadcasted_iota(jnp.int32, (n, n), 1)


def column(row):
    n = row.shape[1]
    out = []
    for k in range(0, n, 128):
        m = min(128, n - k)
        out.append(jnp.sum(jnp.where(eye_mask(m), row[:, k:k + m], 0.0), axis=1, keepdims=True))
    return out[0] if len(out) == 1 else jnp.concatenate(out, axis=0)


def spread(row):
    n = row.shape[1]
    return jnp.concatenate([jnp.broadcast_to(row[:, k:k + 128], (128, 128)).T for k in range(0, n, 128)], axis=0)


def row_of(col):
    n = col.shape[0]
    out = [jnp.sum(jnp.where(eye_mask(128), col[k:k + 128], 0.0), axis=0, keepdims=True) for k in range(0, n, 128)]
    return jnp.concatenate(out, axis=1)


def diag_row(x):
    n = x.shape[1]
    out = [jnp.sum(jnp.where(eye_mask(128), x[k:k + 128, k:k + 128], 0.0), axis=0, keepdims=True)
           for k in range(0, n, 128)]
    return jnp.concatenate(out, axis=1)


def rows16(row):
    return jnp.broadcast_to(row, (16, row.shape[1]))


def pack(noise, shift):
    n = noise.shape[1]
    h = n // 2
    lower = lax.broadcasted_iota(jnp.int32, (h, h), 0) >= lax.broadcasted_iota(jnp.int32, (h, h), 1)
    a, b, c = noise[:h, :h], noise[:h, h:], noise[h:, h:]
    body = jnp.concatenate([jnp.where(lower, a, c), b], axis=1)
    extra = jnp.concatenate([jnp.zeros((1, h), f32), diag_row(noise)[:, h:]], axis=1)
    return jnp.concatenate([body, shift[0:1], extra, jnp.zeros((14, n), f32)], axis=0)


def unpack(x):
    n = x.shape[1]
    h = n // 2
    i = lax.broadcasted_iota(jnp.int32, (h, h), 0)
    j = lax.broadcasted_iota(jnp.int32, (h, h), 1)
    body, b = x[:h, :h], x[:h, h:]
    turned = body.T
    a = jnp.where(i >= j, body, turned)
    c = jnp.where(i == j, x[h + 1:h + 2, h:], jnp.where(i < j, body, turned))
    noise = jnp.concatenate([jnp.concatenate([a, b], axis=1), jnp.concatenate([b.T, c], axis=1)], axis=0)
    return noise, x[h:h + 1]


def rank_of(axes):
    rank = 0
    for name, size in axes:
        rank = rank * size + lax.axis_index(name)
    return rank


def bit_of(rank, bit):
    return (rank // bit) % 2


def put_half(ref, total_ref, upper):
    rows = ref.shape[0]
    ref[...] = jnp.where(upper, total_ref[rows:], total_ref[:rows])


def put_out(ref, total_ref, upper):
    if ref.shape[0] == total_ref.shape[0]:
        ref[...] = total_ref[...]
    else:
        put_half(ref, total_ref, upper)


def whole(upper, mine_ref, others_ref):
    mine, others = mine_ref[...], others_ref[...]
    return jnp.concatenate([jnp.where(upper, others, mine), jnp.where(upper, mine, others)], axis=0)


def identity(n):
    return jnp.where(eye_mask(n), 1.0, 0.0), jnp.zeros((n, n), f32), jnp.zeros((16, n), f32)


def maps_kernel(subs, decay_hbm, coup_hbm, omap_hbm, gain_hbm, seen_hbm,
                g_ref, e_ref, dcol_ref, delta_ref, shift_ref, maps_ref, total_ref,
                decay_ref, coup_ref, omap_ref, gain_ref, seen_ref, small_sem, sem, g_s, part_s, eh_s, row_s):
    n = decay_ref.shape[1]
    steps = coup_ref.shape[1]
    small = [pltpu.make_async_copy(x, y, small_sem.at[k]) for k, (x, y) in enumerate(
        [(decay_hbm, decay_ref), (seen_hbm, seen_ref)])]

    def chunk(j):
        return [pltpu.make_async_copy(x.at[:, j], y.at[:, j], sem.at[k, j]) for k, (x, y) in enumerate(
            [(coup_hbm, coup_ref), (omap_hbm, omap_ref), (gain_hbm, gain_ref)])]

    for c in small + chunk(0):
        c.start()
    for j in range(1, steps):
        for c in chunk(j):
            c.start()
    for c in small:
        c.wait()

    def step(j, first):
        for c in chunk(j):
            c.wait()
        all_subs = range(subs)
        rows = [decay_ref[pl.ds(s * steps + j, 1), :] for s in all_subs]
        obs_f = [(omap_ref[s, j].astype(f32) * rows[s] + nn(omap_ref[s, j], coup_ref[s, j])).astype(bf16)
                 for s in all_subs]

        def build(s):
            t = s * steps + j
            gain = gain_ref[s, j]
            e = coup_ref[s, j].astype(f32) - nn(gain.T, obs_f[s])
            e_h = e.astype(bf16)
            e_ref[s, j] = e_h
            eh_s[s] = e_h
            col = spread(rows[s])
            dcol_ref[s, j] = col
            shift = jnp.sum(gain.astype(f32) * column(seen_ref[pl.ds(t, 1), :]), axis=0, keepdims=True)
            if first:
                g_s[s] = e
                g_ref[s, j] = e
                delta, b_new = rows[s], shift
            else:
                delta = row_s[s, 0:1, :]
                b = row_s[s, 1:2, :]
                part_s[s] = wide(col) * g_s[s] + e * delta
                delta = delta * rows[s]
                b_new = rows[s] * b + row_of(jnp.sum(e * b, axis=1, keepdims=True)) + shift
            shift_ref[pl.ds(t, 1), :] = b_new
            delta_ref[pl.ds(t, 1), :] = delta
            row_s[s, 0:1, :] = delta
            row_s[s, 1:2, :] = b_new

        def follow(s):
            if not first:
                g_new = part_s[s] + nn(eh_s[s], g_s[s].astype(bf16))
                g_s[s] = g_new
                g_ref[s, j] = g_new

        build(0)
        build(1)
        follow(0)
        build(2)
        follow(1)
        build(3)
        follow(2)
        follow(3)

    step(0, True)
    lax.fori_loop(1, steps, lambda j, c: (step(j, False), c)[1], 0)

    eye = eye_mask(n)
    maps = [g_ref[s, steps - 1] + jnp.where(eye, delta_ref[(s + 1) * steps - 1:(s + 1) * steps, :], 0.0)
            for s in range(subs)]
    for s in range(subs):
        maps_ref[s] = maps[s]
    parts = [halves(m) for m in maps]
    low, high = times(parts[1], parts[0]), times(parts[3], parts[2])
    maps_ref[subs] = low
    maps_ref[subs + 1] = high
    total_ref[...] = times(halves(high), halves(low))


def shapes_kernel(omap_ref, gain_ref, nf_ref, _, shaped_ref, seen_s):
    subs, steps, m = omap_ref.shape[:3]
    nf = nf_ref[...]

    def see(j, carry):
        seen_s[j] = nn(jnp.concatenate([omap_ref[s, j] for s in range(subs)], axis=0), nf).astype(bf16)
        return carry

    def shape_step(j, carry):
        shaped = [(nf.astype(f32) - nn(gain_ref[s, j].T, seen_s[j, s * m:(s + 1) * m])).astype(bf16) for s in range(subs)]
        for s in range(subs):
            shaped_ref[s, j] = shaped[s]
        return carry

    lax.fori_loop(0, steps, see, 0, unroll=4)
    lax.fori_loop(0, steps, shape_step, 0, unroll=4)


def noises_kernel(subs, decay_ref, e_ref, dcol_ref, shaped_ref, gain_ref, var_ref, shift_ref,
                  maps_ref, _, diag_ref, noises_ref, total_ref, q_s):
    n = e_ref.shape[-1]
    steps = e_ref.shape[1]
    var_col = column(var_ref[...])
    all_subs = range(subs)

    def noise(s, j):
        shaped, gain = shaped_ref[s, j], gain_ref[s, j]
        return nt(shaped, shaped) + nn(gain.T, (gain.astype(f32) * var_col).astype(bf16))

    def first_half(s, j, q):
        return wide(dcol_ref[s, j]) * q + nn(e_ref[s, j], q.astype(bf16))

    def second_half(s, j, x):
        return x * decay_ref[pl.ds(s * steps + j, 1), :] + (nt(x.astype(bf16), e_ref[s, j]) + noise(s, j))

    def step(j, carry):
        x = [first_half(s, j, q_s[s]) for s in all_subs]
        for s in all_subs:
            q_new = second_half(s, j, x[s])
            q_s[s] = q_new
            diag_ref[pl.ds(s * steps + j, 1), :] = diag_row(q_new)
        return carry

    for s in all_subs:
        q_s[s] = noise(s, 0)

    for s in all_subs:
        diag_ref[pl.ds(s * steps, 1), :] = diag_row(q_s[s])
    lax.fori_loop(1, steps, step, 0)

    shift = [shift_ref[(s + 1) * steps - 1:(s + 1) * steps, :] for s in range(subs)]
    pairs = [(conjugate(apart(maps_ref[s + 1]), q_s[s]) + q_s[s + 1], through(maps_ref[s + 1], shift[s]) + shift[s + 1])
             for s in (0, 2)]
    last = maps_ref[subs + 1]
    total_ref[...] = pack(conjugate(apart(last), pairs[0][0]) + pairs[1][0], through(last, pairs[0][1]) + pairs[1][1])
    for s in range(subs):
        noises_ref[s, 0:n, :] = q_s[s]
        noises_ref[s, n:, :] = rows16(shift[s])


def chip_kernel(axes, own_ref, other_ref, _, out_ref):
    upper = rank_of(axes) % 2 == 1
    own, other = own_ref[...], other_ref[...]
    out_ref[...] = times(halves(jnp.where(upper, own, other)), halves(jnp.where(upper, other, own)))


def core_kernel(axes, own_map_ref, other_map_ref, own_ref, other_ref, out_ref, half_ref):
    upper = rank_of(axes) % 2 == 1
    own, other = unpack(own_ref[...]), unpack(other_ref[...])
    late = jnp.where(upper, own_map_ref[...], other_map_ref[...])
    early_noise, early_shift = (jnp.where(upper, a, b) for a, b in zip(other, own))
    late_noise, late_shift = (jnp.where(upper, a, b) for a, b in zip(own, other))
    out_ref[...] = pack(conjugate(apart(late), early_noise) + late_noise, through(late, early_shift) + late_shift)
    put_half(half_ref, out_ref, upper)


def fetch(rank, refs, dst, sem):
    place = (rank % PLANE) // (PLANE // len(refs))
    copies = [pltpu.make_async_copy(r, dst.at[place ^ k], sem.at[k]) for k, r in enumerate(refs)]
    for c in copies:
        c.start()
    for c in copies:
        c.wait()


def plane_maps_kernel(axes, *refs):
    ins, refs = refs[:4], refs[4:]
    core_ref, var_ref, mean_ref, late_ref, rest_ref, col_ref, row_ref, start_ref, total_ref, half_ref, picks_ref, chip_s, sem = refs
    rank = rank_of(axes)
    fetch(rank, ins, chip_s, sem)

    def keep(k, late):
        late_ref[k] = late
        row_ref[k:k + 1, :], col_ref[k], rest_ref[k] = apart(late)

    chips = [chip_s[k] for k in range(4)]
    pairs = [times(halves(chips[2 * k + 1]), halves(chips[2 * k])) for k in range(2)]
    total = times(halves(pairs[1]), halves(pairs[0]))
    first = rank // PLANE == 0
    n = total.shape[0]
    noise = conjugate(apart(total), jnp.where(eye_mask(n), var_ref[...], 0.0))
    start_ref[0:n, :] = jnp.where(first, noise, 0.0)
    start_ref[n:, :] = rows16(jnp.where(first, through(total, mean_ref[...]), 0.0))
    total_ref[...] = jnp.where(first, 0.0, total)
    for k, late in enumerate((chips[1], chips[3], pairs[1])):
        keep(k, late)
    h = half_ref.shape[0]
    half_ref[...] = jnp.where(rank % 2 == 1, total_ref[h:], total_ref[:h])
    picks_ref[0] = pairs[0]
    picks_ref[1] = chip_s[2 * bit_of(rank, 4)]
    picks_ref[2] = core_ref[...]


def plane_noises_kernel(axes, *refs):
    ins, (late_ref, rest_ref, col_ref, row_ref, start_ref, core_ref, out_ref, picks_ref, in_s, total_s, sem) = refs[:7], refs[7:]
    rank = rank_of(axes)
    place = (rank % PLANE) // 2
    rows = total_s.shape[0] // 2
    copies = [pltpu.make_async_copy(ins[0], in_s.at[place], sem.at[0])]
    for k in range(1, 4):
        for other in range(2):
            part = (rank % 2) ^ other
            copies.append(pltpu.make_async_copy(
                ins[2 * k - 1 + other], in_s.at[place ^ k, pl.ds(pl.multiple_of(part * rows, 8), rows)],
                sem.at[2 * k - 1 + other]))
    for c in copies:
        c.start()
    for c in copies:
        c.wait()
    n = late_ref.shape[-1]

    def join(k, early, late):
        noise = conjugate((row_ref[k:k + 1, :], col_ref[k], rest_ref[k]), early[0])
        return noise + late[0], through(late_ref[k], early[1]) + late[1]

    def pick(k, element):
        picks_ref[k, 0:n], picks_ref[k, n:] = element[0], rows16(element[1])

    chips = [unpack(in_s[k]) for k in range(4)]
    pairs = [join(k, chips[2 * k], chips[2 * k + 1]) for k in range(2)]
    noise, shift = join(2, pairs[0], pairs[1])
    total_s[...] = pack(noise + start_ref[0:n, :], shift + start_ref[n:n + 1, :])
    put_out(out_ref, total_s, rank % 2 == 1)
    pick(0, pairs[0])
    pick(1, unpack(in_s[2 * bit_of(rank, 4)]))
    pick(2, unpack(core_ref[...]))


def level_kernel(axes, bit, own_map_ref, own_ref, r_ref, x_ref, other_ref, _, *outs):
    *outs, total_s = outs
    rank = rank_of(axes)
    upper, high = rank % 2 == 1, bit_of(rank, bit) == 1
    other_map, own_map = whole(upper, r_ref, x_ref), own_map_ref[...]
    other, own = unpack(other_ref[...]), unpack(own_ref[...])
    late = jnp.where(high, own_map, other_map)
    early_noise, early_shift = (jnp.where(high, a, b) for a, b in zip(other, own))
    late_noise, late_shift = (jnp.where(high, a, b) for a, b in zip(own, other))
    total_s[...] = pack(conjugate(apart(late), early_noise) + late_noise, through(late, early_shift) + late_shift)
    put_out(outs[0], total_s, upper)
    if len(outs) > 1:
        outs[1][...] = times(halves(late), halves(jnp.where(high, other_map, own_map)))
        put_half(outs[2], outs[1], upper)


def place_kernel(axes, subs_ref, sub_noises_ref, maps_ref, noises_ref, out_ref, rest_ref, col_ref, row_ref):
    rank = rank_of(axes)
    n = out_ref.shape[2]
    one = identity(n)
    parts = []
    for k, bit in enumerate((4, 2, 1)):
        element = (maps_ref[k], noises_ref[k, 0:n], noises_ref[k, n:])
        parts.append(tuple(jnp.where(bit_of(rank, bit) == 1, a, b) for a, b in zip(element, one)))

    def put(s, element):
        em, en, es = element
        out_ref[s, 0:n, :], out_ref[s, n:2 * n, :], out_ref[s, 2 * n:, :] = em, en, es

    def sub(s, carry):
        before = out_ref[s, 0:n, :], out_ref[s, n:2 * n, :], out_ref[s, 2 * n:, :]
        put(s + 1, joined(before, (subs_ref[s], sub_noises_ref[s, 0:n, :], sub_noises_ref[s, n:, :])))
        return carry

    def split(s, carry):
        row_ref[s, 0:1, :], col_ref[s], rest_ref[s] = apart(out_ref[s, 0:n, :])
        return carry

    put(0, joined(parts[0], joined(parts[1], parts[2])))
    lax.fori_loop(0, out_ref.shape[0] - 1, sub, 0)
    lax.fori_loop(0, out_ref.shape[0], split, 0)


def before_kernel(axes, bits, var_ref, mean_ref, *refs):
    map_ref, noise_ref, shift_ref, rest_ref, col_ref, row_ref = refs[-6:]
    rank = rank_of(axes)
    before = identity(map_ref.shape[0])
    for k, bit in enumerate(bits):
        r_ref, x_ref, other_ref = refs[3 * k:3 * k + 3]
        noise, shift = unpack(other_ref[...])
        other = whole(rank % 2 == 1, r_ref, x_ref), noise, rows16(shift)
        new = other if k == 0 else joined(other, before)
        before = tuple(jnp.where(bit_of(rank, bit) == 1, a, b) for a, b in zip(new, before))
    n = map_ref.shape[0]
    start = jnp.zeros((n, n), f32), jnp.where(eye_mask(n), var_ref[...], 0.0), rows16(mean_ref[...])
    before = tuple(jnp.where(rank // PLANE == 0, a, b) for a, b in zip(start, before))
    map_ref[...], noise_ref[...], shift_ref[...] = before
    row_ref[0:1, :], col_ref[...], rest_ref[...] = apart(before[0])


def finish_kernel(axes, bit, per, g_ref, delta_ref, var_ref, mean_ref, place_ref, rest_ref, col_ref, arow_ref,
                  bmap_ref, bnoise_ref, bshift_ref, brest_ref, bcol_ref, brow_ref, r_ref, x_ref, means_ref, vars_ref,
                  p_s, row_s, state_s):
    parts, steps, n, _ = g_ref.shape
    rank = rank_of(axes)
    is_high = bit_of(rank, bit) == 1
    state_s[0:n, :] = bnoise_ref[...]
    state_s[n:, :] = bshift_ref[0:8, :]

    @pl.when(is_high)
    def _():
        received, moved = unpack(whole(rank % 2 == 1, r_ref, x_ref))
        state_s[0:n, :] += conjugate((brow_ref[0:1, :], bcol_ref[...], brest_ref[...]), received)
        state_s[n:, :] += through(bmap_ref[...], moved)

    state, moved = state_s[0:n, :], state_s[n:n + 1, :]
    for s in range(parts):
        p = conjugate((arow_ref[s, 0:1, :], col_ref[s], rest_ref[s]), state) + place_ref[s, n:2 * n, :]
        mean = through(place_ref[s, 0:n, :], moved) + place_ref[s, 2 * n:2 * n + 1, :]
        p_s[s] = p.astype(bf16)
        row_s[s, 0:1, :] = mean
        row_s[s, 1:2, :] = diag_row(p)

    def step(k, carry):
        s, j = k // (steps // per), (k % (steps // per)) * per
        g = g_ref[s, pl.ds(j, per)]
        both = nn(g.reshape(per * n, n).astype(bf16), p_s[s])
        mean, spread_of = row_s[s, 0:1, :], row_s[s, 1:2, :]
        for i in range(per):
            t = s * steps + j + i
            d = delta_ref[pl.ds(t, 1), :]
            w = both[i * n:(i + 1) * n]
            vars_ref[pl.ds(t, 1), :] = (var_ref[pl.ds(t, 1), :] + d * (d * spread_of + 2.0 * diag_row(w))
                                        + row_of(jnp.sum(g[i] * w, axis=1, keepdims=True)))
            means_ref[pl.ds(t, 1), :] = mean_ref[pl.ds(t, 1), :] + d * mean + through(g[i], mean)
        return carry

    lax.fori_loop(0, parts * steps // per, step, 0)


def vmem():
    return pl.BlockSpec(memory_space=pltpu.VMEM)


def anywhere():
    return pl.BlockSpec(memory_space=pl.ANY)


def shape(*dims, dtype=f32):
    return jax.ShapeDtypeStruct(dims, dtype)


def call(kernel, name, outs, args, specs=None, scratch=(), limit=16, flops=10 ** 5):
    return pl.pallas_call(
        kernel,
        in_specs=specs or [vmem()] * len(args),
        out_specs=[vmem()] * len(outs),
        out_shape=outs,
        scratch_shapes=scratch,
        compiler_params=pltpu.CompilerParams(vmem_limit_bytes=limit * 1024 * 1024),
        cost_estimate=pl.CostEstimate(flops=flops, bytes_accessed=0, transcendentals=0),
        name=name,
    )(*args)


def hbm():
    return pl.BlockSpec(memory_space=pltpu.HBM)


def step_maps(subs, decay, coupling, obs_map, gain, observed):
    T, n = decay.shape
    m = obs_map.shape[1]
    steps = T // subs
    outs = [shape(subs, steps, n, n), shape(subs, steps, n, n, dtype=bf16), shape(subs, steps, n, 128),
            shape(T, n), shape(T, n), shape(subs + 2, n, n), shape(n, n)]
    args = [decay, coupling.reshape(subs, steps, n, n), obs_map.reshape(subs, steps, m, n),
            gain.reshape(subs, steps, m, n), observed]
    scratch = [pltpu.VMEM(x.shape, x.dtype) for x in args]
    args = [pltpu.with_memory_space_constraint(x, pltpu.HBM) for x in args]
    scratch += [pltpu.SemaphoreType.DMA((2,)), pltpu.SemaphoreType.DMA((3, steps)), pltpu.VMEM((subs, n, n), f32),
                pltpu.VMEM((subs, n, n), f32), pltpu.VMEM((subs, n, n), bf16), pltpu.VMEM((subs, 8, n), f32)]
    return call(functools.partial(maps_kernel, subs), "step_maps", outs, args, [hbm()] * len(args), scratch,
                limit=26, flops=10 ** 10)


def step_shapes(subs, obs_map, gain, noise_factor, token):
    T, m, n = obs_map.shape
    steps = T // subs
    return call(shapes_kernel, "step_shapes", [shape(subs, steps, n, n, dtype=bf16)],
                [obs_map.reshape(subs, steps, m, n), gain.reshape(subs, steps, m, n), noise_factor, token],
                [vmem()] * 3 + [anywhere()], [pltpu.VMEM((steps, subs * m, n), bf16)])[0]


def step_noises(subs, decay, e, dcol, shaped, gain, obs_var, shift, maps, token):
    T, n = decay.shape
    m = gain.shape[1]
    args = [decay, e, dcol, shaped, gain.reshape(subs, T // subs, m, n), obs_var.reshape(1, m),
            shift, maps, token]
    return call(functools.partial(noises_kernel, subs), "step_noises",
                [shape(T, n), shape(subs, n + 16, n), shape(n // 2 + 16, n)], args, [vmem()] * 8 + [anywhere()],
                [pltpu.VMEM((subs, n, n), f32)])


def finish(axes, bit, g, delta, var, mean, placed, before, r, x, per=8):
    parts = g.shape[0]
    T, n = var.shape
    return call(functools.partial(finish_kernel, axes, bit, per), "finish", [shape(T, n)] * 2,
                [g, delta, var, mean, *placed, *before, r, x],
                scratch=[pltpu.VMEM((parts, n, n), bf16), pltpu.VMEM((parts, 8, n), f32), pltpu.VMEM((n + 8, n), f32)])


def per_device(axes, init_mean, init_var, decay, coupling, obs_map, gain, noise_factor, obs_var, observed):
    n = decay.shape[1]
    h = n // 2
    subs = 4
    count = 1
    for _, size in axes:
        count *= size
    names = tuple(name for name, _ in axes)

    def swap(x, bit):
        return lax.ppermute(x, names, [(k, k ^ bit) for k in range(count)])

    bits = []
    bit = PLANE
    while bit < count:
        bits.append(bit)
        bit *= 2

    g, e, dcol, delta, shift, maps, own = step_maps(subs, decay, coupling, obs_map, gain, observed)
    other = swap(own, 1)
    shaped = step_shapes(subs, obs_map, gain, noise_factor, delta)
    (chip_map,) = call(functools.partial(chip_kernel, axes), "chip_maps", [shape(n, n)], [own, other, shaped],
                       [vmem()] * 2 + [anywhere()])
    far = [swap(chip_map, bit) for bit in (2, 4, 6)]
    diag, noises, packed = step_noises(subs, decay, e, dcol, shaped, gain, obs_var, shift, maps, chip_map)
    other_packed = swap(packed, 1)
    chip, chip_half = call(functools.partial(core_kernel, axes), "core_noises", [shape(h + 16, n), shape(h // 2 + 8, n)],
                   [own, other, packed, other_packed])
    chips = [chip] + [v for r in [swap(chip_half, bit) for bit in (2, 4, 6)] for v in (r, swap(r, 1))]
    *far, _ = lax.optimization_barrier((*far, chip))
    *late, total, half, map_picks = call(
        functools.partial(plane_maps_kernel, axes), "plane_maps",
        [shape(3, n, n), shape(3, n, n, dtype=bf16), shape(3, n, 128), shape(8, n), shape(n + 16, n), shape(n, n), shape(h, n), shape(3, n, n)],
        [chip_map, *far, other, init_var.reshape(1, n), init_mean.reshape(1, n)], [anywhere()] * 4 + [vmem()] * 3,
        [pltpu.VMEM((4, n, n), f32), pltpu.SemaphoreType.DMA((4,))])
    size = h + 16 if len(bits) > 1 else h // 2 + 8
    packed, noise_picks = call(
        functools.partial(plane_noises_kernel, axes), "plane_noises",
        [shape(size, n), shape(3, n + 16, n)],
        [*chips, *late, other_packed], [anywhere()] * 7 + [vmem()] * 6,
        [pltpu.VMEM((4, h + 16, n), f32), pltpu.VMEM((h + 16, n), f32), pltpu.SemaphoreType.DMA((7,))])
    placed = call(functools.partial(place_kernel, axes), "place",
                  [shape(subs, 2 * n + 16, n), shape(subs, n, n, dtype=bf16), shape(subs, n, 128), shape(subs, 8, n)],
                  [maps, noises, map_picks, noise_picks])
    received = []
    for k, bit in enumerate(bits[:-1]):
        moving = swap(packed, bit)
        r, packed = lax.optimization_barrier((swap(half, bit), packed))
        got = (r, swap(r, 1), moving)
        received += got
        more = k < len(bits) - 2
        size = h + 16 if more else h // 2 + 8
        new = call(functools.partial(level_kernel, axes, bit), "level",
                   [shape(size, n)] + ([shape(n, n), shape(h, n)] if more else []), [total, packed, *got, placed[3]],
                   [vmem()] * 5 + [anywhere()], [pltpu.VMEM((h + 16, n), f32)])
        packed = new[0]
        if more:
            total, half = new[1:]
    before = call(functools.partial(before_kernel, axes, bits[:-1]), "before",
                  [shape(n, n), shape(n, n), shape(16, n), shape(n, n, dtype=bf16), shape(n, 128), shape(8, n)],
                  [init_var.reshape(1, n), init_mean.reshape(1, n), *received])
    r, *_ = lax.optimization_barrier((swap(packed, bits[-1]), *before))
    return tuple(finish(axes, bits[-1], g, delta, diag, shift, placed, before, r, swap(r, 1)))


def solution(mesh):
    axes = tuple((name, mesh.shape[name]) for name in mesh.axis_names)
    time = P(tuple(mesh.axis_names))
    return jax.shard_map(
        functools.partial(per_device, axes),
        mesh=mesh,
        in_specs=(P(), P(), time, time, time, time, P(), P(), time),
        out_specs=(time, time),
        check_vma=False,
    )
```

```python
import functools

import jax
import jax.numpy as jnp
from jax import lax
from jax.experimental import pallas as pl
from jax.experimental.pallas import tpu as pltpu
from jax.sharding import PartitionSpec as P

f32, bf16 = jnp.float32, jnp.bfloat16
PLANE = 8


def nn(a, b):
    return jnp.dot(a, b, preferred_element_type=f32)


def nt(a, b):
    return lax.dot_general(a, b, (((1,), (1,)), ((), ())), preferred_element_type=f32)


def halves(x):
    high = x.astype(bf16)
    return high, (x - high.astype(f32)).astype(bf16)


def times(late, early):
    (lh, ll), (eh, el) = late, early
    return nn(lh, eh) + (nn(ll, eh) + nn(lh, el))


def advance(late, noise, shift):
    n = noise.shape[1]
    lh, ll = late
    xh, xl = halves(jnp.concatenate([times(late, halves(noise)), shift], axis=0))
    out = nt(xh, lh) + (nt(xl, lh) + nt(xh, ll))
    return out[:n], out[n:]


def wide(col):
    return jnp.concatenate([col, col], axis=1)


def apart(late):
    row = diag_row(late)
    return row, spread(row), jnp.where(eye_mask(late.shape[0]), 0.0, late).astype(bf16)


def conjugate(late, noise):
    row, col, rest = late
    x = wide(col) * noise + nn(rest, noise.astype(bf16))
    return x * row + nt(x.astype(bf16), rest)


def through(late, shift):
    return row_of(jnp.sum(late * shift, axis=1, keepdims=True))


def joined(early, late):
    parts = halves(late[0])
    noise, shift = advance(parts, early[1], early[2])
    return times(parts, halves(early[0])), noise + late[1], shift + late[2]


def eye_mask(n):
    return lax.broadcasted_iota(jnp.int32, (n, n), 0) == lax.broadcasted_iota(jnp.int32, (n, n), 1)


def column(row):
    n = row.shape[1]
    out = []
    for k in range(0, n, 128):
        m = min(128, n - k)
        out.append(jnp.sum(jnp.where(eye_mask(m), row[:, k:k + m], 0.0), axis=1, keepdims=True))
    return out[0] if len(out) == 1 else jnp.concatenate(out, axis=0)


def spread(row):
    n = row.shape[1]
    return jnp.concatenate([jnp.broadcast_to(row[:, k:k + 128], (128, 128)).T for k in range(0, n, 128)], axis=0)


def row_of(col):
    n = col.shape[0]
    out = [jnp.sum(jnp.where(eye_mask(128), col[k:k + 128], 0.0), axis=0, keepdims=True) for k in range(0, n, 128)]
    return jnp.concatenate(out, axis=1)


def diag_row(x):
    n = x.shape[1]
    out = [jnp.sum(jnp.where(eye_mask(128), x[k:k + 128, k:k + 128], 0.0), axis=0, keepdims=True)
           for k in range(0, n, 128)]
    return jnp.concatenate(out, axis=1)


def rows16(row):
    return jnp.broadcast_to(row, (16, row.shape[1]))


def pack(noise, shift):
    n = noise.shape[1]
    h = n // 2
    lower = lax.broadcasted_iota(jnp.int32, (h, h), 0) >= lax.broadcasted_iota(jnp.int32, (h, h), 1)
    a, b, c = noise[:h, :h], noise[:h, h:], noise[h:, h:]
    body = jnp.concatenate([jnp.where(lower, a, c), b], axis=1)
    extra = jnp.concatenate([jnp.zeros((1, h), f32), diag_row(noise)[:, h:]], axis=1)
    return jnp.concatenate([body, shift[0:1], extra, jnp.zeros((14, n), f32)], axis=0)


def unpack(x):
    n = x.shape[1]
    h = n // 2
    i = lax.broadcasted_iota(jnp.int32, (h, h), 0)
    j = lax.broadcasted_iota(jnp.int32, (h, h), 1)
    body, b = x[:h, :h], x[:h, h:]
    turned = body.T
    a = jnp.where(i >= j, body, turned)
    c = jnp.where(i == j, x[h + 1:h + 2, h:], jnp.where(i < j, body, turned))
    noise = jnp.concatenate([jnp.concatenate([a, b], axis=1), jnp.concatenate([b.T, c], axis=1)], axis=0)
    return noise, x[h:h + 1]


def rank_of(axes):
    rank = 0
    for name, size in axes:
        rank = rank * size + lax.axis_index(name)
    return rank


def bit_of(rank, bit):
    return (rank // bit) % 2


def put_half(ref, total_ref, upper):
    rows = ref.shape[0]
    ref[...] = jnp.where(upper, total_ref[rows:], total_ref[:rows])


def put_out(ref, total_ref, upper):
    if ref.shape[0] == total_ref.shape[0]:
        ref[...] = total_ref[...]
    else:
        put_half(ref, total_ref, upper)


def whole(upper, mine_ref, others_ref):
    mine, others = mine_ref[...], others_ref[...]
    return jnp.concatenate([jnp.where(upper, others, mine), jnp.where(upper, mine, others)], axis=0)


def identity(n):
    return jnp.where(eye_mask(n), 1.0, 0.0), jnp.zeros((n, n), f32), jnp.zeros((16, n), f32)


def maps_kernel(subs, decay_hbm, coup_hbm, omap_hbm, gain_hbm, seen_hbm,
                g_ref, e_ref, dcol_ref, delta_ref, shift_ref, maps_ref, total_ref,
                decay_ref, coup_ref, omap_ref, gain_ref, seen_ref, small_sem, sem, g_s, part_s, eh_s, row_s):
    n = decay_ref.shape[1]
    steps = coup_ref.shape[1]
    small = [pltpu.make_async_copy(x, y, small_sem.at[k]) for k, (x, y) in enumerate(
        [(decay_hbm, decay_ref), (seen_hbm, seen_ref)])]

    def chunk(j):
        return [pltpu.make_async_copy(x.at[:, j], y.at[:, j], sem.at[k, j]) for k, (x, y) in enumerate(
            [(coup_hbm, coup_ref), (omap_hbm, omap_ref), (gain_hbm, gain_ref)])]

    for c in small + chunk(0):
        c.start()
    for j in range(1, steps):
        for c in chunk(j):
            c.start()
    for c in small:
        c.wait()

    def step(j, first):
        for c in chunk(j):
            c.wait()
        all_subs = range(subs)
        rows = [decay_ref[pl.ds(s * steps + j, 1), :] for s in all_subs]
        obs_f = [(omap_ref[s, j].astype(f32) * rows[s] + nn(omap_ref[s, j], coup_ref[s, j])).astype(bf16)
                 for s in all_subs]

        def build(s):
            t = s * steps + j
            gain = gain_ref[s, j]
            e = coup_ref[s, j].astype(f32) - nn(gain.T, obs_f[s])
            e_h = e.astype(bf16)
            e_ref[s, j] = e_h
            eh_s[s] = e_h
            col = spread(rows[s])
            dcol_ref[s, j] = col
            shift = jnp.sum(gain.astype(f32) * column(seen_ref[pl.ds(t, 1), :]), axis=0, keepdims=True)
            if first:
                g_s[s] = e
                g_ref[s, j] = e
                delta, b_new = rows[s], shift
            else:
                delta = row_s[s, 0:1, :]
                b = row_s[s, 1:2, :]
                part_s[s] = wide(col) * g_s[s] + e * delta
                delta = delta * rows[s]
                b_new = rows[s] * b + row_of(jnp.sum(e * b, axis=1, keepdims=True)) + shift
            shift_ref[pl.ds(t, 1), :] = b_new
            delta_ref[pl.ds(t, 1), :] = delta
            row_s[s, 0:1, :] = delta
            row_s[s, 1:2, :] = b_new

        def follow(s):
            if not first:
                g_new = part_s[s] + nn(eh_s[s], g_s[s].astype(bf16))
                g_s[s] = g_new
                g_ref[s, j] = g_new

        build(0)
        build(1)
        follow(0)
        build(2)
        follow(1)
        build(3)
        follow(2)
        follow(3)

    step(0, True)
    lax.fori_loop(1, steps, lambda j, c: (step(j, False), c)[1], 0)

    eye = eye_mask(n)
    maps = [g_ref[s, steps - 1] + jnp.where(eye, delta_ref[(s + 1) * steps - 1:(s + 1) * steps, :], 0.0)
            for s in range(subs)]
    for s in range(subs):
        maps_ref[s] = maps[s]
    parts = [halves(m) for m in maps]
    low, high = times(parts[1], parts[0]), times(parts[3], parts[2])
    maps_ref[subs] = low
    maps_ref[subs + 1] = high
    total_ref[...] = times(halves(high), halves(low))


def shapes_kernel(omap_ref, gain_ref, nf_ref, _, shaped_ref, seen_s):
    subs, steps, m = omap_ref.shape[:3]
    nf = nf_ref[...]

    def see(j, carry):
        seen_s[j] = nn(jnp.concatenate([omap_ref[s, j] for s in range(subs)], axis=0), nf).astype(bf16)
        return carry

    def shape_step(j, carry):
        shaped = [(nf.astype(f32) - nn(gain_ref[s, j].T, seen_s[j, s * m:(s + 1) * m])).astype(bf16) for s in range(subs)]
        for s in range(subs):
            shaped_ref[s, j] = shaped[s]
        return carry

    lax.fori_loop(0, steps, see, 0, unroll=4)
    lax.fori_loop(0, steps, shape_step, 0, unroll=4)


def noises_kernel(subs, decay_ref, e_ref, dcol_ref, shaped_ref, gain_ref, var_ref, shift_ref,
                  maps_ref, _, diag_ref, noises_ref, total_ref, q_s):
    n = e_ref.shape[-1]
    steps = e_ref.shape[1]
    var_col = column(var_ref[...])
    all_subs = range(subs)

    def noise(s, j):
        shaped, gain = shaped_ref[s, j], gain_ref[s, j]
        return nt(shaped, shaped) + nn(gain.T, (gain.astype(f32) * var_col).astype(bf16))

    def first_half(s, j, q):
        return wide(dcol_ref[s, j]) * q + nn(e_ref[s, j], q.astype(bf16))

    def second_half(s, j, x):
        return x * decay_ref[pl.ds(s * steps + j, 1), :] + (nt(x.astype(bf16), e_ref[s, j]) + noise(s, j))

    def step(j, carry):
        x = [first_half(s, j, q_s[s]) for s in all_subs]
        for s in all_subs:
            q_new = second_half(s, j, x[s])
            q_s[s] = q_new
            diag_ref[pl.ds(s * steps + j, 1), :] = diag_row(q_new)
        return carry

    for s in all_subs:
        q_s[s] = noise(s, 0)

    for s in all_subs:
        diag_ref[pl.ds(s * steps, 1), :] = diag_row(q_s[s])
    lax.fori_loop(1, steps, step, 0)

    shift = [shift_ref[(s + 1) * steps - 1:(s + 1) * steps, :] for s in range(subs)]
    pairs = [(conjugate(apart(maps_ref[s + 1]), q_s[s]) + q_s[s + 1], through(maps_ref[s + 1], shift[s]) + shift[s + 1])
             for s in (0, 2)]
    last = maps_ref[subs + 1]
    total_ref[...] = pack(conjugate(apart(last), pairs[0][0]) + pairs[1][0], through(last, pairs[0][1]) + pairs[1][1])
    for s in range(subs):
        noises_ref[s, 0:n, :] = q_s[s]
        noises_ref[s, n:, :] = rows16(shift[s])


def chip_kernel(axes, own_ref, other_ref, _, out_ref):
    upper = rank_of(axes) % 2 == 1
    own, other = own_ref[...], other_ref[...]
    out_ref[...] = times(halves(jnp.where(upper, own, other)), halves(jnp.where(upper, other, own)))


def core_kernel(axes, own_map_ref, other_map_ref, own_ref, other_ref, out_ref, half_ref):
    upper = rank_of(axes) % 2 == 1
    own, other = unpack(own_ref[...]), unpack(other_ref[...])
    late = jnp.where(upper, own_map_ref[...], other_map_ref[...])
    early_noise, early_shift = (jnp.where(upper, a, b) for a, b in zip(other, own))
    late_noise, late_shift = (jnp.where(upper, a, b) for a, b in zip(own, other))
    out_ref[...] = pack(conjugate(apart(late), early_noise) + late_noise, through(late, early_shift) + late_shift)
    put_half(half_ref, out_ref, upper)


def fetch(rank, refs, dst, sem):
    place = (rank % PLANE) // (PLANE // len(refs))
    copies = [pltpu.make_async_copy(r, dst.at[place ^ k], sem.at[k]) for k, r in enumerate(refs)]
    for c in copies:
        c.start()
    for c in copies:
        c.wait()


def plane_maps_kernel(axes, *refs):
    ins, refs = refs[:4], refs[4:]
    core_ref, var_ref, mean_ref, late_ref, rest_ref, col_ref, row_ref, start_ref, total_ref, half_ref, picks_ref, chip_s, sem = refs
    rank = rank_of(axes)
    fetch(rank, ins, chip_s, sem)

    def keep(k, late):
        late_ref[k] = late
        row_ref[k:k + 1, :], col_ref[k], rest_ref[k] = apart(late)

    chips = [chip_s[k] for k in range(4)]
    pairs = [times(halves(chips[2 * k + 1]), halves(chips[2 * k])) for k in range(2)]
    total = times(halves(pairs[1]), halves(pairs[0]))
    first = rank // PLANE == 0
    n = total.shape[0]
    noise = conjugate(apart(total), jnp.where(eye_mask(n), var_ref[...], 0.0))
    start_ref[0:n, :] = jnp.where(first, noise, 0.0)
    start_ref[n:, :] = rows16(jnp.where(first, through(total, mean_ref[...]), 0.0))
    total_ref[...] = jnp.where(first, 0.0, total)
    for k, late in enumerate((chips[1], chips[3], pairs[1])):
        keep(k, late)
    h = half_ref.shape[0]
    half_ref[...] = jnp.where(rank % 2 == 1, total_ref[h:], total_ref[:h])
    picks_ref[0] = pairs[0]
    picks_ref[1] = chip_s[2 * bit_of(rank, 4)]
    picks_ref[2] = core_ref[...]


def plane_noises_kernel(axes, *refs):
    ins, (late_ref, rest_ref, col_ref, row_ref, start_ref, core_ref, out_ref, picks_ref, in_s, total_s, sem) = refs[:7], refs[7:]
    rank = rank_of(axes)
    place = (rank % PLANE) // 2
    rows = total_s.shape[0] // 2
    copies = [pltpu.make_async_copy(ins[0], in_s.at[place], sem.at[0])]
    for k in range(1, 4):
        for other in range(2):
            part = (rank % 2) ^ other
            copies.append(pltpu.make_async_copy(
                ins[2 * k - 1 + other], in_s.at[place ^ k, pl.ds(pl.multiple_of(part * rows, 8), rows)],
                sem.at[2 * k - 1 + other]))
    for c in copies:
        c.start()
    for c in copies:
        c.wait()
    n = late_ref.shape[-1]

    def join(k, early, late):
        noise = conjugate((row_ref[k:k + 1, :], col_ref[k], rest_ref[k]), early[0])
        return noise + late[0], through(late_ref[k], early[1]) + late[1]

    def pick(k, element):
        picks_ref[k, 0:n], picks_ref[k, n:] = element[0], rows16(element[1])

    chips = [unpack(in_s[k]) for k in range(4)]
    pairs = [join(k, chips[2 * k], chips[2 * k + 1]) for k in range(2)]
    noise, shift = join(2, pairs[0], pairs[1])
    total_s[...] = pack(noise + start_ref[0:n, :], shift + start_ref[n:n + 1, :])
    put_out(out_ref, total_s, rank % 2 == 1)
    pick(0, pairs[0])
    pick(1, unpack(in_s[2 * bit_of(rank, 4)]))
    pick(2, unpack(core_ref[...]))


def level_kernel(axes, bit, own_map_ref, own_ref, r_ref, x_ref, other_ref, _, *outs):
    *outs, total_s = outs
    rank = rank_of(axes)
    upper, high = rank % 2 == 1, bit_of(rank, bit) == 1
    other_map, own_map = whole(upper, r_ref, x_ref), own_map_ref[...]
    other, own = unpack(other_ref[...]), unpack(own_ref[...])
    late = jnp.where(high, own_map, other_map)
    early_noise, early_shift = (jnp.where(high, a, b) for a, b in zip(other, own))
    late_noise, late_shift = (jnp.where(high, a, b) for a, b in zip(own, other))
    total_s[...] = pack(conjugate(apart(late), early_noise) + late_noise, through(late, early_shift) + late_shift)
    put_out(outs[0], total_s, upper)
    if len(outs) > 1:
        outs[1][...] = times(halves(late), halves(jnp.where(high, other_map, own_map)))
        put_half(outs[2], outs[1], upper)


def place_kernel(axes, subs_ref, sub_noises_ref, maps_ref, noises_ref, out_ref, rest_ref, col_ref, row_ref):
    rank = rank_of(axes)
    n = out_ref.shape[2]
    one = identity(n)
    parts = []
    for k, bit in enumerate((4, 2, 1)):
        element = (maps_ref[k], noises_ref[k, 0:n], noises_ref[k, n:])
        parts.append(tuple(jnp.where(bit_of(rank, bit) == 1, a, b) for a, b in zip(element, one)))

    def put(s, element):
        em, en, es = element
        out_ref[s, 0:n, :], out_ref[s, n:2 * n, :], out_ref[s, 2 * n:, :] = em, en, es

    def sub(s, carry):
        before = out_ref[s, 0:n, :], out_ref[s, n:2 * n, :], out_ref[s, 2 * n:, :]
        put(s + 1, joined(before, (subs_ref[s], sub_noises_ref[s, 0:n, :], sub_noises_ref[s, n:, :])))
        return carry

    def split(s, carry):
        row_ref[s, 0:1, :], col_ref[s], rest_ref[s] = apart(out_ref[s, 0:n, :])
        return carry

    put(0, joined(parts[0], joined(parts[1], parts[2])))
    lax.fori_loop(0, out_ref.shape[0] - 1, sub, 0)
    lax.fori_loop(0, out_ref.shape[0], split, 0)


def before_kernel(axes, bits, var_ref, mean_ref, *refs):
    map_ref, noise_ref, shift_ref, rest_ref, col_ref, row_ref = refs[-6:]
    rank = rank_of(axes)
    before = identity(map_ref.shape[0])
    for k, bit in enumerate(bits):
        r_ref, x_ref, other_ref = refs[3 * k:3 * k + 3]
        noise, shift = unpack(other_ref[...])
        other = whole(rank % 2 == 1, r_ref, x_ref), noise, rows16(shift)
        new = other if k == 0 else joined(other, before)
        before = tuple(jnp.where(bit_of(rank, bit) == 1, a, b) for a, b in zip(new, before))
    n = map_ref.shape[0]
    start = jnp.zeros((n, n), f32), jnp.where(eye_mask(n), var_ref[...], 0.0), rows16(mean_ref[...])
    before = tuple(jnp.where(rank // PLANE == 0, a, b) for a, b in zip(start, before))
    map_ref[...], noise_ref[...], shift_ref[...] = before
    row_ref[0:1, :], col_ref[...], rest_ref[...] = apart(before[0])


def finish_kernel(axes, bit, per, g_ref, delta_ref, var_ref, mean_ref, place_ref, rest_ref, col_ref, arow_ref,
                  bmap_ref, bnoise_ref, bshift_ref, brest_ref, bcol_ref, brow_ref, r_ref, x_ref, means_ref, vars_ref,
                  p_s, row_s, state_s):
    parts, steps, n, _ = g_ref.shape
    rank = rank_of(axes)
    is_high = bit_of(rank, bit) == 1
    state_s[0:n, :] = bnoise_ref[...]
    state_s[n:, :] = bshift_ref[0:8, :]

    @pl.when(is_high)
    def _():
        received, moved = unpack(whole(rank % 2 == 1, r_ref, x_ref))
        state_s[0:n, :] += conjugate((brow_ref[0:1, :], bcol_ref[...], brest_ref[...]), received)
        state_s[n:, :] += through(bmap_ref[...], moved)

    state, moved = state_s[0:n, :], state_s[n:n + 1, :]
    for s in range(parts):
        p = conjugate((arow_ref[s, 0:1, :], col_ref[s], rest_ref[s]), state) + place_ref[s, n:2 * n, :]
        mean = through(place_ref[s, 0:n, :], moved) + place_ref[s, 2 * n:2 * n + 1, :]
        p_s[s] = p.astype(bf16)
        row_s[s, 0:1, :] = mean
        row_s[s, 1:2, :] = diag_row(p)

    def step(k, carry):
        s, j = k // (steps // per), (k % (steps // per)) * per
        g = g_ref[s, pl.ds(j, per)]
        both = nn(g.reshape(per * n, n).astype(bf16), p_s[s])
        mean, spread_of = row_s[s, 0:1, :], row_s[s, 1:2, :]
        t = pl.multiple_of(s * steps + j, per)
        d = delta_ref[pl.ds(t, per), :]
        lane = lax.broadcasted_iota(jnp.int32, (n, 128), 1)
        sums = jnp.zeros((n, 128), f32)
        diags = []
        for i in range(per):
            w = both[i * n:(i + 1) * n]
            diags.append(diag_row(w))
            sums = jnp.where(lane == i, jnp.sum(g[i] * w, axis=1, keepdims=True), sums)
            sums = jnp.where(lane == per + i, jnp.sum(g[i] * mean, axis=1, keepdims=True), sums)
        turned = jnp.concatenate([sums[k:k + 128].T for k in range(0, n, 128)], axis=1)
        vars_ref[pl.ds(t, per), :] = (var_ref[pl.ds(t, per), :] + turned[0:per]
                                      + d * (d * spread_of + 2.0 * jnp.concatenate(diags, axis=0)))
        means_ref[pl.ds(t, per), :] = mean_ref[pl.ds(t, per), :] + d * mean + turned[per:2 * per]
        return carry

    lax.fori_loop(0, parts * steps // per, step, 0)


def vmem():
    return pl.BlockSpec(memory_space=pltpu.VMEM)


def anywhere():
    return pl.BlockSpec(memory_space=pl.ANY)


def shape(*dims, dtype=f32):
    return jax.ShapeDtypeStruct(dims, dtype)


def call(kernel, name, outs, args, specs=None, scratch=(), limit=16, flops=10 ** 5):
    return pl.pallas_call(
        kernel,
        in_specs=specs or [vmem()] * len(args),
        out_specs=[vmem()] * len(outs),
        out_shape=outs,
        scratch_shapes=scratch,
        compiler_params=pltpu.CompilerParams(vmem_limit_bytes=limit * 1024 * 1024),
        cost_estimate=pl.CostEstimate(flops=flops, bytes_accessed=0, transcendentals=0),
        name=name,
    )(*args)


def hbm():
    return pl.BlockSpec(memory_space=pltpu.HBM)


def step_maps(subs, decay, coupling, obs_map, gain, observed):
    T, n = decay.shape
    m = obs_map.shape[1]
    steps = T // subs
    outs = [shape(subs, steps, n, n), shape(subs, steps, n, n, dtype=bf16), shape(subs, steps, n, 128),
            shape(T, n), shape(T, n), shape(subs + 2, n, n), shape(n, n)]
    args = [decay, coupling.reshape(subs, steps, n, n), obs_map.reshape(subs, steps, m, n),
            gain.reshape(subs, steps, m, n), observed]
    scratch = [pltpu.VMEM(x.shape, x.dtype) for x in args]
    args = [pltpu.with_memory_space_constraint(x, pltpu.HBM) for x in args]
    scratch += [pltpu.SemaphoreType.DMA((2,)), pltpu.SemaphoreType.DMA((3, steps)), pltpu.VMEM((subs, n, n), f32),
                pltpu.VMEM((subs, n, n), f32), pltpu.VMEM((subs, n, n), bf16), pltpu.VMEM((subs, 8, n), f32)]
    return call(functools.partial(maps_kernel, subs), "step_maps", outs, args, [hbm()] * len(args), scratch,
                limit=26, flops=10 ** 10)


def step_shapes(subs, obs_map, gain, noise_factor, token):
    T, m, n = obs_map.shape
    steps = T // subs
    return call(shapes_kernel, "step_shapes", [shape(subs, steps, n, n, dtype=bf16)],
                [obs_map.reshape(subs, steps, m, n), gain.reshape(subs, steps, m, n), noise_factor, token],
                [vmem()] * 3 + [anywhere()], [pltpu.VMEM((steps, subs * m, n), bf16)])[0]


def step_noises(subs, decay, e, dcol, shaped, gain, obs_var, shift, maps, token):
    T, n = decay.shape
    m = gain.shape[1]
    args = [decay, e, dcol, shaped, gain.reshape(subs, T // subs, m, n), obs_var.reshape(1, m),
            shift, maps, token]
    return call(functools.partial(noises_kernel, subs), "step_noises",
                [shape(T, n), shape(subs, n + 16, n), shape(n // 2 + 16, n)], args, [vmem()] * 8 + [anywhere()],
                [pltpu.VMEM((subs, n, n), f32)])


def finish(axes, bit, g, delta, var, mean, placed, before, r, x, per=8):
    parts = g.shape[0]
    T, n = var.shape
    return call(functools.partial(finish_kernel, axes, bit, per), "finish", [shape(T, n)] * 2,
                [g, delta, var, mean, *placed, *before, r, x],
                scratch=[pltpu.VMEM((parts, n, n), bf16), pltpu.VMEM((parts, 8, n), f32), pltpu.VMEM((n + 8, n), f32)])


def per_device(axes, init_mean, init_var, decay, coupling, obs_map, gain, noise_factor, obs_var, observed):
    n = decay.shape[1]
    h = n // 2
    subs = 4
    count = 1
    for _, size in axes:
        count *= size
    names = tuple(name for name, _ in axes)

    def swap(x, bit):
        return lax.ppermute(x, names, [(k, k ^ bit) for k in range(count)])

    bits = []
    bit = PLANE
    while bit < count:
        bits.append(bit)
        bit *= 2

    g, e, dcol, delta, shift, maps, own = step_maps(subs, decay, coupling, obs_map, gain, observed)
    other = swap(own, 1)
    shaped = step_shapes(subs, obs_map, gain, noise_factor, delta)
    (chip_map,) = call(functools.partial(chip_kernel, axes), "chip_maps", [shape(n, n)], [own, other, shaped],
                       [vmem()] * 2 + [anywhere()])
    far = [swap(chip_map, bit) for bit in (2, 4, 6)]
    diag, noises, packed = step_noises(subs, decay, e, dcol, shaped, gain, obs_var, shift, maps, chip_map)
    other_packed = swap(packed, 1)
    chip, chip_half = call(functools.partial(core_kernel, axes), "core_noises", [shape(h + 16, n), shape(h // 2 + 8, n)],
                   [own, other, packed, other_packed])
    chips = [chip] + [v for r in [swap(chip_half, bit) for bit in (2, 4, 6)] for v in (r, swap(r, 1))]
    *far, _ = lax.optimization_barrier((*far, chip))
    *late, total, half, map_picks = call(
        functools.partial(plane_maps_kernel, axes), "plane_maps",
        [shape(3, n, n), shape(3, n, n, dtype=bf16), shape(3, n, 128), shape(8, n), shape(n + 16, n), shape(n, n), shape(h, n), shape(3, n, n)],
        [chip_map, *far, other, init_var.reshape(1, n), init_mean.reshape(1, n)], [anywhere()] * 4 + [vmem()] * 3,
        [pltpu.VMEM((4, n, n), f32), pltpu.SemaphoreType.DMA((4,))])
    size = h + 16 if len(bits) > 1 else h // 2 + 8
    packed, noise_picks = call(
        functools.partial(plane_noises_kernel, axes), "plane_noises",
        [shape(size, n), shape(3, n + 16, n)],
        [*chips, *late, other_packed], [anywhere()] * 7 + [vmem()] * 6,
        [pltpu.VMEM((4, h + 16, n), f32), pltpu.VMEM((h + 16, n), f32), pltpu.SemaphoreType.DMA((7,))])
    placed = call(functools.partial(place_kernel, axes), "place",
                  [shape(subs, 2 * n + 16, n), shape(subs, n, n, dtype=bf16), shape(subs, n, 128), shape(subs, 8, n)],
                  [maps, noises, map_picks, noise_picks])
    received = []
    for k, bit in enumerate(bits[:-1]):
        moving = swap(packed, bit)
        r, packed = lax.optimization_barrier((swap(half, bit), packed))
        got = (r, swap(r, 1), moving)
        received += got
        more = k < len(bits) - 2
        size = h + 16 if more else h // 2 + 8
        new = call(functools.partial(level_kernel, axes, bit), "level",
                   [shape(size, n)] + ([shape(n, n), shape(h, n)] if more else []), [total, packed, *got, placed[3]],
                   [vmem()] * 5 + [anywhere()], [pltpu.VMEM((h + 16, n), f32)])
        packed = new[0]
        if more:
            total, half = new[1:]
    before = call(functools.partial(before_kernel, axes, bits[:-1]), "before",
                  [shape(n, n), shape(n, n), shape(16, n), shape(n, n, dtype=bf16), shape(n, 128), shape(8, n)],
                  [init_var.reshape(1, n), init_mean.reshape(1, n), *received])
    r, *_ = lax.optimization_barrier((swap(packed, bits[-1]), *before))
    return tuple(finish(axes, bits[-1], g, delta, diag, shift, placed, before, r, swap(r, 1)))


def solution(mesh):
    axes = tuple((name, mesh.shape[name]) for name in mesh.axis_names)
    time = P(tuple(mesh.axis_names))
    return jax.shard_map(
        functools.partial(per_device, axes),
        mesh=mesh,
        in_specs=(P(), P(), time, time, time, time, P(), P(), time),
        out_specs=(time, time),
        check_vma=False,
    )
```

```python
import functools

import jax
import jax.numpy as jnp
from jax import lax
from jax.experimental import pallas as pl
from jax.experimental.pallas import tpu as pltpu
from jax.sharding import PartitionSpec as P

f32, bf16 = jnp.float32, jnp.bfloat16
PLANE = 8


def nn(a, b):
    return jnp.dot(a, b, preferred_element_type=f32)


def nt(a, b):
    return lax.dot_general(a, b, (((1,), (1,)), ((), ())), preferred_element_type=f32)


def halves(x):
    high = x.astype(bf16)
    return high, (x - high.astype(f32)).astype(bf16)


def times(late, early):
    (lh, ll), (eh, el) = late, early
    return nn(lh, eh) + (nn(ll, eh) + nn(lh, el))


def advance(late, noise, shift):
    n = noise.shape[1]
    lh, ll = late
    xh, xl = halves(jnp.concatenate([times(late, halves(noise)), shift], axis=0))
    out = nt(xh, lh) + (nt(xl, lh) + nt(xh, ll))
    return out[:n], out[n:]


def wide(col):
    return jnp.concatenate([col, col], axis=1)


def apart(late):
    row = diag_row(late)
    return row, spread(row), jnp.where(eye_mask(late.shape[0]), 0.0, late).astype(bf16)


def conjugate(late, noise):
    row, col, rest = late
    x = wide(col) * noise + nn(rest, noise.astype(bf16))
    return x * row + nt(x.astype(bf16), rest)


def through(late, shift):
    return row_of(jnp.sum(late * shift, axis=1, keepdims=True))


def joined(early, late):
    parts = halves(late[0])
    noise, shift = advance(parts, early[1], early[2])
    return times(parts, halves(early[0])), noise + late[1], shift + late[2]


def eye_mask(n):
    return lax.broadcasted_iota(jnp.int32, (n, n), 0) == lax.broadcasted_iota(jnp.int32, (n, n), 1)


def column(row):
    n = row.shape[1]
    out = []
    for k in range(0, n, 128):
        m = min(128, n - k)
        out.append(jnp.sum(jnp.where(eye_mask(m), row[:, k:k + m], 0.0), axis=1, keepdims=True))
    return out[0] if len(out) == 1 else jnp.concatenate(out, axis=0)


def spread(row):
    n = row.shape[1]
    return jnp.concatenate([jnp.broadcast_to(row[:, k:k + 128], (128, 128)).T for k in range(0, n, 128)], axis=0)


def row_of(col):
    n = col.shape[0]
    out = [jnp.sum(jnp.where(eye_mask(128), col[k:k + 128], 0.0), axis=0, keepdims=True) for k in range(0, n, 128)]
    return jnp.concatenate(out, axis=1)


def diag_row(x):
    n = x.shape[1]
    out = [jnp.sum(jnp.where(eye_mask(128), x[k:k + 128, k:k + 128], 0.0), axis=0, keepdims=True)
           for k in range(0, n, 128)]
    return jnp.concatenate(out, axis=1)


def rows16(row):
    return jnp.broadcast_to(row, (16, row.shape[1]))


def pack(noise, shift):
    n = noise.shape[1]
    h = n // 2
    lower = lax.broadcasted_iota(jnp.int32, (h, h), 0) >= lax.broadcasted_iota(jnp.int32, (h, h), 1)
    a, b, c = noise[:h, :h], noise[:h, h:], noise[h:, h:]
    body = jnp.concatenate([jnp.where(lower, a, c), b], axis=1)
    extra = jnp.concatenate([jnp.zeros((1, h), f32), diag_row(noise)[:, h:]], axis=1)
    return jnp.concatenate([body, shift[0:1], extra, jnp.zeros((14, n), f32)], axis=0)


def unpack(x):
    n = x.shape[1]
    h = n // 2
    i = lax.broadcasted_iota(jnp.int32, (h, h), 0)
    j = lax.broadcasted_iota(jnp.int32, (h, h), 1)
    body, b = x[:h, :h], x[:h, h:]
    turned = body.T
    a = jnp.where(i >= j, body, turned)
    c = jnp.where(i == j, x[h + 1:h + 2, h:], jnp.where(i < j, body, turned))
    noise = jnp.concatenate([jnp.concatenate([a, b], axis=1), jnp.concatenate([b.T, c], axis=1)], axis=0)
    return noise, x[h:h + 1]


def rank_of(axes):
    rank = 0
    for name, size in axes:
        rank = rank * size + lax.axis_index(name)
    return rank


def bit_of(rank, bit):
    return (rank // bit) % 2


def put_half(ref, total_ref, upper):
    rows = ref.shape[0]
    ref[...] = jnp.where(upper, total_ref[rows:], total_ref[:rows])


def put_out(ref, total_ref, upper):
    if ref.shape[0] == total_ref.shape[0]:
        ref[...] = total_ref[...]
    else:
        put_half(ref, total_ref, upper)


def whole(upper, mine_ref, others_ref):
    mine, others = mine_ref[...], others_ref[...]
    return jnp.concatenate([jnp.where(upper, others, mine), jnp.where(upper, mine, others)], axis=0)


def identity(n):
    return jnp.where(eye_mask(n), 1.0, 0.0), jnp.zeros((n, n), f32), jnp.zeros((16, n), f32)


def maps_kernel(subs, decay_hbm, coup_hbm, omap_hbm, gain_hbm, seen_hbm,
                g_ref, e_ref, dcol_ref, delta_ref, shift_ref, maps_ref, total_ref,
                decay_ref, coup_ref, omap_ref, gain_ref, seen_ref, small_sem, sem, g_s, part_s, eh_s, row_s):
    n = decay_ref.shape[1]
    steps = coup_ref.shape[1]
    small = [pltpu.make_async_copy(x, y, small_sem.at[k]) for k, (x, y) in enumerate(
        [(decay_hbm, decay_ref), (seen_hbm, seen_ref)])]

    def chunk(j):
        return [pltpu.make_async_copy(x.at[:, j], y.at[:, j], sem.at[k, j]) for k, (x, y) in enumerate(
            [(coup_hbm, coup_ref), (omap_hbm, omap_ref), (gain_hbm, gain_ref)])]

    for c in small + chunk(0):
        c.start()
    for j in range(1, steps):
        for c in chunk(j):
            c.start()
    for c in small:
        c.wait()

    def step(j, first):
        for c in chunk(j):
            c.wait()
        all_subs = range(subs)
        rows = [decay_ref[pl.ds(s * steps + j, 1), :] for s in all_subs]
        obs_f = [(omap_ref[s, j].astype(f32) * rows[s] + nn(omap_ref[s, j], coup_ref[s, j])).astype(bf16)
                 for s in all_subs]

        def build(s):
            t = s * steps + j
            gain = gain_ref[s, j]
            e = coup_ref[s, j].astype(f32) - nn(gain.T, obs_f[s])
            e_h = e.astype(bf16)
            e_ref[s, j] = e_h
            eh_s[s] = e_h
            col = spread(rows[s])
            dcol_ref[s, j] = col
            shift = jnp.sum(gain.astype(f32) * column(seen_ref[pl.ds(t, 1), :]), axis=0, keepdims=True)
            if first:
                g_s[s] = e
                g_ref[s, j] = e
                delta, b_new = rows[s], shift
            else:
                delta = row_s[s, 0:1, :]
                b = row_s[s, 1:2, :]
                part_s[s] = wide(col) * g_s[s] + e * delta
                delta = delta * rows[s]
                b_new = rows[s] * b + row_of(jnp.sum(e * b, axis=1, keepdims=True)) + shift
            shift_ref[pl.ds(t, 1), :] = b_new
            delta_ref[pl.ds(t, 1), :] = delta
            row_s[s, 0:1, :] = delta
            row_s[s, 1:2, :] = b_new

        def follow(s):
            if not first:
                g_new = part_s[s] + nn(eh_s[s], g_s[s].astype(bf16))
                g_s[s] = g_new
                g_ref[s, j] = g_new

        build(0)
        build(1)
        follow(0)
        build(2)
        follow(1)
        build(3)
        follow(2)
        follow(3)

    step(0, True)
    lax.fori_loop(1, steps, lambda j, c: (step(j, False), c)[1], 0)

    eye = eye_mask(n)
    maps = [g_ref[s, steps - 1] + jnp.where(eye, delta_ref[(s + 1) * steps - 1:(s + 1) * steps, :], 0.0)
            for s in range(subs)]
    for s in range(subs):
        maps_ref[s] = maps[s]
    parts = [halves(m) for m in maps]
    low, high = times(parts[1], parts[0]), times(parts[3], parts[2])
    maps_ref[subs] = low
    maps_ref[subs + 1] = high
    total_ref[...] = times(halves(high), halves(low))


def shapes_kernel(omap_ref, gain_ref, nf_ref, _, shaped_ref, seen_s):
    subs, steps, m = omap_ref.shape[:3]
    nf = nf_ref[...]

    def see(j, carry):
        seen_s[j] = nn(jnp.concatenate([omap_ref[s, j] for s in range(subs)], axis=0), nf).astype(bf16)
        return carry

    def shape_step(j, carry):
        shaped = [(nf.astype(f32) - nn(gain_ref[s, j].T, seen_s[j, s * m:(s + 1) * m])).astype(bf16) for s in range(subs)]
        for s in range(subs):
            shaped_ref[s, j] = shaped[s]
        return carry

    lax.fori_loop(0, steps, see, 0, unroll=8)
    lax.fori_loop(0, steps, shape_step, 0, unroll=8)


def noises_kernel(subs, decay_ref, e_ref, dcol_ref, shaped_ref, gain_ref, var_ref, shift_ref,
                  maps_ref, _, diag_ref, noises_ref, total_ref, q_s):
    n = e_ref.shape[-1]
    steps = e_ref.shape[1]
    var_col = column(var_ref[...])
    all_subs = range(subs)

    def noise(s, j):
        shaped, gain = shaped_ref[s, j], gain_ref[s, j]
        return nt(shaped, shaped) + nn(gain.T, (gain.astype(f32) * var_col).astype(bf16))

    def first_half(s, j, q):
        return wide(dcol_ref[s, j]) * q + nn(e_ref[s, j], q.astype(bf16))

    def second_half(s, j, x):
        return x * decay_ref[pl.ds(s * steps + j, 1), :] + (nt(x.astype(bf16), e_ref[s, j]) + noise(s, j))

    def step(j, carry):
        x = [first_half(s, j, q_s[s]) for s in all_subs]
        for s in all_subs:
            q_new = second_half(s, j, x[s])
            q_s[s] = q_new
            diag_ref[pl.ds(s * steps + j, 1), :] = diag_row(q_new)
        return carry

    for s in all_subs:
        q_s[s] = noise(s, 0)

    for s in all_subs:
        diag_ref[pl.ds(s * steps, 1), :] = diag_row(q_s[s])
    lax.fori_loop(1, steps, step, 0)

    shift = [shift_ref[(s + 1) * steps - 1:(s + 1) * steps, :] for s in range(subs)]
    pairs = [(conjugate(apart(maps_ref[s + 1]), q_s[s]) + q_s[s + 1], through(maps_ref[s + 1], shift[s]) + shift[s + 1])
             for s in (0, 2)]
    last = maps_ref[subs + 1]
    total_ref[...] = pack(conjugate(apart(last), pairs[0][0]) + pairs[1][0], through(last, pairs[0][1]) + pairs[1][1])
    for s in range(subs):
        noises_ref[s, 0:n, :] = q_s[s]
        noises_ref[s, n:, :] = rows16(shift[s])


def chip_kernel(axes, own_ref, other_ref, _, out_ref):
    upper = rank_of(axes) % 2 == 1
    own, other = own_ref[...], other_ref[...]
    out_ref[...] = times(halves(jnp.where(upper, own, other)), halves(jnp.where(upper, other, own)))


def core_kernel(axes, own_map_ref, other_map_ref, own_ref, other_ref, out_ref, half_ref):
    upper = rank_of(axes) % 2 == 1
    own, other = unpack(own_ref[...]), unpack(other_ref[...])
    late = jnp.where(upper, own_map_ref[...], other_map_ref[...])
    early_noise, early_shift = (jnp.where(upper, a, b) for a, b in zip(other, own))
    late_noise, late_shift = (jnp.where(upper, a, b) for a, b in zip(own, other))
    out_ref[...] = pack(conjugate(apart(late), early_noise) + late_noise, through(late, early_shift) + late_shift)
    put_half(half_ref, out_ref, upper)


def fetch(rank, refs, dst, sem):
    place = (rank % PLANE) // (PLANE // len(refs))
    copies = [pltpu.make_async_copy(r, dst.at[place ^ k], sem.at[k]) for k, r in enumerate(refs)]
    for c in copies:
        c.start()
    for c in copies:
        c.wait()


def plane_maps_kernel(axes, *refs):
    ins, refs = refs[:4], refs[4:]
    core_ref, var_ref, mean_ref, late_ref, rest_ref, col_ref, row_ref, start_ref, total_ref, half_ref, picks_ref, chip_s, sem = refs
    rank = rank_of(axes)
    fetch(rank, ins, chip_s, sem)

    def keep(k, late):
        late_ref[k] = late
        row_ref[k:k + 1, :], col_ref[k], rest_ref[k] = apart(late)

    chips = [chip_s[k] for k in range(4)]
    pairs = [times(halves(chips[2 * k + 1]), halves(chips[2 * k])) for k in range(2)]
    total = times(halves(pairs[1]), halves(pairs[0]))
    first = rank // PLANE == 0
    n = total.shape[0]
    noise = conjugate(apart(total), jnp.where(eye_mask(n), var_ref[...], 0.0))
    start_ref[0:n, :] = jnp.where(first, noise, 0.0)
    start_ref[n:, :] = rows16(jnp.where(first, through(total, mean_ref[...]), 0.0))
    total_ref[...] = jnp.where(first, 0.0, total)
    for k, late in enumerate((chips[1], chips[3], pairs[1])):
        keep(k, late)
    h = half_ref.shape[0]
    half_ref[...] = jnp.where(rank % 2 == 1, total_ref[h:], total_ref[:h])
    picks_ref[0] = pairs[0]
    picks_ref[1] = chip_s[2 * bit_of(rank, 4)]
    picks_ref[2] = core_ref[...]


def plane_noises_kernel(axes, *refs):
    ins, (late_ref, rest_ref, col_ref, row_ref, start_ref, core_ref, out_ref, picks_ref, in_s, total_s, sem) = refs[:7], refs[7:]
    rank = rank_of(axes)
    place = (rank % PLANE) // 2
    rows = total_s.shape[0] // 2
    copies = [pltpu.make_async_copy(ins[0], in_s.at[place], sem.at[0])]
    for k in range(1, 4):
        for other in range(2):
            part = (rank % 2) ^ other
            copies.append(pltpu.make_async_copy(
                ins[2 * k - 1 + other], in_s.at[place ^ k, pl.ds(pl.multiple_of(part * rows, 8), rows)],
                sem.at[2 * k - 1 + other]))
    for c in copies:
        c.start()
    for c in copies:
        c.wait()
    n = late_ref.shape[-1]

    def join(k, early, late):
        noise = conjugate((row_ref[k:k + 1, :], col_ref[k], rest_ref[k]), early[0])
        return noise + late[0], through(late_ref[k], early[1]) + late[1]

    def pick(k, element):
        picks_ref[k, 0:n], picks_ref[k, n:] = element[0], rows16(element[1])

    chips = [unpack(in_s[k]) for k in range(4)]
    pairs = [join(k, chips[2 * k], chips[2 * k + 1]) for k in range(2)]
    noise, shift = join(2, pairs[0], pairs[1])
    total_s[...] = pack(noise + start_ref[0:n, :], shift + start_ref[n:n + 1, :])
    put_out(out_ref, total_s, rank % 2 == 1)
    pick(0, pairs[0])
    pick(1, unpack(in_s[2 * bit_of(rank, 4)]))
    pick(2, unpack(core_ref[...]))


def level_kernel(axes, bit, own_map_ref, own_ref, r_ref, x_ref, other_ref, _, *outs):
    *outs, total_s = outs
    rank = rank_of(axes)
    upper, high = rank % 2 == 1, bit_of(rank, bit) == 1
    other_map, own_map = whole(upper, r_ref, x_ref), own_map_ref[...]
    other, own = unpack(other_ref[...]), unpack(own_ref[...])
    late = jnp.where(high, own_map, other_map)
    early_noise, early_shift = (jnp.where(high, a, b) for a, b in zip(other, own))
    late_noise, late_shift = (jnp.where(high, a, b) for a, b in zip(own, other))
    total_s[...] = pack(conjugate(apart(late), early_noise) + late_noise, through(late, early_shift) + late_shift)
    put_out(outs[0], total_s, upper)
    if len(outs) > 1:
        outs[1][...] = times(halves(late), halves(jnp.where(high, other_map, own_map)))
        put_half(outs[2], outs[1], upper)


def place_kernel(axes, subs_ref, sub_noises_ref, maps_ref, noises_ref, out_ref, rest_ref, col_ref, row_ref):
    rank = rank_of(axes)
    n = out_ref.shape[2]
    one = identity(n)
    parts = []
    for k, bit in enumerate((4, 2, 1)):
        element = (maps_ref[k], noises_ref[k, 0:n], noises_ref[k, n:])
        parts.append(tuple(jnp.where(bit_of(rank, bit) == 1, a, b) for a, b in zip(element, one)))

    def put(s, element):
        em, en, es = element
        out_ref[s, 0:n, :], out_ref[s, n:2 * n, :], out_ref[s, 2 * n:, :] = em, en, es

    def sub(s, carry):
        before = out_ref[s, 0:n, :], out_ref[s, n:2 * n, :], out_ref[s, 2 * n:, :]
        put(s + 1, joined(before, (subs_ref[s], sub_noises_ref[s, 0:n, :], sub_noises_ref[s, n:, :])))
        return carry

    def split(s, carry):
        row_ref[s, 0:1, :], col_ref[s], rest_ref[s] = apart(out_ref[s, 0:n, :])
        return carry

    put(0, joined(parts[0], joined(parts[1], parts[2])))
    lax.fori_loop(0, out_ref.shape[0] - 1, sub, 0)
    lax.fori_loop(0, out_ref.shape[0], split, 0)


def before_kernel(axes, bits, var_ref, mean_ref, *refs):
    map_ref, noise_ref, shift_ref, rest_ref, col_ref, row_ref = refs[-6:]
    rank = rank_of(axes)
    before = identity(map_ref.shape[0])
    for k, bit in enumerate(bits):
        r_ref, x_ref, other_ref = refs[3 * k:3 * k + 3]
        noise, shift = unpack(other_ref[...])
        other = whole(rank % 2 == 1, r_ref, x_ref), noise, rows16(shift)
        new = other if k == 0 else joined(other, before)
        before = tuple(jnp.where(bit_of(rank, bit) == 1, a, b) for a, b in zip(new, before))
    n = map_ref.shape[0]
    start = jnp.zeros((n, n), f32), jnp.where(eye_mask(n), var_ref[...], 0.0), rows16(mean_ref[...])
    before = tuple(jnp.where(rank // PLANE == 0, a, b) for a, b in zip(start, before))
    map_ref[...], noise_ref[...], shift_ref[...] = before
    row_ref[0:1, :], col_ref[...], rest_ref[...] = apart(before[0])


def finish_kernel(axes, bit, per, g_ref, delta_ref, var_ref, mean_ref, place_ref, rest_ref, col_ref, arow_ref,
                  bmap_ref, bnoise_ref, bshift_ref, brest_ref, bcol_ref, brow_ref, r_ref, x_ref, means_ref, vars_ref,
                  p_s, row_s, state_s):
    parts, steps, n, _ = g_ref.shape
    rank = rank_of(axes)
    is_high = bit_of(rank, bit) == 1
    state_s[0:n, :] = bnoise_ref[...]
    state_s[n:, :] = bshift_ref[0:8, :]

    @pl.when(is_high)
    def _():
        received, moved = unpack(whole(rank % 2 == 1, r_ref, x_ref))
        state_s[0:n, :] += conjugate((brow_ref[0:1, :], bcol_ref[...], brest_ref[...]), received)
        state_s[n:, :] += through(bmap_ref[...], moved)

    state, moved = state_s[0:n, :], state_s[n:n + 1, :]
    for s in range(parts):
        p = conjugate((arow_ref[s, 0:1, :], col_ref[s], rest_ref[s]), state) + place_ref[s, n:2 * n, :]
        mean = through(place_ref[s, 0:n, :], moved) + place_ref[s, 2 * n:2 * n + 1, :]
        p_s[s] = p.astype(bf16)
        row_s[s, 0:1, :] = mean
        row_s[s, 1:2, :] = diag_row(p)

    def step(k, carry):
        s, j = k // (steps // per), (k % (steps // per)) * per
        g = g_ref[s, pl.ds(j, per)]
        both = nn(g.reshape(per * n, n).astype(bf16), p_s[s])
        mean, spread_of = row_s[s, 0:1, :], row_s[s, 1:2, :]
        t = pl.multiple_of(s * steps + j, per)
        d = delta_ref[pl.ds(t, per), :]
        lane = lax.broadcasted_iota(jnp.int32, (n, 128), 1)
        sums = jnp.zeros((n, 128), f32)
        diags = []
        for i in range(per):
            w = both[i * n:(i + 1) * n]
            diags.append(diag_row(w))
            sums = jnp.where(lane == i, jnp.sum(g[i] * w, axis=1, keepdims=True), sums)
            sums = jnp.where(lane == per + i, jnp.sum(g[i] * mean, axis=1, keepdims=True), sums)
        turned = jnp.concatenate([sums[k:k + 128].T for k in range(0, n, 128)], axis=1)
        vars_ref[pl.ds(t, per), :] = (var_ref[pl.ds(t, per), :] + turned[0:per]
                                      + d * (d * spread_of + 2.0 * jnp.concatenate(diags, axis=0)))
        means_ref[pl.ds(t, per), :] = mean_ref[pl.ds(t, per), :] + d * mean + turned[per:2 * per]
        return carry

    lax.fori_loop(0, parts * steps // per, step, 0)


def vmem():
    return pl.BlockSpec(memory_space=pltpu.VMEM)


def anywhere():
    return pl.BlockSpec(memory_space=pl.ANY)


def shape(*dims, dtype=f32):
    return jax.ShapeDtypeStruct(dims, dtype)


def call(kernel, name, outs, args, specs=None, scratch=(), limit=16, flops=10 ** 5):
    return pl.pallas_call(
        kernel,
        in_specs=specs or [vmem()] * len(args),
        out_specs=[vmem()] * len(outs),
        out_shape=outs,
        scratch_shapes=scratch,
        compiler_params=pltpu.CompilerParams(vmem_limit_bytes=limit * 1024 * 1024),
        cost_estimate=pl.CostEstimate(flops=flops, bytes_accessed=0, transcendentals=0),
        name=name,
    )(*args)


def hbm():
    return pl.BlockSpec(memory_space=pltpu.HBM)


def step_maps(subs, decay, coupling, obs_map, gain, observed):
    T, n = decay.shape
    m = obs_map.shape[1]
    steps = T // subs
    outs = [shape(subs, steps, n, n), shape(subs, steps, n, n, dtype=bf16), shape(subs, steps, n, 128),
            shape(T, n), shape(T, n), shape(subs + 2, n, n), shape(n, n)]
    args = [decay, coupling.reshape(subs, steps, n, n), obs_map.reshape(subs, steps, m, n),
            gain.reshape(subs, steps, m, n), observed]
    scratch = [pltpu.VMEM(x.shape, x.dtype) for x in args]
    args = [pltpu.with_memory_space_constraint(x, pltpu.HBM) for x in args]
    scratch += [pltpu.SemaphoreType.DMA((2,)), pltpu.SemaphoreType.DMA((3, steps)), pltpu.VMEM((subs, n, n), f32),
                pltpu.VMEM((subs, n, n), f32), pltpu.VMEM((subs, n, n), bf16), pltpu.VMEM((subs, 8, n), f32)]
    return call(functools.partial(maps_kernel, subs), "step_maps", outs, args, [hbm()] * len(args), scratch,
                limit=26, flops=10 ** 10)


def step_shapes(subs, obs_map, gain, noise_factor, token):
    T, m, n = obs_map.shape
    steps = T // subs
    return call(shapes_kernel, "step_shapes", [shape(subs, steps, n, n, dtype=bf16)],
                [obs_map.reshape(subs, steps, m, n), gain.reshape(subs, steps, m, n), noise_factor, token],
                [vmem()] * 3 + [anywhere()], [pltpu.VMEM((steps, subs * m, n), bf16)])[0]


def step_noises(subs, decay, e, dcol, shaped, gain, obs_var, shift, maps, token):
    T, n = decay.shape
    m = gain.shape[1]
    args = [decay, e, dcol, shaped, gain.reshape(subs, T // subs, m, n), obs_var.reshape(1, m),
            shift, maps, token]
    return call(functools.partial(noises_kernel, subs), "step_noises",
                [shape(T, n), shape(subs, n + 16, n), shape(n // 2 + 16, n)], args, [vmem()] * 8 + [anywhere()],
                [pltpu.VMEM((subs, n, n), f32)])


def finish(axes, bit, g, delta, var, mean, placed, before, r, x, per=8):
    parts = g.shape[0]
    T, n = var.shape
    return call(functools.partial(finish_kernel, axes, bit, per), "finish", [shape(T, n)] * 2,
                [g, delta, var, mean, *placed, *before, r, x],
                scratch=[pltpu.VMEM((parts, n, n), bf16), pltpu.VMEM((parts, 8, n), f32), pltpu.VMEM((n + 8, n), f32)])


def per_device(axes, init_mean, init_var, decay, coupling, obs_map, gain, noise_factor, obs_var, observed):
    n = decay.shape[1]
    h = n // 2
    subs = 4
    count = 1
    for _, size in axes:
        count *= size
    names = tuple(name for name, _ in axes)

    def swap(x, bit):
        return lax.ppermute(x, names, [(k, k ^ bit) for k in range(count)])

    bits = []
    bit = PLANE
    while bit < count:
        bits.append(bit)
        bit *= 2

    g, e, dcol, delta, shift, maps, own = step_maps(subs, decay, coupling, obs_map, gain, observed)
    other = swap(own, 1)
    shaped = step_shapes(subs, obs_map, gain, noise_factor, delta)
    (chip_map,) = call(functools.partial(chip_kernel, axes), "chip_maps", [shape(n, n)], [own, other, shaped],
                       [vmem()] * 2 + [anywhere()])
    far = [swap(chip_map, bit) for bit in (2, 4, 6)]
    diag, noises, packed = step_noises(subs, decay, e, dcol, shaped, gain, obs_var, shift, maps, chip_map)
    other_packed = swap(packed, 1)
    chip, chip_half = call(functools.partial(core_kernel, axes), "core_noises", [shape(h + 16, n), shape(h // 2 + 8, n)],
                   [own, other, packed, other_packed])
    chips = [chip] + [v for r in [swap(chip_half, bit) for bit in (2, 4, 6)] for v in (r, swap(r, 1))]
    *far, _ = lax.optimization_barrier((*far, chip))
    *late, total, half, map_picks = call(
        functools.partial(plane_maps_kernel, axes), "plane_maps",
        [shape(3, n, n), shape(3, n, n, dtype=bf16), shape(3, n, 128), shape(8, n), shape(n + 16, n), shape(n, n), shape(h, n), shape(3, n, n)],
        [chip_map, *far, other, init_var.reshape(1, n), init_mean.reshape(1, n)], [anywhere()] * 4 + [vmem()] * 3,
        [pltpu.VMEM((4, n, n), f32), pltpu.SemaphoreType.DMA((4,))])
    size = h + 16 if len(bits) > 1 else h // 2 + 8
    packed, noise_picks = call(
        functools.partial(plane_noises_kernel, axes), "plane_noises",
        [shape(size, n), shape(3, n + 16, n)],
        [*chips, *late, other_packed], [anywhere()] * 7 + [vmem()] * 6,
        [pltpu.VMEM((4, h + 16, n), f32), pltpu.VMEM((h + 16, n), f32), pltpu.SemaphoreType.DMA((7,))])
    placed = call(functools.partial(place_kernel, axes), "place",
                  [shape(subs, 2 * n + 16, n), shape(subs, n, n, dtype=bf16), shape(subs, n, 128), shape(subs, 8, n)],
                  [maps, noises, map_picks, noise_picks])
    received = []
    for k, bit in enumerate(bits[:-1]):
        moving = swap(packed, bit)
        r, packed = lax.optimization_barrier((swap(half, bit), packed))
        got = (r, swap(r, 1), moving)
        received += got
        more = k < len(bits) - 2
        size = h + 16 if more else h // 2 + 8
        new = call(functools.partial(level_kernel, axes, bit), "level",
                   [shape(size, n)] + ([shape(n, n), shape(h, n)] if more else []), [total, packed, *got, placed[3]],
                   [vmem()] * 5 + [anywhere()], [pltpu.VMEM((h + 16, n), f32)])
        packed = new[0]
        if more:
            total, half = new[1:]
    before = call(functools.partial(before_kernel, axes, bits[:-1]), "before",
                  [shape(n, n), shape(n, n), shape(16, n), shape(n, n, dtype=bf16), shape(n, 128), shape(8, n)],
                  [init_var.reshape(1, n), init_mean.reshape(1, n), *received])
    r, *_ = lax.optimization_barrier((swap(packed, bits[-1]), *before))
    return tuple(finish(axes, bits[-1], g, delta, diag, shift, placed, before, r, swap(r, 1)))


def solution(mesh):
    axes = tuple((name, mesh.shape[name]) for name in mesh.axis_names)
    time = P(tuple(mesh.axis_names))
    return jax.shard_map(
        functools.partial(per_device, axes),
        mesh=mesh,
        in_specs=(P(), P(), time, time, time, time, P(), P(), time),
        out_specs=(time, time),
        check_vma=False,
    )
```
